32 devices in a mesh: tm: 4 (over z), elem: 8 (over y, x, core).
Axes of the slice: x: 2, y: 2, z: 4, core: 2. Of those that a mesh axis runs over, the one named last changes fastest.
Arguments:
- state: float32 [16, 5, 8, 125, 128], P('tm', None, 'elem'), may hold values from -6 to 6
- metric_scale: float32 [8, 125, 128], P('elem'), may hold values from 0.1 to 0.4
- flux_jacobians: float32 [3, 5, 5], replicated, may hold values from -1.5 to 1.5, as said below
- preconditioner: float32 [16, 5, 5, 8, 128], P('tm', None, None, 'elem'), may hold values from -0.04 to 0.24
- inflow: float32 [16, 5, 8, 25], P('tm', None, 'elem'), may hold values from -6 to 6
Outputs:
- new_state: float32 [16, 5, 8, 125, 128], P('tm', None, 'elem')
- final_residual: float32 [16, 5, 8, 125, 128], P('tm', None, 'elem')
The draws below stay inside these ranges and needn't reach their ends.
Inputs may be any that keep to these rules, and one draw needn't show every extreme that they name: `flux_jacobians`: symmetric in its last two dimensions.
All inputs are finite; a program needn't handle non-finite values.
Results may differ from the reference program's by a relative error of at most 0.0001.
Values sent between devices are 32-bit elements; how exact they have to be, the bound alone decides.
No kernel may reach another device: no remote copies, remote signals or barrier semaphores. Data moves between devices by JAX's collectives and lax.ppermute only.
A program may use at most 128 MiB of HBM per device.

```python
import math
import jax
import jax.numpy as jnp
import numpy as np
from jax import lax

NI = 16
NV = 5
PR = 8
PASSES = 3
NAX = 128
COLS = 8
NCIRC = 1


def draw_flux_jacobians(key, part):
    sampled = jnp.clip(jax.random.normal(key, (3, NV, NV), jnp.float32) * 0.45, -1.5, 1.5)
    return 0.5 * (sampled + jnp.swapaxes(sampled, 1, 2))


def draw_preconditioner(key, part):
    key_scale = jax.random.fold_in(key, 11)
    key_mix = jax.random.fold_in(key, 23)
    scales = jnp.exp(jax.random.uniform(key_scale, (NI, 1, 1, COLS, NAX), jnp.float32, math.log(0.05), math.log(0.2)))
    mixing = jax.random.uniform(key_mix, (NI, NV, NV, COLS, NAX), jnp.float32, -0.2, 0.2)
    identity = jnp.eye(NV, dtype=jnp.float32)[None, :, :, None, None]
    return scales * (identity * (1.0 + mixing) + (1.0 - identity) * mixing)


def shard_levels(rng, shape, cuts, least, top_value):
    factor_of, own = 1.0, jax.random.fold_in(rng, 6)
    for dim, parts in cuts:
        draws = jnp.exp(jax.random.uniform(jax.random.fold_in(own, dim), (parts,), jnp.float32, least / len(cuts), top_value / len(cuts)))
        factor_of = factor_of * jnp.repeat(draws, shape[dim] // parts).reshape([-1 if axis == dim else 1 for axis in range(len(shape))])
    return factor_of


def bell_draw(key, extent, spread, bound, cuts=(), held_as=jnp.bfloat16):
    values = jax.random.normal(key, extent, jnp.float32) * spread
    if len(cuts) > 0:
        values = shard_levels(key, extent, cuts, -0.22, 0.18) * values
    return jnp.clip(values, min=-bound, max=bound).astype(held_as)


def setup_inputs(seed: int = 0) -> dict:
    key_of = jax.random.split(jax.random.key(seed), 6)
    return {
        "state": bell_draw(key_of[0], (NI, NV, COLS, 125, NAX), 1.0, 6.0, ((0, 4), (2, 8)), jnp.float32),
        "metric_scale": jnp.clip(jnp.exp(math.log(0.4) - 1.3862944 * jax.random.uniform(key_of[1], (COLS, 125, NAX), jnp.float32) ** shard_levels(key_of[1], (COLS, 125, NAX), ((0, 8),), -0.2, 0.2)), 0.1, 0.4),
        "flux_jacobians": draw_flux_jacobians(jax.random.fold_in(key_of[5], 71), 0),
        "preconditioner": draw_preconditioner(jax.random.fold_in(key_of[5], 71), 0),
        "inflow": bell_draw(key_of[4], (NI, NV, COLS, 25), 1.0, 6.0, ((0, 4), (2, 8)), jnp.float32),
    }


precise = lax.Precision.HIGHEST

def gll_derivative():
    points = np.array([-1.0, -math.sqrt(3.0 / 7.0), 0.0, math.sqrt(3.0 / 7.0), 1.0])
    legendre = (35.0 * points ** 4 - 30.0 * points ** 2 + 3.0) / 8.0
    identity = np.eye(5, dtype=bool)
    spacing = np.where(identity, 1.0, points[:, None] - points[None, :])
    matrix = legendre[:, None] / legendre[None, :] / spacing
    corner = np.array([-5.0, 0.0, 0.0, 0.0, 5.0])[None, :]
    return np.where(identity, corner, matrix)

def spectral_rows(row_ids, col_ids, count):
    offset = row_ids[:, None] - col_ids[None, :]
    parity = 1.0 - 2.0 * jnp.remainder(offset, 2).astype(jnp.float32)
    angle = jnp.pi * offset.astype(jnp.float32) / count
    diagonal = offset == 0
    sine = jnp.where(diagonal, 1.0, jnp.sin(angle))
    return jnp.where(diagonal, 0.0, 0.5 * parity * jnp.cos(angle) / sine)

def apply_matrix(matrix, values):
    return jnp.einsum('vw,nw...->nv...', matrix, values, precision=precise)

def lift_faces(lows, highs, beyond_low, beyond_high, matrix, damping, node_axis):
    jump_high = beyond_high - highs
    jump_low = beyond_low - lows
    high_term = 0.5 * (apply_matrix(matrix, jump_high) - damping * jump_high)
    low_term = -0.5 * (apply_matrix(matrix, jump_low) + damping * jump_low)
    middle = jnp.zeros_like(lows)
    return jnp.stack([low_term, middle, middle, middle, high_term], axis=node_axis)

def reference(state, metric_scale, flux_jacobians, preconditioner, inflow):
    derivative = jnp.asarray(gll_derivative(), dtype=jnp.float32)
    damping = lax.optimization_barrier(jnp.max(lax.optimization_barrier(jnp.sum(jnp.abs(flux_jacobians), axis=2)), axis=1))
    instances = jnp.arange(NI, dtype=jnp.int32)
    coupling = spectral_rows(instances, instances, NI)
    spectral = jnp.dot(coupling, state.reshape(NI, -1), precision=precise, preferred_element_type=jnp.float32).reshape(state.shape)
    half_col = PR // 2
    grid_shape = (NI, NV, NCIRC, PR, 5, 5, 5, NAX)
    metric = jnp.roll(metric_scale, half_col, axis=0).reshape((1, 1) + grid_shape[2:])
    inflow_nodes = jnp.roll(inflow, half_col, axis=2).reshape(NI, NV, NCIRC, PR, 5, 5, 1)
    reflect = jnp.array([1.0, 1.0, -1.0, 1.0, 1.0], dtype=jnp.float32).reshape(1, NV, 1, 1, 1, 1, 1)
    outputs = ('nvcrpjka', 'nvcripka', 'nvcrijpa')
    inputs = ('pi,nvcrijka', 'pj,nvcrijka', 'pk,nvcrijka')

    def full_residual(current):
        fields = jnp.roll(current, half_col, axis=2).reshape(grid_shape)
        volume = jnp.zeros_like(fields)
        for direction in range(3):
            fluxes = apply_matrix(flux_jacobians[direction], fields)
            volume = volume + jnp.einsum(inputs[direction] + '->' + outputs[direction], derivative, fluxes, precision=precise)
        lows = fields[:, :, :, :, 0]
        highs = fields[:, :, :, :, 4]
        surface = lift_faces(lows, highs, jnp.roll(highs, 1, axis=2), jnp.roll(lows, -1, axis=2), flux_jacobians[0], damping[0], 4)
        lows = fields[:, :, :, :, :, 0]
        highs = fields[:, :, :, :, :, 4]
        beyond_high = jnp.concatenate([lows[:, :, :, 1:], reflect * highs[:, :, :, -1:]], axis=3)
        beyond_low = jnp.concatenate([reflect * lows[:, :, :, :1], highs[:, :, :, :-1]], axis=3)
        surface = surface + lift_faces(lows, highs, beyond_low, beyond_high, flux_jacobians[1], damping[1], 5)
        lows = fields[:, :, :, :, :, :, 0]
        highs = fields[:, :, :, :, :, :, 4]
        beyond_high = jnp.concatenate([lows[..., 1:], highs[..., -1:]], axis=6)
        beyond_low = jnp.concatenate([inflow_nodes, highs[..., :-1]], axis=6)
        surface = surface + lift_faces(lows, highs, beyond_low, beyond_high, flux_jacobians[2], damping[2], 6)
        spatial = (metric * (volume + 10.0 * surface)).reshape(state.shape)
        return jnp.roll(spatial, -half_col, axis=2) + spectral
    iterate = state
    for sweep_index in range(PASSES):
        update = jnp.einsum('nvwca,nwcqa->nvcqa', preconditioner, full_residual(iterate), precision=precise)
        iterate = iterate - update
    return (iterate, full_residual(iterate))
```

```python
import math

import jax
import jax.numpy as jnp
import ml_dtypes
import numpy as np
from jax import lax
from jax.experimental import pallas as pl
from jax.experimental.pallas import tpu as pltpu
from jax.sharding import PartitionSpec as P

PR = 8
PASSES = 3
GROUPS = 2
ROWS = 128
FACE = 32
HIGH = 96

F32 = jnp.float32
BF16 = jnp.bfloat16


def gll_derivative():
    points = np.array([-1.0, -math.sqrt(3.0 / 7.0), 0.0, math.sqrt(3.0 / 7.0), 1.0])
    legendre = (35.0 * points**4 - 30.0 * points**2 + 3.0) / 8.0
    identity = np.eye(5, dtype=bool)
    spacing = np.where(identity, 1.0, points[:, None] - points[None, :])
    matrix = legendre[:, None] / legendre[None, :] / spacing
    corner = np.array([-5.0, 0.0, 0.0, 0.0, 5.0])[None, :]
    return np.where(identity, corner, matrix)


def coupling_value(offset, count):
    offset = offset % count
    if offset == 0:
        return 0.0
    angle = math.pi * offset / count
    return 0.5 * (-1.0) ** offset * math.cos(angle) / math.sin(angle)


def node_rows():
    rows = np.zeros(125, dtype=np.int64)
    free = list(range(25, HIGH)) + list(range(HIGH + 25, ROWS))
    for i in range(5):
        for j in range(5):
            for k in range(5):
                node = 25 * i + 5 * j + k
                if j == 0:
                    rows[node] = 5 * i + k
                elif j == 4:
                    rows[node] = HIGH + 5 * i + k
                else:
                    rows[node] = free.pop(0)
    return rows


def split_bf16(matrix):
    high = matrix.astype(np.float32).astype(ml_dtypes.bfloat16)
    low = (matrix - high.astype(np.float64)).astype(np.float32).astype(ml_dtypes.bfloat16)
    return high, low


def tables(own_circ):
    table = gll_derivative()
    eye = np.eye(5)
    first, last = np.diag([1.0, 0, 0, 0, 0]), np.diag([0, 0, 0, 0, 1.0])
    to_first, to_last = np.zeros((5, 5)), np.zeros((5, 5))
    to_first[0, 4] = 1.0
    to_last[4, 0] = 1.0

    def along(matrix, direction):
        parts = [eye, eye, eye]
        parts[direction] = matrix
        return np.kron(np.kron(parts[0], parts[1]), parts[2])

    rows = node_rows()
    order = np.zeros((ROWS, ROWS))
    order[rows, np.arange(125)] = 1.0

    def placed(matrix):
        return order[:, :125] @ matrix @ order[:, :125].T

    mix, damp = [], []
    for d in range(3):
        mix.append(placed(along(table - 5.0 * last + 5.0 * first, d)))
        damp.append(placed(along(5.0 * last + 5.0 * first, d)))
    if own_circ:
        mix[0] = mix[0] + placed(along(5.0 * to_last - 5.0 * to_first, 0))
        damp[0] = damp[0] + placed(along(-5.0 * to_last - 5.0 * to_first, 0))
    none = np.zeros((ROWS, ROWS))
    axial_mix = placed(along(5.0 * to_last - 5.0 * to_first, 2))
    axial_damp = placed(along(-5.0 * to_last - 5.0 * to_first, 2))
    fluxes = np.concatenate(
        [
            np.concatenate([mix[0], none], 1),
            np.concatenate([mix[1], none], 1),
            np.concatenate([mix[2], axial_mix], 1),
        ],
        0,
    )
    fluxes = np.stack(split_bf16(fluxes))
    dampers = np.stack(
        [
            np.concatenate([damp[0], none], 1),
            np.concatenate([damp[1], none], 1),
            np.concatenate([damp[2], axial_damp], 1),
        ]
    ).astype(np.float32)
    return order, fluxes, dampers


def lane_masks(lanes):
    rows = node_rows()
    k_first, k_last = rows[0::5], rows[4::5]
    masks = np.zeros((3, ROWS, lanes), dtype=np.float32)
    masks[0][k_last, 1:] = 1.0
    masks[1][k_first, :-1] = 1.0
    masks[2][k_last, -1] = 5.0
    return masks


def halves(values):
    high = values.astype(BF16)
    low = (values - high.astype(F32)).astype(BF16)
    return high, low


def dot32(a, b):
    return jnp.dot(a, b, preferred_element_type=F32)


def reorder(matrix, values, terms):
    total = None
    for _ in range(terms):
        part = values.astype(BF16)
        moved = dot32(matrix, part)
        total = moved if total is None else total + moved
        values = values - part.astype(F32)
    return total


def mixed(weights, parts):
    total = weights[0] * parts[0]
    for weight, part in zip(weights[1:], parts[1:]):
        total = total + weight * part
    return total


VMEM_LIMIT = 48 * 2**20


def call(kernel, outs, ins, in_spaces, out_spaces=None, scratch=(), flops=0, alias=None, name=None):
    out_spaces = out_spaces or ["v"] * len(outs)
    space = {"v": pltpu.VMEM, "s": pltpu.SMEM, "a": pl.ANY}
    nbytes = sum(int(np.prod(x.shape)) * x.dtype.itemsize for x in list(ins) + list(outs))
    return pl.pallas_call(
        kernel,
        out_shape=outs,
        in_specs=[pl.BlockSpec(memory_space=space[s]) for s in in_spaces],
        out_specs=[pl.BlockSpec(memory_space=space[s]) for s in out_spaces],
        scratch_shapes=list(scratch),
        input_output_aliases=alias or {},
        compiler_params=pltpu.CompilerParams(vmem_limit_bytes=VMEM_LIMIT),
        cost_estimate=pl.CostEstimate(flops=flops, bytes_accessed=nbytes, transcendentals=0),
        name=name,
    )(*ins)


def shape(*dims, dtype=F32):
    return jax.ShapeDtypeStruct(dims, dtype)


def per_device(state, metric_scale, flux_jacobians, preconditioner, inflow):
    inst, nv, _, nodes, lanes = state.shape
    n_tm = lax.axis_size("tm")
    n_elem = lax.axis_size("elem")
    count = inst * n_tm
    own_circ = n_elem == PR
    block = ROWS // n_tm
    groups = GROUPS if inst % GROUPS == 0 else 1
    per = inst // groups
    order, flux_table, damp_table = tables(own_circ)
    order_b = order.astype(ml_dtypes.bfloat16)
    back_b = np.ascontiguousarray(order.T).astype(ml_dtypes.bfloat16)
    masks = lane_masks(lanes)
    node_row = node_rows()
    inlet_table = np.zeros((ROWS, ROWS), dtype=np.float32)
    inlet_table[node_row[0::5], np.arange(25)] = 1.0

    damping = jnp.max(jnp.sum(jnp.abs(flux_jacobians), axis=2), axis=1)
    coef = jnp.concatenate([flux_jacobians.reshape(-1), damping])
    precond = preconditioner.reshape(inst, nv, nv, lanes)
    inlet = inflow.reshape(inst, nv, 25)
    inlet = jnp.stack(
        [
            -5.0
            * (
                sum(flux_jacobians[2, v, w] * inlet[:, w] for w in range(nv))
                + damping[2] * inlet[:, v]
            )
            for v in range(nv)
        ],
        axis=1,
    ).reshape(inst * nv, 25)
    inlet = jnp.pad(inlet, ((0, ROWS - inst * nv), (0, ROWS - 25)))

    def jac(ref, d, v, w):
        return ref[(d * nv + v) * nv + w]

    def damp(ref, d):
        return ref[3 * nv * nv + d]

    def pack_kernel(state_ref, *refs):
        outs, padded, sem = refs[:n_tm], refs[n_tm], refs[n_tm + 1]
        copies = []
        for n in range(inst):
            for v in range(nv):
                padded[n, v, pl.ds(ROWS - 8, 8), :] = jnp.zeros((8, lanes), F32)
        for n in range(inst):
            for v in range(nv):
                copies.append(
                    pltpu.make_async_copy(
                        state_ref.at[n, v, :, 0, :],
                        padded.at[n, v, pl.ds(0, nodes), :],
                        sem.at[n, v],
                    )
                )
        for copy in copies:
            copy.start()
        for copy in copies:
            copy.wait()
        me = lax.axis_index("tm")
        for d in range(n_tm):
            start = pl.multiple_of(lax.rem(me + d, n_tm) * block, block)
            for n in range(inst):
                for v in range(nv):
                    outs[d][n, v] = padded[n, v, pl.ds(start, block), :]

    piece = shape(inst, nv, block, lanes)
    packed = call(
        pack_kernel,
        [piece] * n_tm + [shape(inst, nv, ROWS, lanes)],
        [state.reshape(inst, nv, nodes, 1, lanes)],
        "a",
        scratch=[pltpu.SemaphoreType.DMA((inst, nv))],
        name="pack",
    )
    pieces, padded = packed[:n_tm], packed[n_tm]

    def along_tm(x, d):
        return lax.ppermute(x, "tm", [(i, (i + d) % n_tm) for i in range(n_tm)])

    def along_elem(x, d):
        return lax.ppermute(x, "elem", [(i, (i + d) % n_elem) for i in range(n_elem)])

    arrived = [pieces[0]] + [along_tm(pieces[d], d) for d in range(1, n_tm)]

    def prep_kernel(
        padded_ref, metric_ref, coef_ref, order_ref, flux_ref, damp_ref, inlet_ref, inlet_table_ref,
        x_ref, lo_ref, hi_ref, m_ref, mf_ref, lhs_ref, col_ref, buf, sem,
    ):
        buf[pl.ds(ROWS - 8, 8), :] = jnp.zeros((8, lanes), F32)
        copy = pltpu.make_async_copy(metric_ref.at[:, 0, :], buf.at[pl.ds(0, nodes), :], sem)
        copy.start()
        copy.wait()
        metric = reorder(order_ref[...], buf[...], 3)
        m_ref[...] = metric
        row = lax.broadcasted_iota(jnp.int32, (FACE, lanes), 0)
        mf_ref[0] = jnp.where(row < 25, metric[0:FACE], 0.0)
        mf_ref[1] = jnp.where(row < 25, metric[HIGH:ROWS], 0.0)
        for part in range(2):
            lhs_ref[part, 0 : 3 * ROWS, :] = flux_ref[part]
        total = damp(coef_ref, 0) * damp_ref[0]
        for d in range(1, 3):
            total = total + damp(coef_ref, d) * damp_ref[d]
        high, low = halves(total)
        lhs_ref[0, 3 * ROWS : 4 * ROWS, :] = high
        lhs_ref[1, 3 * ROWS : 4 * ROWS, :] = low
        cols = lax.dot_general(
            inlet_table_ref[...],
            inlet_ref[...],
            (((1,), (1,)), ((), ())),
            precision=lax.Precision.HIGHEST,
            preferred_element_type=F32,
        )
        col_ref[...] = metric[:, 0:1] * cols
        for n in range(inst):
            natural = jnp.concatenate([padded_ref[n, v] for v in range(nv)], axis=1)
            moved = reorder(order_ref[...], natural, 3)
            for v in range(nv):
                part = moved[:, v * lanes : (v + 1) * lanes]
                x_ref[n, v] = part
                lo_ref[n, v] = part[0:FACE]
                hi_ref[n, v] = part[HIGH:ROWS]

    x0, lo0, hi0, metric, metric_face, lhs, inlet_cols = call(
        prep_kernel,
        [
            shape(inst, nv, ROWS, lanes),
            shape(inst, nv, FACE, lanes),
            shape(inst, nv, FACE, lanes),
            shape(ROWS, lanes),
            shape(2, FACE, lanes),
            shape(2, 4 * ROWS, 2 * ROWS, dtype=BF16),
            shape(ROWS, ROWS),
        ],
        [
            padded,
            metric_scale.reshape(nodes, 1, lanes),
            coef,
            order_b,
            flux_table,
            damp_table,
            inlet,
            inlet_table,
        ],
        "vasvvvvv",
        scratch=[pltpu.VMEM((ROWS, lanes), F32), pltpu.SemaphoreType.DMA],
        name="prep",
    )

    def bulk(x, coef_ref, lhs_ref, masks_ref, metric_value):
        wide = jnp.concatenate(x, axis=1)
        shifted = jnp.concatenate(
            [
                pltpu.roll(part, 1, 1) * masks_ref[0] + pltpu.roll(part, lanes - 1, 1) * masks_ref[1]
                for part in x
            ],
            axis=1,
        )
        high, low = halves(jnp.concatenate([wide, shifted], axis=0))
        grads = dot32(lhs_ref[0], high) + dot32(lhs_ref[1], high) + dot32(lhs_ref[0], low)

        def grad(d, w):
            return grads[d * ROWS : (d + 1) * ROWS, w * lanes : (w + 1) * lanes]

        edge = [masks_ref[2] * part for part in x]
        parts = [grad(0, w) for w in range(nv)] + [grad(1, w) for w in range(nv)]
        parts = parts + [grad(2, w) + edge[w] for w in range(nv)]
        result = []
        for v in range(nv):
            weights = [jac(coef_ref, d, v, w) for d in range(3) for w in range(nv)]
            total = mixed(weights, parts) + grad(3, v) - damp(coef_ref, 2) * edge[v]
            result.append(metric_value * total)
        return result

    def whole(lo_ref, z_ref, hi_ref, n, at, v):
        return jnp.concatenate([lo_ref[n, v], z_ref[at, v, FACE:HIGH, :], hi_ref[n, v]], axis=0)

    bulk_flops = 2 * 3 * 4 * ROWS * 2 * ROWS * nv * lanes

    def advance(z, lo, hi, extra, first, size):
        def kernel(*refs):
            z_ref, lo_ref, hi_ref, m_ref, p_ref, coef_ref, lhs_ref, masks_ref = refs[:8]
            out_ref = refs[-1]
            metric_value = m_ref[...]

            def body(n, carry):
                x = [whole(lo_ref, z_ref, hi_ref, n, n, v) for v in range(nv)]
                res = bulk(x, coef_ref, lhs_ref, masks_ref, metric_value)
                if extra is not None:
                    res = [res[v] + refs[8][n, v] for v in range(nv)]
                for v in range(nv):
                    weights = [p_ref[first + n, v, pl.ds(w, 1), :] for w in range(nv)]
                    out_ref[n, v] = x[v] - mixed(weights, res)
                return carry

            lax.fori_loop(0, size, body, 0)

        ins = [z, lo, hi, metric, precond, coef, lhs, masks]
        ins = ins + ([] if extra is None else [extra])
        return call(
            kernel,
            [shape(size, nv, ROWS, lanes)],
            ins,
            "vvvvvsvv" + ("" if extra is None else "v"),
            flops=bulk_flops * size,
            name="advance",
        )[0]

    def face_terms(n, lo_ref, hi_ref, below_ref, above_ref, coef_ref, mf_ref):
        position = lax.rem(lax.axis_index("elem") + PR // 2, PR)
        low_w, high_w = [], []
        for v in range(nv):
            sign = -1.0 if v == 2 else 1.0
            low_w.append(jnp.where(position == 0, sign * lo_ref[n, v], below_ref[n, v]))
            high_w.append(jnp.where(position == PR - 1, sign * hi_ref[n, v], above_ref[n, v]))
        lows, highs = [], []
        for v in range(nv):
            weights = [jac(coef_ref, 1, v, w) for w in range(nv)]
            lows.append((mixed(weights, low_w) + damp(coef_ref, 1) * low_w[v]) * (-5.0 * mf_ref[0]))
            highs.append((mixed(weights, high_w) - damp(coef_ref, 1) * high_w[v]) * (5.0 * mf_ref[1]))
        return lows, highs

    def swap_faces(lo, hi):
        return along_elem(hi, 1), along_elem(lo, -1)

    def close_faces(z, lo, hi, below, above, first, size):
        def kernel(z_ref, lo_ref, hi_ref, below_ref, above_ref, coef_ref, mf_ref, p_ref, nlo_ref, nhi_ref):
            def body(n, carry):
                lows, highs = face_terms(n, lo_ref, hi_ref, below_ref, above_ref, coef_ref, mf_ref)
                for v in range(nv):
                    weights = [p_ref[first + n, v, pl.ds(w, 1), :] for w in range(nv)]
                    nlo_ref[n, v] = z_ref[n, v, 0:FACE, :] - mixed(weights, lows)
                    nhi_ref[n, v] = z_ref[n, v, HIGH:ROWS, :] - mixed(weights, highs)
                return carry

            lax.fori_loop(0, size, body, 0)

        return call(
            kernel,
            [shape(size, nv, FACE, lanes)] * 2,
            [z, lo, hi, below, above, coef, metric_face, precond],
            "vvvvvsvv",
            name="faces",
        )

    def circ_extra(z, lo, hi):
        x = jnp.concatenate([lo, z[:, :, FACE:HIGH], hi], axis=2)
        picks = np.zeros((2, 25, ROWS), dtype=np.float32)
        picks[0, np.arange(25), node_row[0:25]] = 1.0
        picks[1, np.arange(25), node_row[100:125]] = 1.0
        exact = lax.Precision.HIGHEST

        def picked(which):
            return jnp.einsum("pq,nvqa->nvpa", picks[which], x, precision=exact)

        def mix(values):
            return jnp.einsum("vw,nwqa->nvqa", flux_jacobians[0], values, precision=exact)

        def placed(which, values):
            return jnp.einsum("pq,nvpa->nvqa", picks[which], values, precision=exact)

        above, below = along_elem(picked(0), -PR), along_elem(picked(1), PR)
        high_term = 5.0 * (mix(above) - damping[0] * above)
        low_term = -5.0 * (mix(below) + damping[0] * below)
        return metric * (placed(1, high_term) + placed(0, low_term))

    below0, above0 = swap_faces(lo0, hi0)
    t0 = advance(x0, lo0, hi0, None if own_circ else circ_extra(x0, lo0, hi0), 0, inst)
    tlo, thi = close_faces(t0, lo0, hi0, below0, above0, 0, inst)

    half_pair = n_tm % 2 == 0

    def coupling_kernel(*refs):
        x_refs, outs = refs[:n_tm], refs[n_tm:]

        def weight(offset, sign):
            return 0.5 * (
                coupling_value(offset, count) + sign * coupling_value(offset + count // 2, count)
            )

        def emit(e, j, rows, v, value):
            outs[e * groups + j // per][j % per, v, rows, :] = value

        def body(step, carry):
            v, rows = step // (block // 8), pl.ds(pl.multiple_of((step % (block // 8)) * 8, 8), 8)
            x = [[x_refs[d][i, v, rows, :] for i in range(inst)] for d in range(n_tm)]
            if half_pair:
                half = n_tm // 2
                sums = [x[d][i] + x[d + half][i] for d in range(half) for i in range(inst)]
                diffs = [x[d][i] - x[d + half][i] for d in range(half) for i in range(inst)]
                for e in range(half):
                    for j in range(inst):
                        offsets = [inst * (e + d) + j - i for d in range(half) for i in range(inst)]
                        terms = [(weight(o, 1), s) for o, s in zip(offsets, sums)]
                        terms = [(c, s) for c, s in terms if abs(c) > 1e-12]
                        even = mixed([c for c, _ in terms], [s for _, s in terms])
                        terms = [(weight(o, -1), s) for o, s in zip(offsets, diffs)]
                        terms = [(c, s) for c, s in terms if abs(c) > 1e-12]
                        odd = mixed([c for c, _ in terms], [s for _, s in terms])
                        emit(e, j, rows, v, even + odd)
                        emit(e + half, j, rows, v, even - odd)
            else:
                for e in range(n_tm):
                    for j in range(inst):
                        terms = [
                            (coupling_value(inst * (e + d) + j - i, count), x[d][i])
                            for d in range(n_tm)
                            for i in range(inst)
                        ]
                        emit(e, j, rows, v, mixed([c for c, _ in terms], [s for _, s in terms]))
            return carry

        lax.fori_loop(0, nv * (block // 8), body, 0)

    coupled = call(
        coupling_kernel,
        [shape(per, nv, block, lanes)] * (n_tm * groups),
        arrived,
        "v" * n_tm,
        name="coupling",
    )
    spectral = [
        [coupled[g]] + [along_tm(coupled[e * groups + g], e) for e in range(1, n_tm)]
        for g in range(groups)
    ]

    def first_pass(parts, first):
        def kernel(*refs):
            part_refs = refs[:n_tm]
            t_ref, tlo_ref, thi_ref, p_ref, col_ref, order_ref = refs[n_tm : n_tm + 6]
            x_ref, lo_ref, hi_ref, s_ref, buf = refs[n_tm + 6 :]
            me = lax.axis_index("tm")
            for d in range(n_tm):
                start = pl.multiple_of(lax.rem(me - d + n_tm, n_tm) * block, block)
                for n in range(per):
                    for v in range(nv):
                        buf[n, v, pl.ds(start, block), :] = part_refs[d][n, v]
            lane = lax.broadcasted_iota(jnp.int32, (ROWS, lanes), 1)
            for n in range(per):
                natural = jnp.concatenate([buf[n, v] for v in range(nv)], axis=1)
                moved = reorder(order_ref[...], natural, 2)
                terms = []
                for v in range(nv):
                    c = (first + n) * nv + v
                    column = jnp.broadcast_to(col_ref[:, c : c + 1], (ROWS, lanes))
                    term = moved[:, v * lanes : (v + 1) * lanes] + jnp.where(lane == 0, column, 0.0)
                    s_ref[n, v] = term
                    terms.append(term)
                for v in range(nv):
                    weights = [p_ref[first + n, v, pl.ds(w, 1), :] for w in range(nv)]
                    x = whole(tlo_ref, t_ref, thi_ref, first + n, first + n, v) - mixed(weights, terms)
                    x_ref[n, v] = x
                    lo_ref[n, v] = x[0:FACE]
                    hi_ref[n, v] = x[HIGH:ROWS]

        return call(
            kernel,
            [
                shape(per, nv, ROWS, lanes),
                shape(per, nv, FACE, lanes),
                shape(per, nv, FACE, lanes),
                shape(per, nv, ROWS, lanes),
            ],
            list(parts) + [t0, tlo, thi, precond, inlet_cols, order_b],
            "v" * (n_tm + 6),
            scratch=[pltpu.VMEM((per, nv, ROWS, lanes), F32)],
            name="first_pass",
        )

    def write_out(moved_ref, out_ref, sem, first, work):
        copies = []
        for n in range(per):
            work(n)
            for v in range(nv):
                copy = pltpu.make_async_copy(
                    moved_ref.at[n, v, pl.ds(0, nodes), :], out_ref.at[first + n, v, :, 0, :], sem.at[n, v]
                )
                copy.start()
                copies.append(copy)
        for copy in copies:
            copy.wait()

    def last_bulk(z, lo, hi, extra, first, out):
        def kernel(*refs):
            z_ref, lo_ref, hi_ref, m_ref, coef_ref, lhs_ref, masks_ref, extra_ref, back_ref = refs[:9]
            r_ref, out_ref, buf, sem = refs[-4:]
            metric_value = m_ref[...]

            def work(n):
                x = [whole(lo_ref, z_ref, hi_ref, n, n, v) for v in range(nv)]
                moved = reorder(back_ref[...], jnp.concatenate(x, axis=1), 3)
                for v in range(nv):
                    buf[n, v] = moved[:, v * lanes : (v + 1) * lanes]

            def residual(n, carry):
                x = [whole(lo_ref, z_ref, hi_ref, n, n, v) for v in range(nv)]
                res = bulk(x, coef_ref, lhs_ref, masks_ref, metric_value)
                for v in range(nv):
                    r_ref[n, v] = res[v] + extra_ref[n, v]
                return carry

            lax.fori_loop(0, per, residual, 0)
            write_out(buf, out_ref, sem, first, work)

        ins = [z, lo, hi, metric, coef, lhs, masks, extra, back_b] + ([] if out is None else [out])
        return call(
            kernel,
            [shape(per, nv, ROWS, lanes), shape(inst, nv, nodes, 1, lanes)],
            ins,
            "vvvvsvvvv" + ("" if out is None else "a"),
            out_spaces="va",
            scratch=[pltpu.VMEM((per, nv, ROWS, lanes), F32), pltpu.SemaphoreType.DMA((per, nv))],
            flops=bulk_flops * per,
            alias=None if out is None else {9: 1},
            name="last_bulk",
        )

    def last_faces(r, lo, hi, below, above, first, out):
        def kernel(*refs):
            r_ref, lo_ref, hi_ref, below_ref, above_ref, coef_ref, mf_ref, back_ref = refs[:8]
            out_ref, buf, sem = refs[-3:]

            def work(n):
                lows, highs = face_terms(n, lo_ref, hi_ref, below_ref, above_ref, coef_ref, mf_ref)
                full = [
                    jnp.concatenate(
                        [
                            r_ref[n, v, 0:FACE, :] + lows[v],
                            r_ref[n, v, FACE:HIGH, :],
                            r_ref[n, v, HIGH:ROWS, :] + highs[v],
                        ],
                        axis=0,
                    )
                    for v in range(nv)
                ]
                moved = reorder(back_ref[...], jnp.concatenate(full, axis=1), 2)
                for v in range(nv):
                    buf[n, v] = moved[:, v * lanes : (v + 1) * lanes]

            write_out(buf, out_ref, sem, first, work)

        ins = [r, lo, hi, below, above, coef, metric_face, back_b] + ([] if out is None else [out])
        return call(
            kernel,
            [shape(inst, nv, nodes, 1, lanes)],
            ins,
            "vvvvvsvv" + ("" if out is None else "a"),
            out_spaces="a",
            scratch=[pltpu.VMEM((per, nv, ROWS, lanes), F32), pltpu.SemaphoreType.DMA((per, nv))],
            alias=None if out is None else {8: 0},
            name="last_faces",
        )[0]

    new_state, final_residual = None, None
    for g in range(groups):
        first = g * per
        z, lo, hi, spec = first_pass(spectral[g], first)
        for sweep in range(PASSES):
            below, above = swap_faces(lo, hi)
            extra = spec if own_circ else spec + circ_extra(z, lo, hi)
            if sweep < PASSES - 1:
                z = advance(z, lo, hi, extra, first, per)
                lo, hi = close_faces(z, lo, hi, below, above, first, per)
            else:
                res, new_state = last_bulk(z, lo, hi, extra, first, new_state)
                final_residual = last_faces(res, lo, hi, below, above, first, final_residual)
    return (new_state.reshape(state.shape), final_residual.reshape(state.shape))


def solution(mesh):
    in_specs = (
        P("tm", None, "elem", None, None),
        P("elem", None, None),
        P(),
        P("tm", None, None, "elem", None),
        P("tm", None, "elem", None),
    )
    out_specs = (P("tm", None, "elem", None, None), P("tm", None, "elem", None, None))
    return jax.shard_map(
        per_device, mesh=mesh, in_specs=in_specs, out_specs=out_specs, check_vma=False
    )
```

```python
import math

import jax
import jax.numpy as jnp
import ml_dtypes
import numpy as np
from jax import lax
from jax.experimental import pallas as pl
from jax.experimental.pallas import tpu as pltpu
from jax.sharding import PartitionSpec as P

PR = 8
PASSES = 3
GROUPS = 2
ROWS = 128
FACE = 32
HIGH = 96

F32 = jnp.float32
BF16 = jnp.bfloat16


def gll_derivative():
    points = np.array([-1.0, -math.sqrt(3.0 / 7.0), 0.0, math.sqrt(3.0 / 7.0), 1.0])
    legendre = (35.0 * points**4 - 30.0 * points**2 + 3.0) / 8.0
    identity = np.eye(5, dtype=bool)
    spacing = np.where(identity, 1.0, points[:, None] - points[None, :])
    matrix = legendre[:, None] / legendre[None, :] / spacing
    corner = np.array([-5.0, 0.0, 0.0, 0.0, 5.0])[None, :]
    return np.where(identity, corner, matrix)


def coupling_value(offset, count):
    offset = offset % count
    if offset == 0:
        return 0.0
    angle = math.pi * offset / count
    return 0.5 * (-1.0) ** offset * math.cos(angle) / math.sin(angle)


FIRST = ((8, 16), (24, 40), (104, 112))
LAST = ((16, 24), (40, 56), (112, 120))
ENDS = 64


def node_rows():
    rows = np.zeros((5, 5, 5), dtype=np.int64)
    face_rest = list(range(0, 11)) + [16, 17, 18, 24]
    rest = [40] + list(range(56, HIGH)) + list(range(HIGH + 25, ROWS))
    face_used, used = 0, 0
    for i in range(5):
        for k in range(5):
            if k in (0, 4):
                local = (11 if k == 0 else 19) + i
            else:
                local = face_rest[face_used]
                face_used += 1
            rows[i, 0, k], rows[i, 4, k] = local, HIGH + local
            for j in range(1, 4):
                if k in (0, 4):
                    rows[i, j, k] = (25 if k == 0 else 41) + 3 * i + j - 1
                else:
                    rows[i, j, k] = rest[used]
                    used += 1
    return rows.reshape(125)


def end_rows():
    return [r for part in (FIRST, LAST) for a, b in part for r in range(a, b)]


def tables(own_circ):
    table = gll_derivative()
    eye = np.eye(5)
    first, last = np.diag([1.0, 0, 0, 0, 0]), np.diag([0, 0, 0, 0, 1.0])
    to_first, to_last = np.zeros((5, 5)), np.zeros((5, 5))
    to_first[0, 4] = 1.0
    to_last[4, 0] = 1.0

    def along(matrix, direction):
        parts = [eye, eye, eye]
        parts[direction] = matrix
        return np.kron(np.kron(parts[0], parts[1]), parts[2])

    rows = node_rows()
    order = np.zeros((ROWS, ROWS))
    order[rows, np.arange(125)] = 1.0

    def placed(matrix):
        return order[:, :125] @ matrix @ order[:, :125].T

    mix, damp = [], []
    for d in range(3):
        mix.append(placed(along(table - 5.0 * last + 5.0 * first, d)))
        damp.append(placed(along(5.0 * last + 5.0 * first, d)))
    if own_circ:
        mix[0] = mix[0] + placed(along(5.0 * to_last - 5.0 * to_first, 0))
        damp[0] = damp[0] + placed(along(-5.0 * to_last - 5.0 * to_first, 0))
    ends = end_rows()
    axial_mix = placed(along(5.0 * to_last - 5.0 * to_first, 2))[:, ends]
    axial_damp = placed(along(-5.0 * to_last - 5.0 * to_first, 2))[:, ends]
    none = np.zeros((ROWS, ENDS))

    def pair(matrix):
        return [np.concatenate([matrix, none], 1), np.concatenate([none, matrix], 1)]

    fluxes = np.stack(mix + pair(axial_mix)).astype(np.float32)
    dampers = np.stack(damp + pair(axial_damp)).astype(np.float32)
    return order, fluxes, dampers


def halves(values):
    high = values.astype(BF16)
    low = (values - high.astype(F32)).astype(BF16)
    return high, low


def dot32(a, b):
    return jnp.dot(a, b, preferred_element_type=F32)


def reorder(matrix, values, terms):
    total = None
    for _ in range(terms):
        part = values.astype(BF16)
        moved = dot32(matrix, part)
        total = moved if total is None else total + moved
        values = values - part.astype(F32)
    return total


def mixed(weights, parts):
    total = weights[0] * parts[0]
    for weight, part in zip(weights[1:], parts[1:]):
        total = total + weight * part
    return total


VMEM_LIMIT = 20 * 2**20
VMEM_ALONE = 56 * 2**20


def call(kernel, outs, ins, in_spaces, out_spaces=None, scratch=(), flops=0, alias=None, name=None, limit=VMEM_LIMIT):
    out_spaces = out_spaces or ["v"] * len(outs)
    space = {"v": pltpu.VMEM, "s": pltpu.SMEM, "a": pl.ANY, "h": pltpu.HBM}
    nbytes = sum(int(np.prod(x.shape)) * x.dtype.itemsize for x in list(ins) + list(outs))
    return pl.pallas_call(
        kernel,
        out_shape=outs,
        in_specs=[pl.BlockSpec(memory_space=space[s]) for s in in_spaces],
        out_specs=[pl.BlockSpec(memory_space=space[s]) for s in out_spaces],
        scratch_shapes=list(scratch),
        input_output_aliases=alias or {},
        compiler_params=pltpu.CompilerParams(vmem_limit_bytes=limit),
        cost_estimate=pl.CostEstimate(flops=flops, bytes_accessed=nbytes, transcendentals=0),
        name=name,
    )(*ins)


def shape(*dims, dtype=F32):
    return jax.ShapeDtypeStruct(dims, dtype)


def per_device(state, metric_scale, flux_jacobians, preconditioner, inflow):
    inst, nv, _, nodes, lanes = state.shape
    n_tm = lax.axis_size("tm")
    n_elem = lax.axis_size("elem")
    count = inst * n_tm
    own_circ = n_elem == PR
    block = ROWS // n_tm
    groups = GROUPS if inst % GROUPS == 0 else 1
    per = inst // groups
    order, flux_table, damp_table = tables(own_circ)
    order_b = order.astype(ml_dtypes.bfloat16)
    back_b = np.ascontiguousarray(order.T).astype(ml_dtypes.bfloat16)
    pairs = (nv + 1) // 2
    depth = nv * ROWS + pairs * 2 * ENDS
    node_row = node_rows()
    inlet_table = np.zeros((ROWS, ROWS), dtype=np.float32)
    inlet_table[node_row[0::5], np.arange(25)] = 1.0

    damping = jnp.max(jnp.sum(jnp.abs(flux_jacobians), axis=2), axis=1)
    coef = jnp.concatenate([flux_jacobians.reshape(-1), damping])
    precond = preconditioner.reshape(inst, nv, nv, lanes)
    inlet = jnp.pad(inflow.reshape(inst * nv, 25), ((0, ROWS - inst * nv), (0, ROWS - 25)))
    mix_index = np.full((ROWS, ROWS), -1, dtype=np.int32)
    for n in range(inst):
        for v in range(nv):
            for w in range(nv):
                mix_index[n * nv + w, n * nv + v] = v * nv + w

    def jac(ref, d, v, w):
        return ref[(d * nv + v) * nv + w]

    def damp(ref, d):
        return ref[3 * nv * nv + d]

    state_rows = state.reshape(inst, nv, nodes, 1, lanes)
    starts = [min(q * block, nodes - block) for q in range(n_tm)]
    spectral_order = np.zeros((ROWS, ROWS))
    for q in range(n_tm):
        for r in range(block):
            if starts[q] + r >= q * block:
                spectral_order[:, q * block + r] = order[:, starts[q] + r]

    def pack_kernel(state_ref, *refs):
        outs, sem = refs[:n_tm], refs[n_tm]
        me = lax.axis_index("tm")
        copies = []
        for d in range(n_tm):
            start = jnp.minimum(lax.rem(me + d, n_tm) * block, nodes - block)
            for n in range(inst):
                for v in range(nv):
                    copies.append(
                        pltpu.make_async_copy(
                            state_ref.at[n, v, pl.ds(start, block), 0, :], outs[d].at[n, v], sem.at[d, n, v]
                        )
                    )
        for copy in copies:
            copy.start()
        for copy in copies:
            copy.wait()

    piece = shape(inst, nv, block, lanes)
    pieces = call(
        pack_kernel,
        [piece] * n_tm,
        [state_rows],
        "h",
        scratch=[pltpu.SemaphoreType.DMA((n_tm, inst, nv))],
        name="pack",
        limit=VMEM_ALONE,
    )

    def after(x, *before):
        return lax.optimization_barrier((x, *before))[0]

    def along_tm(x, d):
        return lax.ppermute(x, "tm", [(i, (i + d) % n_tm) for i in range(n_tm)])

    def along_elem(x, d):
        return lax.ppermute(x, "elem", [(i, (i + d) % n_elem) for i in range(n_elem)])

    arrived = [pieces[0]] + [None] * (n_tm - 1)
    for d in sorted(range(1, n_tm), key=lambda d: abs(2 * d - n_tm)):
        arrived[d] = along_tm(pieces[d], d)

    def prep_kernel(
        state_ref, metric_ref, coef_ref, order_ref, flux_ref, damp_ref, inlet_ref, inlet_table_ref, mix_ref, p_ref,
        x_ref, lo_ref, hi_ref, m_ref, mf_ref, lhs_ref, col_ref, fc_ref, pc_ref, padded_ref, buf, sem,
    ):
        buf[pl.ds(ROWS - 8, 8), :] = jnp.zeros((8, lanes), F32)
        padded_ref[:, :, pl.ds(ROWS - 8, 8), :] = jnp.zeros((inst, nv, 8, lanes), F32)
        copies = [
            pltpu.make_async_copy(metric_ref.at[:, 0, :], buf.at[pl.ds(0, nodes), :], sem.at[0]),
        ]
        for n in range(inst):
            for v in range(nv):
                copies.append(
                    pltpu.make_async_copy(
                        state_ref.at[n, v, :, 0, :],
                        padded_ref.at[n, v, pl.ds(0, nodes), :],
                        sem.at[1 + n * nv + v],
                    )
                )
        for copy in copies:
            copy.start()
        for copy in copies:
            copy.wait()
        metric = reorder(order_ref[...], buf[...], 3)
        m_ref[...] = metric
        row = lax.broadcasted_iota(jnp.int32, (FACE, lanes), 0)
        mf_ref[0] = jnp.where(row < 25, metric[0:FACE], 0.0)
        mf_ref[1] = jnp.where(row < 25, metric[HIGH:ROWS], 0.0)
        for v in range(nv):
            for w in range(nv):
                value, own = jac(coef_ref, 1, v, w), damp(coef_ref, 1) if v == w else 0.0
                fc_ref[0, v, pl.ds(w, 1), :] = jnp.full((1, lanes), -5.0 * (value + own), F32)
                fc_ref[1, v, pl.ds(w, 1), :] = jnp.full((1, lanes), 5.0 * (value - own), F32)
        for side in range(2):
            tables_of = [fc_ref[side, u] for u in range(nv)]
            for n in range(inst):
                for v in range(nv):
                    weights = [p_ref[n, v, pl.ds(u, 1), :] for u in range(nv)]
                    pc_ref[side, n, v] = mixed(weights, tables_of)
        for v in range(nv):
            rows = pl.ds(v * ROWS, ROWS)
            for w in range(nv):
                total = mixed([jac(coef_ref, d, v, w) for d in range(3)], [flux_ref[d] for d in range(3)])
                if v == w:
                    for d in range(3):
                        total = total + damp(coef_ref, d) * damp_ref[d]
                high, low = halves(total)
                at = w * ROWS
                lhs_ref[rows, pl.ds(at, ROWS)] = high
                lhs_ref[rows, pl.ds(depth + at, ROWS)] = low
            for c in range(pairs):
                total = jac(coef_ref, 2, v, 2 * c) * flux_ref[3]
                if 2 * c + 1 < nv:
                    total = total + jac(coef_ref, 2, v, 2 * c + 1) * flux_ref[4]
                if v // 2 == c:
                    total = total + damp(coef_ref, 2) * damp_ref[3 + v % 2]
                high, low = halves(total)
                at = nv * ROWS + c * 2 * ENDS
                lhs_ref[rows, pl.ds(at, 2 * ENDS)] = high
                lhs_ref[rows, pl.ds(depth + at, 2 * ENDS)] = low
        cols = lax.dot_general(
            inlet_table_ref[...],
            inlet_ref[...],
            (((1,), (1,)), ((), ())),
            precision=lax.Precision.HIGHEST,
            preferred_element_type=F32,
        )
        blend = jnp.zeros((ROWS, ROWS), F32)
        for v in range(nv):
            for w in range(nv):
                value = jac(coef_ref, 2, v, w)
                if v == w:
                    value = value + damp(coef_ref, 2)
                blend = jnp.where(mix_ref[...] == v * nv + w, -5.0 * value, blend)
        cols = jnp.dot(cols, blend, precision=lax.Precision.HIGHEST, preferred_element_type=F32)
        col_ref[...] = metric[:, 0:1] * cols
        for n in range(inst):
            natural = jnp.concatenate([padded_ref[n, v] for v in range(nv)], axis=1)
            moved = reorder(order_ref[...], natural, 3)
            for v in range(nv):
                part = moved[:, v * lanes : (v + 1) * lanes]
                x_ref[n, v] = part
                lo_ref[n, v] = part[0:FACE]
                hi_ref[n, v] = part[HIGH:ROWS]

    x0, lo0, hi0, metric, metric_face, lhs, inlet_cols, face_coef, face_update = call(
        prep_kernel,
        [
            shape(inst, nv, ROWS, lanes),
            shape(inst, nv, FACE, lanes),
            shape(inst, nv, FACE, lanes),
            shape(ROWS, lanes),
            shape(2, FACE, lanes),
            shape(nv * ROWS, 2 * depth, dtype=BF16),
            shape(ROWS, ROWS),
            shape(2, nv, nv, lanes),
            shape(2, inst, nv, nv, lanes),
        ],
        [
            state_rows,
            metric_scale.reshape(nodes, 1, lanes),
            coef,
            order_b,
            flux_table,
            damp_table,
            inlet,
            inlet_table,
            mix_index,
            precond,
        ],
        "hhsvvvvvvv",
        scratch=[
            pltpu.VMEM((inst, nv, ROWS, lanes), F32),
            pltpu.VMEM((ROWS, lanes), F32),
            pltpu.SemaphoreType.DMA((1 + inst * nv,)),
        ],
        name="prep",
    )

    def bulk(xs, lhs_ref):
        cols = []
        lane = lax.broadcasted_iota(jnp.int32, (ENDS // 2, lanes), 1)
        for x in xs:
            ends = []
            for part in x:
                first = jnp.concatenate([part[a:b] for a, b in FIRST], axis=0)
                last = jnp.concatenate([part[a:b] for a, b in LAST], axis=0)
                ends.append(jnp.where(lane == lanes - 1, last, pltpu.roll(first, lanes - 1, 1)))
                ends.append(jnp.where(lane == 0, 0.0, pltpu.roll(last, 1, 1)))
            if nv % 2:
                ends.append(jnp.zeros((ENDS, lanes), F32))
            cols.append(jnp.concatenate(list(x) + ends, axis=0))
        high, low = halves(jnp.concatenate(cols, axis=1) if len(cols) > 1 else cols[0])
        both = dot32(lhs_ref[...], jnp.concatenate([high, high], axis=0))
        return both + dot32(lhs_ref[:, 0:depth], low)

    def block_of(result, n, v):
        return result[v * ROWS : (v + 1) * ROWS, n * lanes : (n + 1) * lanes]

    def whole(lo_ref, z_ref, hi_ref, n, at, v):
        return jnp.concatenate([lo_ref[n, v], z_ref[at, v, FACE:HIGH, :], hi_ref[n, v]], axis=0)

    bulk_flops = 2 * 3 * depth * nv * ROWS * lanes

    def advance(z, lo, hi, extra, first, size):
        def kernel(*refs):
            z_ref, lo_ref, hi_ref, m_ref, p_ref, lhs_ref = refs[:6]
            out_ref = refs[-1]
            metric_value = m_ref[...]
            for at in range(0, size, 2):
                ids = list(range(at, min(at + 2, size)))
                xs = [[whole(lo_ref, z_ref, hi_ref, n, n, v) for v in range(nv)] for n in ids]
                result = bulk(xs, lhs_ref)
                for m, n in enumerate(ids):
                    res = [metric_value * block_of(result, m, v) for v in range(nv)]
                    if extra is not None:
                        res = [res[v] + refs[6][n, v] for v in range(nv)]
                    for v in range(nv):
                        weights = [p_ref[first + n, v, pl.ds(w, 1), :] for w in range(nv)]
                        out_ref[n, v] = xs[m][v] - mixed(weights, res)

        ins = [z, lo, hi, metric, precond, lhs]
        ins = ins + ([] if extra is None else [extra])
        return call(
            kernel,
            [shape(size, nv, ROWS, lanes)],
            ins,
            "vvvvvv" + ("" if extra is None else "v"),
            flops=bulk_flops * size,
            name="advance",
        )[0]

    def face_terms(n, lo_ref, hi_ref, below_ref, above_ref, table_of, mf_ref):
        position = lax.rem(lax.axis_index("elem") + PR // 2, PR)
        low_w, high_w = [], []
        for v in range(nv):
            sign = -1.0 if v == 2 else 1.0
            low_w.append(jnp.where(position == 0, sign * lo_ref[n, v], below_ref[n, v]))
            high_w.append(jnp.where(position == PR - 1, sign * hi_ref[n, v], above_ref[n, v]))
        lows, highs = [], []
        for v in range(nv):
            lows.append(mf_ref[0] * mixed([table_of(0, v, w) for w in range(nv)], low_w))
            highs.append(mf_ref[1] * mixed([table_of(1, v, w) for w in range(nv)], high_w))
        return lows, highs

    def swap_faces(lo, hi):
        return along_elem(hi, 1), along_elem(lo, -1)

    def close_faces(z, lo, hi, below, above, first, size):
        def kernel(z_ref, lo_ref, hi_ref, below_ref, above_ref, mf_ref, pc_ref, nlo_ref, nhi_ref):
            for n in range(size):

                def table_of(side, v, w, n=n):
                    return pc_ref[side, first + n, v, pl.ds(w, 1), :]

                lows, highs = face_terms(n, lo_ref, hi_ref, below_ref, above_ref, table_of, mf_ref)
                for v in range(nv):
                    nlo_ref[n, v] = z_ref[n, v, 0:FACE, :] - lows[v]
                    nhi_ref[n, v] = z_ref[n, v, HIGH:ROWS, :] - highs[v]

        return call(
            kernel,
            [shape(size, nv, FACE, lanes)] * 2,
            [z, lo, hi, below, above, metric_face, face_update],
            "v" * 7,
            name="faces",
        )

    def circ_extra(z, lo, hi):
        x = jnp.concatenate([lo, z[:, :, FACE:HIGH], hi], axis=2)
        picks = np.zeros((2, 25, ROWS), dtype=np.float32)
        picks[0, np.arange(25), node_row[0:25]] = 1.0
        picks[1, np.arange(25), node_row[100:125]] = 1.0
        exact = lax.Precision.HIGHEST

        def picked(which):
            return jnp.einsum("pq,nvqa->nvpa", picks[which], x, precision=exact)

        def mix(values):
            return jnp.einsum("vw,nwqa->nvqa", flux_jacobians[0], values, precision=exact)

        def placed(which, values):
            return jnp.einsum("pq,nvpa->nvqa", picks[which], values, precision=exact)

        above, below = along_elem(picked(0), -PR), along_elem(picked(1), PR)
        high_term = 5.0 * (mix(above) - damping[0] * above)
        low_term = -5.0 * (mix(below) + damping[0] * below)
        return metric * (placed(1, high_term) + placed(0, low_term))

    below0, above0 = swap_faces(lo0, hi0)
    t0 = advance(x0, lo0, hi0, None if own_circ else circ_extra(x0, lo0, hi0), 0, inst)
    tlo, thi = close_faces(t0, lo0, hi0, below0, above0, 0, inst)

    half_pair = n_tm % 2 == 0

    def weight(offset, sign):
        return 0.5 * (coupling_value(offset, count) + sign * coupling_value(offset + count // 2, count))

    def weighted(terms):
        terms = [(c, x) for c, x in terms if abs(c) > 1e-12]
        return mixed([c for c, _ in terms], [x for _, x in terms])

    def coupling_kernel(*refs):
        x_refs, outs = refs[:n_tm], refs[n_tm:]

        def body(step, carry):
            v, rows = step // (block // 8), pl.ds(pl.multiple_of((step % (block // 8)) * 8, 8), 8)
            x = [[x_refs[d][i, v, rows, :] for i in range(inst)] for d in range(n_tm)]
            if half_pair:
                half = n_tm // 2
                sources = [(d, i) for d in range(half) for i in range(inst)]
                sums = [x[d][i] + x[d + half][i] for d, i in sources]
                diffs = [x[d][i] - x[d + half][i] for d, i in sources]
                for e in range(half):
                    for j in range(inst):
                        offsets = [inst * (e + d) + j - i for d, i in sources]
                        even = weighted([(weight(o, 1), s) for o, s in zip(offsets, sums)])
                        odd = weighted([(weight(o, -1), s) for o, s in zip(offsets, diffs)])
                        outs[e * groups + j // per][j % per, v, rows, :] = even + odd
                        outs[(e + half) * groups + j // per][j % per, v, rows, :] = even - odd
            else:
                sources = [(d, i) for d in range(n_tm) for i in range(inst)]
                for e in range(n_tm):
                    for j in range(inst):
                        offsets = [inst * (e + d) + j - i for d, i in sources]
                        outs[e * groups + j // per][j % per, v, rows, :] = weighted(
                            [(coupling_value(o, count), x[d][i]) for o, (d, i) in zip(offsets, sources)]
                        )
            return carry

        lax.fori_loop(0, nv * (block // 8), body, 0)

    coupled = call(
        coupling_kernel,
        [shape(per, nv, block, lanes)] * (n_tm * groups),
        arrived,
        "v" * n_tm,
        name="coupling",
    )
    spectral = [[coupled[g]] + [None] * (n_tm - 1) for g in range(groups)]
    for g in range(groups):
        for e in sorted(range(1, n_tm), key=lambda e: abs(2 * e - n_tm)):
            spectral[g][e] = along_tm(coupled[e * groups + g], e)

    def first_pass(parts, first):
        def kernel(*refs):
            part_refs = refs[:n_tm]
            t_ref, tlo_ref, thi_ref, p_ref, col_ref, order_ref = refs[n_tm : n_tm + 6]
            x_ref, lo_ref, hi_ref, s_ref, buf = refs[n_tm + 6 :]
            me = lax.axis_index("tm")
            for d in range(n_tm):
                start = pl.multiple_of(lax.rem(me - d + n_tm, n_tm) * block, block)
                for n in range(per):
                    for v in range(nv):
                        buf[n, v, pl.ds(start, block), :] = part_refs[d][n, v]
            lane = lax.broadcasted_iota(jnp.int32, (ROWS, lanes), 1)
            for n in range(per):
                natural = jnp.concatenate([buf[n, v] for v in range(nv)], axis=1)
                moved = reorder(order_ref[...], natural, 2)
                terms = []
                for v in range(nv):
                    c = (first + n) * nv + v
                    column = jnp.broadcast_to(col_ref[:, c : c + 1], (ROWS, lanes))
                    term = moved[:, v * lanes : (v + 1) * lanes] + jnp.where(lane == 0, column, 0.0)
                    s_ref[n, v] = term
                    terms.append(term)
                for v in range(nv):
                    weights = [p_ref[first + n, v, pl.ds(w, 1), :] for w in range(nv)]
                    x = whole(tlo_ref, t_ref, thi_ref, first + n, first + n, v) - mixed(weights, terms)
                    x_ref[n, v] = x
                    lo_ref[n, v] = x[0:FACE]
                    hi_ref[n, v] = x[HIGH:ROWS]

        return call(
            kernel,
            [
                shape(per, nv, ROWS, lanes),
                shape(per, nv, FACE, lanes),
                shape(per, nv, FACE, lanes),
                shape(per, nv, ROWS, lanes),
            ],
            list(parts) + [t0, tlo, thi, precond, inlet_cols, spectral_order.astype(ml_dtypes.bfloat16)],
            "v" * (n_tm + 6),
            scratch=[pltpu.VMEM((per, nv, ROWS, lanes), F32)],
            name="first_pass",
        )

    def write_out(moved_ref, out_ref, sem, first, work, meanwhile=None):
        copies = []
        for n in range(per):
            work(n)
            for v in range(nv):
                copy = pltpu.make_async_copy(
                    moved_ref.at[n, v, pl.ds(0, nodes), :], out_ref.at[first + n, v, :, 0, :], sem.at[n, v]
                )
                copy.start()
                copies.append(copy)
        if meanwhile is not None:
            meanwhile()
        for copy in copies:
            copy.wait()

    def last_bulk(z, lo, hi, extra, first, out):
        def kernel(*refs):
            z_ref, lo_ref, hi_ref, m_ref, lhs_ref, extra_ref, back_ref = refs[:7]
            r_ref, out_ref, buf, sem = refs[-4:]
            metric_value = m_ref[...]

            def work(n):
                x = [whole(lo_ref, z_ref, hi_ref, n, n, v) for v in range(nv)]
                moved = reorder(back_ref[...], jnp.concatenate(x, axis=1), 3)
                for v in range(nv):
                    buf[n, v] = moved[:, v * lanes : (v + 1) * lanes]

            def residual():
                for at in range(0, per, 2):
                    ids = list(range(at, min(at + 2, per)))
                    xs = [[whole(lo_ref, z_ref, hi_ref, n, n, v) for v in range(nv)] for n in ids]
                    result = bulk(xs, lhs_ref)
                    for m, n in enumerate(ids):
                        for v in range(nv):
                            r_ref[n, v] = metric_value * block_of(result, m, v) + extra_ref[n, v]

            write_out(buf, out_ref, sem, first, work, residual)

        ins = [z, lo, hi, metric, lhs, extra, back_b] + ([] if out is None else [out])
        return call(
            kernel,
            [shape(per, nv, ROWS, lanes), shape(inst, nv, nodes, 1, lanes)],
            ins,
            "vvvvvvv" + ("" if out is None else "a"),
            out_spaces="va",
            scratch=[pltpu.VMEM((per, nv, ROWS, lanes), F32), pltpu.SemaphoreType.DMA((per, nv))],
            flops=bulk_flops * per,
            alias=None if out is None else {7: 1},
            name="last_bulk",
        )

    def last_faces(r, lo, hi, below, above, first, out):
        def kernel(*refs):
            r_ref, lo_ref, hi_ref, below_ref, above_ref, mf_ref, fc_ref, back_ref = refs[:8]
            out_ref, buf, sem = refs[-3:]

            def table_of(side, v, w):
                return fc_ref[side, v, pl.ds(w, 1), :]

            def work(n):
                lows, highs = face_terms(n, lo_ref, hi_ref, below_ref, above_ref, table_of, mf_ref)
                full = [
                    jnp.concatenate(
                        [
                            r_ref[n, v, 0:FACE, :] + lows[v],
                            r_ref[n, v, FACE:HIGH, :],
                            r_ref[n, v, HIGH:ROWS, :] + highs[v],
                        ],
                        axis=0,
                    )
                    for v in range(nv)
                ]
                moved = reorder(back_ref[...], jnp.concatenate(full, axis=1), 2)
                for v in range(nv):
                    buf[n, v] = moved[:, v * lanes : (v + 1) * lanes]

            write_out(buf, out_ref, sem, first, work)

        ins = [r, lo, hi, below, above, metric_face, face_coef, back_b] + ([] if out is None else [out])
        return call(
            kernel,
            [shape(inst, nv, nodes, 1, lanes)],
            ins,
            "vvvvvvvv" + ("" if out is None else "a"),
            out_spaces="a",
            scratch=[pltpu.VMEM((per, nv, ROWS, lanes), F32), pltpu.SemaphoreType.DMA((per, nv))],
            alias=None if out is None else {8: 0},
            name="last_faces",
        )[0]

    new_state, final_residual = None, None
    chains, last = [None] * groups, None

    def begin(g):
        parts = spectral[g] if last is None else [after(spectral[g][0], last)] + spectral[g][1:]
        z, lo, hi, spec = first_pass(parts, g * per)
        chains[g] = (z, lo, hi, swap_faces(lo, hi), spec)
        return lo

    def local_part(g, count_done):
        nonlocal new_state
        z, lo, hi, swapped, spec = chains[g]
        extra = after(spec if own_circ else spec + circ_extra(z, lo, hi), last)
        if count_done < PASSES - 1:
            z = advance(z, lo, hi, extra, g * per, per)
        else:
            z, new_state = last_bulk(z, lo, hi, extra, g * per, new_state)
        chains[g] = (z, lo, hi, swapped, spec)
        return z

    def face_part(g, count_done):
        nonlocal final_residual
        z, lo, hi, (below, above), spec = chains[g]
        z = after(z, last)
        if count_done < PASSES - 1:
            lo, hi = close_faces(z, lo, hi, below, above, g * per, per)
            chains[g] = (z, lo, hi, swap_faces(lo, hi), spec)
            return lo
        final_residual = last_faces(z, lo, hi, below, above, g * per, final_residual)
        return final_residual

    for g in range(groups - 1):
        last = begin(g)
        last = local_part(g, 0)
    last = begin(groups - 1)
    for count_done in range(PASSES):
        for g in range(groups - 1):
            last = face_part(g, count_done)
        last = local_part(groups - 1, count_done)
        last = face_part(groups - 1, count_done)
        if count_done < PASSES - 1:
            for g in range(groups - 1):
                last = local_part(g, count_done + 1)
    return (new_state.reshape(state.shape), final_residual.reshape(state.shape))


def solution(mesh):
    in_specs = (
        P("tm", None, "elem", None, None),
        P("elem", None, None),
        P(),
        P("tm", None, None, "elem", None),
        P("tm", None, "elem", None),
    )
    out_specs = (P("tm", None, "elem", None, None), P("tm", None, "elem", None, None))
    return jax.shard_map(
        per_device, mesh=mesh, in_specs=in_specs, out_specs=out_specs, check_vma=False
    )
```

```python
import math

import jax
import jax.numpy as jnp
import ml_dtypes
import numpy as np
from jax import lax
from jax.experimental import pallas as pl
from jax.experimental.pallas import tpu as pltpu
from jax.sharding import PartitionSpec as P

PR = 8
PASSES = 3
GROUPS = 2
ROWS = 128
FACE = 32
HIGH = 96

F32 = jnp.float32
BF16 = jnp.bfloat16


def gll_derivative():
    points = np.array([-1.0, -math.sqrt(3.0 / 7.0), 0.0, math.sqrt(3.0 / 7.0), 1.0])
    legendre = (35.0 * points**4 - 30.0 * points**2 + 3.0) / 8.0
    identity = np.eye(5, dtype=bool)
    spacing = np.where(identity, 1.0, points[:, None] - points[None, :])
    matrix = legendre[:, None] / legendre[None, :] / spacing
    corner = np.array([-5.0, 0.0, 0.0, 0.0, 5.0])[None, :]
    return np.where(identity, corner, matrix)


def coupling_value(offset, count):
    offset = offset % count
    if offset == 0:
        return 0.0
    angle = math.pi * offset / count
    return 0.5 * (-1.0) ** offset * math.cos(angle) / math.sin(angle)


FIRST = ((8, 16), (24, 40), (104, 112))
LAST = ((16, 24), (40, 56), (112, 120))
ENDS = 64


def node_rows():
    rows = np.zeros((5, 5, 5), dtype=np.int64)
    face_rest = list(range(0, 11)) + [16, 17, 18, 24]
    rest = [40] + list(range(56, HIGH)) + list(range(HIGH + 25, ROWS))
    face_used, used = 0, 0
    for i in range(5):
        for k in range(5):
            if k in (0, 4):
                local = (11 if k == 0 else 19) + i
            else:
                local = face_rest[face_used]
                face_used += 1
            rows[i, 0, k], rows[i, 4, k] = local, HIGH + local
            for j in range(1, 4):
                if k in (0, 4):
                    rows[i, j, k] = (25 if k == 0 else 41) + 3 * i + j - 1
                else:
                    rows[i, j, k] = rest[used]
                    used += 1
    return rows.reshape(125)


def end_rows():
    return [r for part in (FIRST, LAST) for a, b in part for r in range(a, b)]


def tables(own_circ):
    table = gll_derivative()
    eye = np.eye(5)
    first, last = np.diag([1.0, 0, 0, 0, 0]), np.diag([0, 0, 0, 0, 1.0])
    to_first, to_last = np.zeros((5, 5)), np.zeros((5, 5))
    to_first[0, 4] = 1.0
    to_last[4, 0] = 1.0

    def along(matrix, direction):
        parts = [eye, eye, eye]
        parts[direction] = matrix
        return np.kron(np.kron(parts[0], parts[1]), parts[2])

    rows = node_rows()
    order = np.zeros((ROWS, ROWS))
    order[rows, np.arange(125)] = 1.0

    def placed(matrix):
        return order[:, :125] @ matrix @ order[:, :125].T

    mix, damp = [], []
    for d in range(3):
        mix.append(placed(along(table - 5.0 * last + 5.0 * first, d)))
        damp.append(placed(along(5.0 * last + 5.0 * first, d)))
    if own_circ:
        mix[0] = mix[0] + placed(along(5.0 * to_last - 5.0 * to_first, 0))
        damp[0] = damp[0] + placed(along(-5.0 * to_last - 5.0 * to_first, 0))
    ends = end_rows()
    axial_mix = placed(along(5.0 * to_last - 5.0 * to_first, 2))[:, ends]
    axial_damp = placed(along(-5.0 * to_last - 5.0 * to_first, 2))[:, ends]
    none = np.zeros((ROWS, ENDS))

    def pair(matrix):
        return [np.concatenate([matrix, none], 1), np.concatenate([none, matrix], 1)]

    fluxes = np.stack(mix + pair(axial_mix)).astype(np.float32)
    dampers = np.stack(damp + pair(axial_damp)).astype(np.float32)
    return order, fluxes, dampers


def halves(values):
    high = values.astype(BF16)
    low = (values - high.astype(F32)).astype(BF16)
    return high, low


def dot32(a, b):
    return jnp.dot(a, b, preferred_element_type=F32)


def reorder(matrix, values, terms):
    total = None
    for _ in range(terms):
        part = values.astype(BF16)
        moved = dot32(matrix, part)
        total = moved if total is None else total + moved
        values = values - part.astype(F32)
    return total


def mixed(weights, parts):
    total = weights[0] * parts[0]
    for weight, part in zip(weights[1:], parts[1:]):
        total = total + weight * part
    return total


VMEM_LIMIT = 20 * 2**20
LONG = 2 * 10**9


def call(kernel, outs, ins, in_spaces, out_spaces=None, scratch=(), flops=0, alias=None, name=None):
    out_spaces = out_spaces or ["v"] * len(outs)
    space = {"v": pltpu.VMEM, "s": pltpu.SMEM, "a": pl.ANY, "h": pltpu.HBM}
    return pl.pallas_call(
        kernel,
        out_shape=outs,
        in_specs=[pl.BlockSpec(memory_space=space[s]) for s in in_spaces],
        out_specs=[pl.BlockSpec(memory_space=space[s]) for s in out_spaces],
        scratch_shapes=list(scratch),
        input_output_aliases=alias or {},
        compiler_params=pltpu.CompilerParams(vmem_limit_bytes=VMEM_LIMIT),
        cost_estimate=pl.CostEstimate(flops=max(flops, 1), bytes_accessed=1, transcendentals=0),
        name=name,
    )(*ins)


def shape(*dims, dtype=F32):
    return jax.ShapeDtypeStruct(dims, dtype)


def per_device(state, metric_scale, flux_jacobians, preconditioner, inflow):
    inst, nv, _, nodes, lanes = state.shape
    n_tm = lax.axis_size("tm")
    n_elem = lax.axis_size("elem")
    count = inst * n_tm
    own_circ = n_elem == PR
    block = ROWS // n_tm
    groups = GROUPS if inst % GROUPS == 0 else 1
    per = inst // groups
    order, flux_table, damp_table = tables(own_circ)
    order_b = order.astype(ml_dtypes.bfloat16)
    back_b = np.ascontiguousarray(order.T).astype(ml_dtypes.bfloat16)
    pairs = (nv + 1) // 2
    depth = nv * ROWS + pairs * 2 * ENDS
    node_row = node_rows()
    inlet_table = np.zeros((ROWS, ROWS), dtype=np.float32)
    inlet_table[node_row[0::5], np.arange(25)] = 1.0

    damping = jnp.max(jnp.sum(jnp.abs(flux_jacobians), axis=2), axis=1)
    coef = jnp.concatenate([flux_jacobians.reshape(-1), damping])
    precond = preconditioner.reshape(inst, nv, nv, lanes)
    inlet = jnp.pad(inflow.reshape(inst * nv, 25), ((0, ROWS - inst * nv), (0, ROWS - 25)))
    mix_index = np.full((ROWS, ROWS), -1, dtype=np.int32)
    for n in range(inst):
        for v in range(nv):
            for w in range(nv):
                mix_index[n * nv + w, n * nv + v] = v * nv + w

    def jac(ref, d, v, w):
        return ref[(d * nv + v) * nv + w]

    def damp(ref, d):
        return ref[3 * nv * nv + d]

    state_rows = state.reshape(inst, nv, nodes, 1, lanes)
    starts = [min(q * block, nodes - block) for q in range(n_tm)]
    spectral_order = np.zeros((ROWS, ROWS))
    for q in range(n_tm):
        for r in range(block):
            if starts[q] + r >= q * block:
                spectral_order[:, q * block + r] = order[:, starts[q] + r]

    def pack_kernel(state_ref, *refs):
        outs, sem = refs[:n_tm], refs[n_tm]
        me = lax.axis_index("tm")
        copies = []
        for d in range(n_tm):
            start = jnp.minimum(lax.rem(me + d, n_tm) * block, nodes - block)
            copies.append(
                pltpu.make_async_copy(state_ref.at[:, :, pl.ds(start, block), 0, :], outs[d], sem.at[d])
            )
        for copy in copies:
            copy.start()
        for copy in copies:
            copy.wait()

    piece = shape(inst, nv, block, lanes)
    pieces = call(
        pack_kernel,
        [piece] * n_tm,
        [state_rows],
        "h",
        scratch=[pltpu.SemaphoreType.DMA((n_tm,))],
        name="pack",
    )

    def after(x, *before):
        return lax.optimization_barrier((x, *before))[0]

    def along_tm(x, d):
        return lax.ppermute(x, "tm", [(i, (i + d) % n_tm) for i in range(n_tm)])

    def along_elem(x, d):
        return lax.ppermute(x, "elem", [(i, (i + d) % n_elem) for i in range(n_elem)])

    arrived = [pieces[0]] + [None] * (n_tm - 1)
    for d in sorted(range(1, n_tm), key=lambda d: abs(2 * d - n_tm)):
        arrived[d] = along_tm(pieces[d], d)

    scale_at = inst * nv + -(-inst * nv // (FACE // 8))

    def table_place(index):
        return inst * nv + index // (FACE // 8), 8 * (index % (FACE // 8))

    def prep_kernel(
        state_ref, metric_ref, coef_ref, order_ref, flux_ref, damp_ref, inlet_ref, inlet_table_ref, mix_ref, p_ref,
        x_ref, lo_ref, hi_ref, m_ref, mf_ref, lhs_ref, col_ref, fc_ref, pc_ref, low_table_ref, high_table_ref, padded_ref, buf, sem,
    ):
        buf[pl.ds(ROWS - 8, 8), :] = jnp.zeros((8, lanes), F32)
        padded_ref[:, :, pl.ds(ROWS - 8, 8), :] = jnp.zeros((inst, nv, 8, lanes), F32)
        copies = [
            pltpu.make_async_copy(metric_ref.at[:, 0, :], buf.at[pl.ds(0, nodes), :], sem.at[0]),
        ]
        for n in range(inst):
            for v in range(nv):
                copies.append(
                    pltpu.make_async_copy(
                        state_ref.at[n, v, :, 0, :],
                        padded_ref.at[n, v, pl.ds(0, nodes), :],
                        sem.at[1 + n * nv + v],
                    )
                )
        for copy in copies:
            copy.start()
        for copy in copies:
            copy.wait()
        metric = reorder(order_ref[...], buf[...], 3)
        m_ref[...] = metric
        row = lax.broadcasted_iota(jnp.int32, (FACE, lanes), 0)
        mf_ref[0] = jnp.where(row < 25, metric[0:FACE], 0.0)
        mf_ref[1] = jnp.where(row < 25, metric[HIGH:ROWS], 0.0)
        for v in range(nv):
            for w in range(nv):
                value, own = jac(coef_ref, 1, v, w), damp(coef_ref, 1) if v == w else 0.0
                fc_ref[0, v, pl.ds(w, 1), :] = jnp.full((1, lanes), -5.0 * (value + own), F32)
                fc_ref[1, v, pl.ds(w, 1), :] = jnp.full((1, lanes), 5.0 * (value - own), F32)
        for side in range(2):
            tables_of = [fc_ref[side, u] for u in range(nv)]
            for n in range(inst):
                for v in range(nv):
                    weights = [p_ref[n, v, pl.ds(u, 1), :] for u in range(nv)]
                    update = mixed(weights, tables_of)
                    pc_ref[side, n, v] = update
                    at, row = table_place(n * nv + v)
                    table_ref = (low_table_ref, high_table_ref)[side]
                    table_ref[at, pl.ds(row, 8), :] = jnp.concatenate(
                        [update, jnp.zeros((8 - nv, lanes), F32)], axis=0
                    )
            for spare in range(inst * nv, (scale_at - inst * nv) * (FACE // 8)):
                at, row = table_place(spare)
                table_ref[at, pl.ds(row, 8), :] = jnp.zeros((8, lanes), F32)
            table_ref[scale_at] = mf_ref[side]
        for v in range(nv):
            rows = pl.ds(v * ROWS, ROWS)
            for w in range(nv):
                total = mixed([jac(coef_ref, d, v, w) for d in range(3)], [flux_ref[d] for d in range(3)])
                if v == w:
                    for d in range(3):
                        total = total + damp(coef_ref, d) * damp_ref[d]
                high, low = halves(total)
                at = w * ROWS
                lhs_ref[rows, pl.ds(at, ROWS)] = high
                lhs_ref[rows, pl.ds(depth + at, ROWS)] = low
            for c in range(pairs):
                total = jac(coef_ref, 2, v, 2 * c) * flux_ref[3]
                if 2 * c + 1 < nv:
                    total = total + jac(coef_ref, 2, v, 2 * c + 1) * flux_ref[4]
                if v // 2 == c:
                    total = total + damp(coef_ref, 2) * damp_ref[3 + v % 2]
                high, low = halves(total)
                at = nv * ROWS + c * 2 * ENDS
                lhs_ref[rows, pl.ds(at, 2 * ENDS)] = high
                lhs_ref[rows, pl.ds(depth + at, 2 * ENDS)] = low
        cols = lax.dot_general(
            inlet_table_ref[...],
            inlet_ref[...],
            (((1,), (1,)), ((), ())),
            precision=lax.Precision.HIGHEST,
            preferred_element_type=F32,
        )
        blend = jnp.zeros((ROWS, ROWS), F32)
        for v in range(nv):
            for w in range(nv):
                value = jac(coef_ref, 2, v, w)
                if v == w:
                    value = value + damp(coef_ref, 2)
                blend = jnp.where(mix_ref[...] == v * nv + w, -5.0 * value, blend)
        cols = jnp.dot(cols, blend, precision=lax.Precision.HIGHEST, preferred_element_type=F32)
        col_ref[...] = metric[:, 0:1] * cols
        for n in range(inst):
            natural = jnp.concatenate([padded_ref[n, v] for v in range(nv)], axis=1)
            moved = reorder(order_ref[...], natural, 3)
            for v in range(nv):
                part = moved[:, v * lanes : (v + 1) * lanes]
                x_ref[n, v] = part
                lo_ref[n, v] = part[0:FACE]
                hi_ref[n, v] = part[HIGH:ROWS]
                low_table_ref[n * nv + v] = part[0:FACE]
                high_table_ref[n * nv + v] = part[HIGH:ROWS]

    x0, lo0, hi0, metric, metric_face, lhs, inlet_cols, face_coef, face_update, low_table, high_table = call(
        prep_kernel,
        [
            shape(inst, nv, ROWS, lanes),
            shape(inst, nv, FACE, lanes),
            shape(inst, nv, FACE, lanes),
            shape(ROWS, lanes),
            shape(2, FACE, lanes),
            shape(nv * ROWS, 2 * depth, dtype=BF16),
            shape(ROWS, ROWS),
            shape(2, nv, nv, lanes),
            shape(2, inst, nv, nv, lanes),
            shape(scale_at + 1, FACE, lanes),
            shape(scale_at + 1, FACE, lanes),
        ],
        [
            state_rows,
            metric_scale.reshape(nodes, 1, lanes),
            coef,
            order_b,
            flux_table,
            damp_table,
            inlet,
            inlet_table,
            mix_index,
            precond,
        ],
        "hhsvvvvvvv",
        scratch=[
            pltpu.VMEM((inst, nv, ROWS, lanes), F32),
            pltpu.VMEM((ROWS, lanes), F32),
            pltpu.SemaphoreType.DMA((1 + inst * nv,)),
        ],
        name="prep",
    )

    def bulk(xs, lhs_ref):
        cols = []
        lane = lax.broadcasted_iota(jnp.int32, (ENDS // 2, lanes), 1)
        for x in xs:
            ends = []
            for part in x:
                first = jnp.concatenate([part[a:b] for a, b in FIRST], axis=0)
                last = jnp.concatenate([part[a:b] for a, b in LAST], axis=0)
                ends.append(jnp.where(lane == lanes - 1, last, pltpu.roll(first, lanes - 1, 1)))
                ends.append(jnp.where(lane == 0, 0.0, pltpu.roll(last, 1, 1)))
            if nv % 2:
                ends.append(jnp.zeros((ENDS, lanes), F32))
            cols.append(jnp.concatenate(list(x) + ends, axis=0))
        high, low = halves(jnp.concatenate(cols, axis=1) if len(cols) > 1 else cols[0])
        both = dot32(lhs_ref[...], jnp.concatenate([high, high], axis=0))
        return both + dot32(lhs_ref[:, 0:depth], low)

    def block_of(result, n, v):
        return result[v * ROWS : (v + 1) * ROWS, n * lanes : (n + 1) * lanes]

    def whole(lo_ref, z_ref, hi_ref, n, at, v):
        return jnp.concatenate([lo_ref[n, v], z_ref[at, v, FACE:HIGH, :], hi_ref[n, v]], axis=0)


    def advance(z, lo, hi, extra, first, size, flops=0):
        def kernel(*refs):
            z_ref, lo_ref, hi_ref, m_ref, p_ref, lhs_ref = refs[:6]
            out_ref = refs[-1]
            metric_value = m_ref[...]
            for at in range(0, size, 2):
                ids = list(range(at, min(at + 2, size)))
                xs = [[whole(lo_ref, z_ref, hi_ref, n, n, v) for v in range(nv)] for n in ids]
                result = bulk(xs, lhs_ref)
                for m, n in enumerate(ids):
                    res = [metric_value * block_of(result, m, v) for v in range(nv)]
                    if extra is not None:
                        res = [res[v] + refs[6][n, v] for v in range(nv)]
                    for v in range(nv):
                        weights = [p_ref[first + n, v, pl.ds(w, 1), :] for w in range(nv)]
                        out_ref[n, v] = xs[m][v] - mixed(weights, res)

        ins = [z, lo, hi, metric, precond, lhs]
        ins = ins + ([] if extra is None else [extra])
        return call(
            kernel,
            [shape(size, nv, ROWS, lanes)],
            ins,
            "vvvvvv" + ("" if extra is None else "v"),
            flops=flops,
            name="advance",
        )[0]

    def face_terms(n, lo_ref, hi_ref, below, above, table_of, mf_ref):
        position = lax.rem(lax.axis_index("elem") + PR // 2, PR)
        low_w, high_w = [], []
        for v in range(nv):
            sign = -1.0 if v == 2 else 1.0
            low_w.append(jnp.where(position == 0, sign * lo_ref[n, v], below[v]))
            high_w.append(jnp.where(position == PR - 1, sign * hi_ref[n, v], above[v]))
        lows, highs = [], []
        for v in range(nv):
            lows.append(mf_ref[0] * mixed([table_of(0, v, w) for w in range(nv)], low_w))
            highs.append(mf_ref[1] * mixed([table_of(1, v, w) for w in range(nv)], high_w))
        return lows, highs

    def swap_faces(lo, hi):
        return along_elem(hi, 1), along_elem(lo, -1)

    def close_faces(z, lo, hi, below, above, first, size):
        def kernel(z_ref, lo_ref, hi_ref, below_ref, above_ref, mf_ref, pc_ref, nlo_ref, nhi_ref):
            for n in range(size):

                def table_of(side, v, w, n=n):
                    return pc_ref[side, first + n, v, pl.ds(w, 1), :]

                flat = len(below_ref.shape) == 3
                below = [below_ref[n * nv + v] if flat else below_ref[n, v] for v in range(nv)]
                above = [above_ref[n * nv + v] if flat else above_ref[n, v] for v in range(nv)]
                lows, highs = face_terms(n, lo_ref, hi_ref, below, above, table_of, mf_ref)
                for v in range(nv):
                    nlo_ref[n, v] = z_ref[n, v, 0:FACE, :] - lows[v]
                    nhi_ref[n, v] = z_ref[n, v, HIGH:ROWS, :] - highs[v]

        return call(
            kernel,
            [shape(size, nv, FACE, lanes)] * 2,
            [z, lo, hi, below, above, metric_face, face_update],
            "v" * 7,
            name="faces",
        )

    def paired_first(z, lo, hi, spec, first):
        def kernel(z_ref, lo_ref, hi_ref, m_ref, p_ref, lhs_ref, spec_ref, out_ref, down_ref, up_ref):
            metric_value = m_ref[...]
            for at in range(0, per, 2):
                ids = list(range(at, min(at + 2, per)))
                xs = [[whole(lo_ref, z_ref, hi_ref, n, n, v) for v in range(nv)] for n in ids]
                result = bulk(xs, lhs_ref)
                for m, n in enumerate(ids):
                    res = [metric_value * block_of(result, m, v) + spec_ref[n, v] for v in range(nv)]
                    for v in range(nv):
                        weights = [p_ref[first + n, v, pl.ds(w, 1), :] for w in range(nv)]
                        value = xs[m][v] - mixed(weights, res)
                        out_ref[n, v] = value
                        down_ref[0, n, v], up_ref[0, n, v] = lo_ref[n, v], hi_ref[n, v]
                        down_ref[1, n, v], up_ref[1, n, v] = value[0:FACE], value[HIGH:ROWS]

        return call(
            kernel,
            [shape(per, nv, ROWS, lanes)] + [shape(2, per, nv, FACE, lanes)] * 2,
            [z, lo, hi, metric, precond, lhs, spec],
            "v" * 7,
            name="paired_first",
        )

    def paired_second(z, down, up, below, above, below_table, above_table, spec, first):
        def kernel(*refs):
            z_ref, down_ref, up_ref, below_ref, above_ref = refs[:5]
            low_ref, high_ref, below_table_ref, above_table_ref = refs[5:9]
            m_ref, p_ref, lhs_ref, spec_ref, out_ref, out_lo_ref, out_hi_ref = refs[9:]
            metric_value = m_ref[...]
            position = lax.rem(lax.axis_index("elem") + PR // 2, PR)

            def update(table_ref, n, values):
                result = []
                for v in range(nv):
                    at, row = table_place((first + n) * nv + v)
                    weights = [table_ref[at, pl.ds(row + w, 1), :] for w in range(nv)]
                    result.append(table_ref[scale_at] * mixed(weights, values))
                return result

            def across(at, own, other):
                return [
                    jnp.where(position == at, -own[v] if v == 2 else own[v], other[v]) for v in range(nv)
                ]

            def minus(a, b):
                return [p - q for p, q in zip(a, b)]

            for at in range(0, per, 2):
                ids = list(range(at, min(at + 2, per)))
                xs, beyond = [], []
                for n in ids:
                    lo, zlo = ([down_ref[k, n, v] for v in range(nv)] for k in range(2))
                    hi, zhi = ([up_ref[k, n, v] for v in range(nv)] for k in range(2))
                    low_w, low_z = ([below_ref[k, n, v] for v in range(nv)] for k in range(2))
                    high_w, high_z = ([above_ref[k, n, v] for v in range(nv)] for k in range(2))
                    new_lo = minus(zlo, update(low_ref, n, across(0, lo, low_w)))
                    new_hi = minus(zhi, update(high_ref, n, across(PR - 1, hi, high_w)))
                    next_low = across(0, new_lo, minus(low_z, update(below_table_ref, n, lo)))
                    next_high = across(PR - 1, new_hi, minus(high_z, update(above_table_ref, n, hi)))
                    xs.append(
                        [
                            jnp.concatenate([new_lo[v], z_ref[n, v, FACE:HIGH, :], new_hi[v]], axis=0)
                            for v in range(nv)
                        ]
                    )
                    beyond.append((update(low_ref, n, next_low), update(high_ref, n, next_high)))
                result = bulk(xs, lhs_ref)
                for m, n in enumerate(ids):
                    res = [metric_value * block_of(result, m, v) + spec_ref[n, v] for v in range(nv)]
                    for v in range(nv):
                        weights = [p_ref[first + n, v, pl.ds(w, 1), :] for w in range(nv)]
                        value = xs[m][v] - mixed(weights, res)
                        lo, hi = value[0:FACE] - beyond[m][0][v], value[HIGH:ROWS] - beyond[m][1][v]
                        out_ref[n, v] = value
                        out_lo_ref[n, v] = lo
                        out_hi_ref[n, v] = hi

        return call(
            kernel,
            [shape(per, nv, ROWS, lanes)] + [shape(per, nv, FACE, lanes)] * 2,
            [z, down, up, below, above, low_table, high_table, below_table, above_table]
            + [metric, precond, lhs, spec],
            "v" * 13,
            name="paired_second",
        )

    def circ_extra(z, lo, hi):
        x = jnp.concatenate([lo, z[:, :, FACE:HIGH], hi], axis=2)
        picks = np.zeros((2, 25, ROWS), dtype=np.float32)
        picks[0, np.arange(25), node_row[0:25]] = 1.0
        picks[1, np.arange(25), node_row[100:125]] = 1.0
        exact = lax.Precision.HIGHEST

        def picked(which):
            return jnp.einsum("pq,nvqa->nvpa", picks[which], x, precision=exact)

        def mix(values):
            return jnp.einsum("vw,nwqa->nvqa", flux_jacobians[0], values, precision=exact)

        def placed(which, values):
            return jnp.einsum("pq,nvpa->nvqa", picks[which], values, precision=exact)

        above, below = along_elem(picked(0), -PR), along_elem(picked(1), PR)
        high_term = 5.0 * (mix(above) - damping[0] * above)
        low_term = -5.0 * (mix(below) + damping[0] * below)
        return metric * (placed(1, high_term) + placed(0, low_term))

    below0, above0 = swap_faces(low_table, high_table)
    t0 = advance(x0, lo0, hi0, None if own_circ else circ_extra(x0, lo0, hi0), 0, inst)
    tlo, thi = close_faces(t0, lo0, hi0, below0, above0, 0, inst)

    half_pair = n_tm % 2 == 0

    def weight(offset, sign):
        return 0.5 * (coupling_value(offset, count) + sign * coupling_value(offset + count // 2, count))

    def weighted(terms):
        terms = [(c, x) for c, x in terms if abs(c) > 1e-12]
        return mixed([c for c, _ in terms], [x for _, x in terms])

    def coupling_kernel(*refs):
        x_refs, outs = refs[:n_tm], refs[n_tm:]

        def body(step, carry):
            v, rows = step // (block // 8), pl.ds(pl.multiple_of((step % (block // 8)) * 8, 8), 8)
            x = [[x_refs[d][i, v, rows, :] for i in range(inst)] for d in range(n_tm)]
            if half_pair:
                half = n_tm // 2
                sources = [(d, i) for d in range(half) for i in range(inst)]
                sums = [x[d][i] + x[d + half][i] for d, i in sources]
                diffs = [x[d][i] - x[d + half][i] for d, i in sources]
                for e in range(half):
                    for j in range(inst):
                        offsets = [inst * (e + d) + j - i for d, i in sources]
                        even = weighted([(weight(o, 1), s) for o, s in zip(offsets, sums)])
                        odd = weighted([(weight(o, -1), s) for o, s in zip(offsets, diffs)])
                        outs[e * groups + j // per][j % per, v, rows, :] = even + odd
                        outs[(e + half) * groups + j // per][j % per, v, rows, :] = even - odd
            else:
                sources = [(d, i) for d in range(n_tm) for i in range(inst)]
                for e in range(n_tm):
                    for j in range(inst):
                        offsets = [inst * (e + d) + j - i for d, i in sources]
                        outs[e * groups + j // per][j % per, v, rows, :] = weighted(
                            [(coupling_value(o, count), x[d][i]) for o, (d, i) in zip(offsets, sources)]
                        )
            return carry

        lax.fori_loop(0, nv * (block // 8), body, 0)

    coupled = call(
        coupling_kernel,
        [shape(per, nv, block, lanes)] * (n_tm * groups),
        arrived,
        "v" * n_tm,
        name="coupling",
    )
    spectral = [[coupled[g]] + [None] * (n_tm - 1) for g in range(groups)]
    for g in range(groups):
        for e in sorted(range(1, n_tm), key=lambda e: abs(2 * e - n_tm)):
            spectral[g][e] = along_tm(coupled[e * groups + g], e)

    def first_pass(parts, first, flops=0):
        distances = list(range(n_tm))
        if first > 0:
            distances.sort(key=lambda d: min(d, n_tm - d))

        def kernel(*refs):
            part_refs = [refs[distances.index(d)] for d in range(n_tm)]
            t_ref, tlo_ref, thi_ref, p_ref, col_ref, order_ref = refs[n_tm : n_tm + 6]
            x_ref, lo_ref, hi_ref, s_ref, buf = refs[n_tm + 6 :]
            me = lax.axis_index("tm")
            for d in range(n_tm):
                start = pl.multiple_of(lax.rem(me - d + n_tm, n_tm) * block, block)
                for n in range(per):
                    for v in range(nv):
                        buf[n, v, pl.ds(start, block), :] = part_refs[d][n, v]
            lane = lax.broadcasted_iota(jnp.int32, (ROWS, lanes), 1)
            for n in range(per):
                natural = jnp.concatenate([buf[n, v] for v in range(nv)], axis=1)
                moved = reorder(order_ref[...], natural, 2)
                terms = []
                for v in range(nv):
                    c = (first + n) * nv + v
                    column = jnp.broadcast_to(col_ref[:, c : c + 1], (ROWS, lanes))
                    term = moved[:, v * lanes : (v + 1) * lanes] + jnp.where(lane == 0, column, 0.0)
                    s_ref[n, v] = term
                    terms.append(term)
                for v in range(nv):
                    weights = [p_ref[first + n, v, pl.ds(w, 1), :] for w in range(nv)]
                    x = whole(tlo_ref, t_ref, thi_ref, first + n, first + n, v) - mixed(weights, terms)
                    x_ref[n, v] = x
                    lo_ref[n, v] = x[0:FACE]
                    hi_ref[n, v] = x[HIGH:ROWS]

        return call(
            kernel,
            [
                shape(per, nv, ROWS, lanes),
                shape(per, nv, FACE, lanes),
                shape(per, nv, FACE, lanes),
                shape(per, nv, ROWS, lanes),
            ],
            [parts[d] for d in distances] + [t0, tlo, thi, precond, inlet_cols, spectral_order.astype(ml_dtypes.bfloat16)],
            "v" * (n_tm + 6),
            scratch=[pltpu.VMEM((per, nv, ROWS, lanes), F32)],
            flops=flops,
            name="first_pass",
        )

    def write_out(moved_ref, out_ref, sem, first, work, meanwhile=None):
        copies = []
        for n in range(per):
            work(n)
            for v in range(nv):
                copy = pltpu.make_async_copy(
                    moved_ref.at[n, v, pl.ds(0, nodes), :], out_ref.at[first + n, v, :, 0, :], sem.at[n, v]
                )
                copy.start()
                copies.append(copy)
        if meanwhile is not None:
            meanwhile()
        for copy in copies:
            copy.wait()

    def last_bulk(z, lo, hi, extra, first, out):
        def kernel(*refs):
            z_ref, lo_ref, hi_ref, m_ref, lhs_ref, extra_ref, back_ref = refs[:7]
            r_ref, out_ref, buf, sem = refs[-4:]
            metric_value = m_ref[...]

            def work(n):
                x = [whole(lo_ref, z_ref, hi_ref, n, n, v) for v in range(nv)]
                moved = reorder(back_ref[...], jnp.concatenate(x, axis=1), 3)
                for v in range(nv):
                    buf[n, v] = moved[:, v * lanes : (v + 1) * lanes]

            def residual():
                for at in range(0, per, 2):
                    ids = list(range(at, min(at + 2, per)))
                    xs = [[whole(lo_ref, z_ref, hi_ref, n, n, v) for v in range(nv)] for n in ids]
                    result = bulk(xs, lhs_ref)
                    for m, n in enumerate(ids):
                        for v in range(nv):
                            r_ref[n, v] = metric_value * block_of(result, m, v) + extra_ref[n, v]

            write_out(buf, out_ref, sem, first, work, residual)

        ins = [z, lo, hi, metric, lhs, extra, back_b] + ([] if out is None else [out])
        return call(
            kernel,
            [shape(per, nv, ROWS, lanes), shape(inst, nv, nodes, 1, lanes)],
            ins,
            "vvvvvvv" + ("" if out is None else "a"),
            out_spaces="va",
            scratch=[pltpu.VMEM((per, nv, ROWS, lanes), F32), pltpu.SemaphoreType.DMA((per, nv))],
            alias=None if out is None else {7: 1},
            name="last_bulk",
        )

    def last_faces(r, lo, hi, below, above, first, out):
        def kernel(*refs):
            r_ref, lo_ref, hi_ref, below_ref, above_ref, mf_ref, fc_ref, back_ref = refs[:8]
            out_ref, buf, sem = refs[-3:]

            def table_of(side, v, w):
                return fc_ref[side, v, pl.ds(w, 1), :]

            def work(n):
                below = [below_ref[n, v] for v in range(nv)]
                above = [above_ref[n, v] for v in range(nv)]
                lows, highs = face_terms(n, lo_ref, hi_ref, below, above, table_of, mf_ref)
                full = [
                    jnp.concatenate(
                        [
                            r_ref[n, v, 0:FACE, :] + lows[v],
                            r_ref[n, v, FACE:HIGH, :],
                            r_ref[n, v, HIGH:ROWS, :] + highs[v],
                        ],
                        axis=0,
                    )
                    for v in range(nv)
                ]
                moved = reorder(back_ref[...], jnp.concatenate(full, axis=1), 2)
                for v in range(nv):
                    buf[n, v] = moved[:, v * lanes : (v + 1) * lanes]

            write_out(buf, out_ref, sem, first, work)

        ins = [r, lo, hi, below, above, metric_face, face_coef, back_b] + ([] if out is None else [out])
        return call(
            kernel,
            [shape(inst, nv, nodes, 1, lanes)],
            ins,
            "vvvvvvvv" + ("" if out is None else "a"),
            out_spaces="a",
            scratch=[pltpu.VMEM((per, nv, ROWS, lanes), F32), pltpu.SemaphoreType.DMA((per, nv))],
            alias=None if out is None else {8: 0},
            name="last_faces",
        )[0]

    new_state, final_residual = None, None
    chains, last = [None] * groups, None

    def begin(g, swap):
        parts = spectral[g] if last is None else [after(spectral[g][0], last)] + spectral[g][1:]
        z, lo, hi, spec = first_pass(parts, g * per, LONG if g == groups - 1 else 0)
        chains[g] = (z, lo, hi, swap_faces(lo, hi) if swap else None, spec)
        return lo

    def local_part(g, count_done):
        nonlocal new_state
        z, lo, hi, swapped, spec = chains[g]
        extra = spec if own_circ else spec + circ_extra(z, lo, hi)
        extra = extra if last is None else after(extra, last)
        if count_done < PASSES - 1:
            z = advance(z, lo, hi, extra, g * per, per, LONG)
        else:
            z, new_state = last_bulk(z, lo, hi, extra, g * per, new_state)
        chains[g] = (z, lo, hi, swapped, spec)
        return z

    def face_part(g, count_done):
        nonlocal final_residual
        z, lo, hi, (below, above), spec = chains[g]
        z = after(z, last)
        if count_done < PASSES - 1:
            lo, hi = close_faces(z, lo, hi, below, above, g * per, per)
            chains[g] = (z, lo, hi, swap_faces(lo, hi), spec)
            return lo
        final_residual = last_faces(z, lo, hi, below, above, g * per, final_residual)
        return final_residual

    def pair_begin(g):
        z, lo, hi, _, spec = chains[g]
        z, down, up = paired_first(z, lo, hi, after(spec, last), g * per)
        chains[g] = (z, down, up, (along_elem(up, 1), along_elem(down, -1)), spec)
        return z

    def pair_end(g, *before):
        z, down, up, (below, above), spec = chains[g]
        z, lo, hi = paired_second(
            z, down, up, below, above, below0, above0, after(spec, last), g * per
        )
        chains[g] = (z, lo, hi, None, spec)
        return z

    def pair_swap(g):
        z, lo, hi, _, spec = chains[g]
        lo, hi = lax.optimization_barrier((lo, hi, last))[:2]
        chains[g] = (z, lo, hi, swap_faces(lo, hi), spec)

    end = groups - 1
    if own_circ and PASSES == 3:
        for g in range(end):
            last = begin(g, False)
            last = pair_begin(g)
        last = begin(end, True)
        last = local_part(end, 0)
        for g in range(end):
            last = pair_end(g)
        last = face_part(end, 0)
        for g in range(end):
            pair_swap(g)
        last = local_part(end, 1)
        for g in range(end):
            last = local_part(g, 2)
        last = face_part(end, 1)
        for g in range(end):
            last = face_part(g, 2)
        last = local_part(end, 2)
        last = face_part(end, 2)
    else:
        for g in range(groups):
            last = begin(g, True)
            for count_done in range(PASSES):
                last = local_part(g, count_done)
                last = face_part(g, count_done)
    return (new_state.reshape(state.shape), final_residual.reshape(state.shape))


def solution(mesh):
    in_specs = (
        P("tm", None, "elem", None, None),
        P("elem", None, None),
        P(),
        P("tm", None, None, "elem", None),
        P("tm", None, "elem", None),
    )
    out_specs = (P("tm", None, "elem", None, None), P("tm", None, "elem", None, None))
    return jax.shard_map(
        per_device, mesh=mesh, in_specs=in_specs, out_specs=out_specs, check_vma=False
    )
```

```python
import math

import jax
import jax.numpy as jnp
import ml_dtypes
import numpy as np
from jax import lax
from jax.experimental import pallas as pl
from jax.experimental.pallas import tpu as pltpu
from jax.sharding import PartitionSpec as P

PR = 8
PASSES = 3
GROUPS = 2
ROWS = 128
FACE = 32
HIGH = 96

F32 = jnp.float32
BF16 = jnp.bfloat16


def gll_derivative():
    points = np.array([-1.0, -math.sqrt(3.0 / 7.0), 0.0, math.sqrt(3.0 / 7.0), 1.0])
    legendre = (35.0 * points**4 - 30.0 * points**2 + 3.0) / 8.0
    identity = np.eye(5, dtype=bool)
    spacing = np.where(identity, 1.0, points[:, None] - points[None, :])
    matrix = legendre[:, None] / legendre[None, :] / spacing
    corner = np.array([-5.0, 0.0, 0.0, 0.0, 5.0])[None, :]
    return np.where(identity, corner, matrix)


def coupling_value(offset, count):
    offset = offset % count
    if offset == 0:
        return 0.0
    angle = math.pi * offset / count
    return 0.5 * (-1.0) ** offset * math.cos(angle) / math.sin(angle)


FIRST = ((8, 16), (24, 40), (104, 112))
LAST = ((16, 24), (40, 56), (112, 120))
ENDS = 64


def node_rows():
    rows = np.zeros((5, 5, 5), dtype=np.int64)
    face_rest = list(range(0, 11)) + [16, 17, 18, 24]
    rest = [40] + list(range(56, HIGH)) + list(range(HIGH + 25, ROWS))
    face_used, used = 0, 0
    for i in range(5):
        for k in range(5):
            if k in (0, 4):
                local = (11 if k == 0 else 19) + i
            else:
                local = face_rest[face_used]
                face_used += 1
            rows[i, 0, k], rows[i, 4, k] = local, HIGH + local
            for j in range(1, 4):
                if k in (0, 4):
                    rows[i, j, k] = (25 if k == 0 else 41) + 3 * i + j - 1
                else:
                    rows[i, j, k] = rest[used]
                    used += 1
    return rows.reshape(125)


def end_rows():
    return [r for part in (FIRST, LAST) for a, b in part for r in range(a, b)]


def tables(own_circ):
    table = gll_derivative()
    eye = np.eye(5)
    first, last = np.diag([1.0, 0, 0, 0, 0]), np.diag([0, 0, 0, 0, 1.0])
    to_first, to_last = np.zeros((5, 5)), np.zeros((5, 5))
    to_first[0, 4] = 1.0
    to_last[4, 0] = 1.0

    def along(matrix, direction):
        parts = [eye, eye, eye]
        parts[direction] = matrix
        return np.kron(np.kron(parts[0], parts[1]), parts[2])

    rows = node_rows()
    order = np.zeros((ROWS, ROWS))
    order[rows, np.arange(125)] = 1.0

    def placed(matrix):
        return order[:, :125] @ matrix @ order[:, :125].T

    mix, damp = [], []
    for d in range(3):
        mix.append(placed(along(table - 5.0 * last + 5.0 * first, d)))
        damp.append(placed(along(5.0 * last + 5.0 * first, d)))
    if own_circ:
        mix[0] = mix[0] + placed(along(5.0 * to_last - 5.0 * to_first, 0))
        damp[0] = damp[0] + placed(along(-5.0 * to_last - 5.0 * to_first, 0))
    ends = end_rows()
    axial_mix = placed(along(5.0 * to_last - 5.0 * to_first, 2))[:, ends]
    axial_damp = placed(along(-5.0 * to_last - 5.0 * to_first, 2))[:, ends]
    none = np.zeros((ROWS, ENDS))

    def pair(matrix):
        return [np.concatenate([matrix, none], 1), np.concatenate([none, matrix], 1)]

    fluxes = np.stack(mix + pair(axial_mix)).astype(np.float32)
    dampers = np.stack(damp + pair(axial_damp)).astype(np.float32)
    return order, fluxes, dampers


def halves(values):
    high = values.astype(BF16)
    low = (values - high.astype(F32)).astype(BF16)
    return high, low


def dot32(a, b):
    return jnp.dot(a, b, preferred_element_type=F32)


def reorder(matrix, values, terms):
    total = None
    for _ in range(terms):
        part = values.astype(BF16)
        moved = dot32(matrix, part)
        total = moved if total is None else total + moved
        values = values - part.astype(F32)
    return total


SIDE = 25


def put_rows(ref, at, v, value):
    ref[(*at, pl.ds(SIDE * v, SIDE), slice(None))] = value[0:SIDE]


def get_rows(ref, at, v):
    rows = ref[(*at, pl.ds(SIDE * v, SIDE), slice(None))]
    return jnp.concatenate([rows, jnp.zeros((FACE - SIDE, rows.shape[1]), F32)], axis=0)


def mixed(weights, parts):
    total = weights[0] * parts[0]
    for weight, part in zip(weights[1:], parts[1:]):
        total = total + weight * part
    return total


VMEM_LIMIT = 20 * 2**20
LONG = 2 * 10**9


def call(kernel, outs, ins, in_spaces, out_spaces=None, scratch=(), flops=0, alias=None, name=None):
    out_spaces = out_spaces or ["v"] * len(outs)
    space = {"v": pltpu.VMEM, "s": pltpu.SMEM, "a": pl.ANY, "h": pltpu.HBM}
    return pl.pallas_call(
        kernel,
        out_shape=outs,
        in_specs=[pl.BlockSpec(memory_space=space[s]) for s in in_spaces],
        out_specs=[pl.BlockSpec(memory_space=space[s]) for s in out_spaces],
        scratch_shapes=list(scratch),
        input_output_aliases=alias or {},
        compiler_params=pltpu.CompilerParams(vmem_limit_bytes=VMEM_LIMIT),
        cost_estimate=pl.CostEstimate(flops=max(flops, 1), bytes_accessed=1, transcendentals=0),
        name=name,
    )(*ins)


def shape(*dims, dtype=F32):
    return jax.ShapeDtypeStruct(dims, dtype)


def per_device(state, metric_scale, flux_jacobians, preconditioner, inflow):
    inst, nv, _, nodes, lanes = state.shape
    n_tm = lax.axis_size("tm")
    n_elem = lax.axis_size("elem")
    count = inst * n_tm
    own_circ = n_elem == PR
    block = ROWS // n_tm
    groups = GROUPS if inst % GROUPS == 0 else 1
    per = inst // groups
    order, flux_table, damp_table = tables(own_circ)
    order_b = order.astype(ml_dtypes.bfloat16)
    back_b = np.ascontiguousarray(order.T).astype(ml_dtypes.bfloat16)
    pairs = (nv + 1) // 2
    depth = nv * ROWS + pairs * 2 * ENDS
    node_row = node_rows()
    inlet_table = np.zeros((ROWS, ROWS), dtype=np.float32)
    inlet_table[node_row[0::5], np.arange(25)] = 1.0

    damping = jnp.max(jnp.sum(jnp.abs(flux_jacobians), axis=2), axis=1)
    coef = jnp.concatenate([flux_jacobians.reshape(-1), damping])
    precond = preconditioner.reshape(inst, nv, nv, lanes)
    inlet = jnp.pad(inflow.reshape(inst * nv, 25), ((0, ROWS - inst * nv), (0, ROWS - 25)))
    mix_index = np.full((ROWS, ROWS), -1, dtype=np.int32)
    for n in range(inst):
        for v in range(nv):
            for w in range(nv):
                mix_index[n * nv + w, n * nv + v] = v * nv + w

    def jac(ref, d, v, w):
        return ref[(d * nv + v) * nv + w]

    def damp(ref, d):
        return ref[3 * nv * nv + d]

    state_rows = state.reshape(inst, nv, nodes, 1, lanes)
    starts = [min(q * block, nodes - block) for q in range(n_tm)]
    spectral_order = np.zeros((ROWS, ROWS))
    for q in range(n_tm):
        for r in range(block):
            if starts[q] + r >= q * block:
                spectral_order[:, q * block + r] = order[:, starts[q] + r]

    def pack_kernel(state_ref, *refs):
        outs, sem = refs[:n_tm], refs[n_tm]
        me = lax.axis_index("tm")
        copies = []
        for d in range(n_tm):
            start = jnp.minimum(lax.rem(me + d, n_tm) * block, nodes - block)
            copies.append(
                pltpu.make_async_copy(state_ref.at[:, :, pl.ds(start, block), 0, :], outs[d], sem.at[d])
            )
        for copy in copies:
            copy.start()
        for copy in copies:
            copy.wait()

    piece = shape(inst, nv, block, lanes)
    pieces = call(
        pack_kernel,
        [piece] * n_tm,
        [state_rows],
        "h",
        scratch=[pltpu.SemaphoreType.DMA((n_tm,))],
        name="pack",
    )

    def after(x, *before):
        return lax.optimization_barrier((x, *before))[0]

    def along_tm(x, d):
        return lax.ppermute(x, "tm", [(i, (i + d) % n_tm) for i in range(n_tm)])

    def along_elem(x, d):
        return lax.ppermute(x, "elem", [(i, (i + d) % n_elem) for i in range(n_elem)])

    arrived = [pieces[0]] + [None] * (n_tm - 1)
    for d in sorted(range(1, n_tm), key=lambda d: abs(2 * d - n_tm)):
        arrived[d] = along_tm(pieces[d], d)

    scale_at = inst * nv + -(-inst * nv // (FACE // 8))

    def table_place(index):
        return inst * nv + index // (FACE // 8), 8 * (index % (FACE // 8))

    def prep_kernel(
        state_ref, metric_ref, coef_ref, order_ref, flux_ref, damp_ref, inlet_ref, inlet_table_ref, mix_ref, p_ref,
        x_ref, lo_ref, hi_ref, m_ref, mf_ref, lhs_ref, col_ref, fc_ref, pc_ref, low_table_ref, high_table_ref, padded_ref, buf, sem,
    ):
        buf[pl.ds(ROWS - 8, 8), :] = jnp.zeros((8, lanes), F32)
        padded_ref[:, :, pl.ds(ROWS - 8, 8), :] = jnp.zeros((inst, nv, 8, lanes), F32)
        copies = [
            pltpu.make_async_copy(metric_ref.at[:, 0, :], buf.at[pl.ds(0, nodes), :], sem.at[0]),
        ]
        for n in range(inst):
            for v in range(nv):
                copies.append(
                    pltpu.make_async_copy(
                        state_ref.at[n, v, :, 0, :],
                        padded_ref.at[n, v, pl.ds(0, nodes), :],
                        sem.at[1 + n * nv + v],
                    )
                )
        for copy in copies:
            copy.start()
        for copy in copies:
            copy.wait()
        metric = reorder(order_ref[...], buf[...], 3)
        m_ref[...] = metric
        row = lax.broadcasted_iota(jnp.int32, (FACE, lanes), 0)
        mf_ref[0] = jnp.where(row < 25, metric[0:FACE], 0.0)
        mf_ref[1] = jnp.where(row < 25, metric[HIGH:ROWS], 0.0)
        for v in range(nv):
            for w in range(nv):
                value, own = jac(coef_ref, 1, v, w), damp(coef_ref, 1) if v == w else 0.0
                fc_ref[0, v, pl.ds(w, 1), :] = jnp.full((1, lanes), -5.0 * (value + own), F32)
                fc_ref[1, v, pl.ds(w, 1), :] = jnp.full((1, lanes), 5.0 * (value - own), F32)
        for side in range(2):
            tables_of = [fc_ref[side, u] for u in range(nv)]
            for n in range(inst):
                for v in range(nv):
                    weights = [p_ref[n, v, pl.ds(u, 1), :] for u in range(nv)]
                    update = mixed(weights, tables_of)
                    pc_ref[side, n, v] = update
                    at, row = table_place(n * nv + v)
                    table_ref = (low_table_ref, high_table_ref)[side]
                    table_ref[at, pl.ds(row, 8), :] = jnp.concatenate(
                        [update, jnp.zeros((8 - nv, lanes), F32)], axis=0
                    )
            for spare in range(inst * nv, (scale_at - inst * nv) * (FACE // 8)):
                at, row = table_place(spare)
                table_ref[at, pl.ds(row, 8), :] = jnp.zeros((8, lanes), F32)
            table_ref[scale_at] = mf_ref[side]
        for v in range(nv):
            rows = pl.ds(v * ROWS, ROWS)
            for w in range(nv):
                total = mixed([jac(coef_ref, d, v, w) for d in range(3)], [flux_ref[d] for d in range(3)])
                if v == w:
                    for d in range(3):
                        total = total + damp(coef_ref, d) * damp_ref[d]
                high, low = halves(total)
                at = w * ROWS
                lhs_ref[rows, pl.ds(at, ROWS)] = high
                lhs_ref[rows, pl.ds(depth + at, ROWS)] = low
            for c in range(pairs):
                total = jac(coef_ref, 2, v, 2 * c) * flux_ref[3]
                if 2 * c + 1 < nv:
                    total = total + jac(coef_ref, 2, v, 2 * c + 1) * flux_ref[4]
                if v // 2 == c:
                    total = total + damp(coef_ref, 2) * damp_ref[3 + v % 2]
                high, low = halves(total)
                at = nv * ROWS + c * 2 * ENDS
                lhs_ref[rows, pl.ds(at, 2 * ENDS)] = high
                lhs_ref[rows, pl.ds(depth + at, 2 * ENDS)] = low
        cols = lax.dot_general(
            inlet_table_ref[...],
            inlet_ref[...],
            (((1,), (1,)), ((), ())),
            precision=lax.Precision.HIGHEST,
            preferred_element_type=F32,
        )
        blend = jnp.zeros((ROWS, ROWS), F32)
        for v in range(nv):
            for w in range(nv):
                value = jac(coef_ref, 2, v, w)
                if v == w:
                    value = value + damp(coef_ref, 2)
                blend = jnp.where(mix_ref[...] == v * nv + w, -5.0 * value, blend)
        cols = jnp.dot(cols, blend, precision=lax.Precision.HIGHEST, preferred_element_type=F32)
        col_ref[...] = metric[:, 0:1] * cols
        for n in range(inst):
            natural = jnp.concatenate([padded_ref[n, v] for v in range(nv)], axis=1)
            moved = reorder(order_ref[...], natural, 3)
            for v in range(nv):
                part = moved[:, v * lanes : (v + 1) * lanes]
                x_ref[n, v] = part
                lo_ref[n, v] = part[0:FACE]
                hi_ref[n, v] = part[HIGH:ROWS]
                low_table_ref[n * nv + v] = part[0:FACE]
                high_table_ref[n * nv + v] = part[HIGH:ROWS]

    x0, lo0, hi0, metric, metric_face, lhs, inlet_cols, face_coef, face_update, low_table, high_table = call(
        prep_kernel,
        [
            shape(inst, nv, ROWS, lanes),
            shape(inst, nv, FACE, lanes),
            shape(inst, nv, FACE, lanes),
            shape(ROWS, lanes),
            shape(2, FACE, lanes),
            shape(nv * ROWS, 2 * depth, dtype=BF16),
            shape(ROWS, ROWS),
            shape(2, nv, nv, lanes),
            shape(2, inst, nv, nv, lanes),
            shape(scale_at + 1, FACE, lanes),
            shape(scale_at + 1, FACE, lanes),
        ],
        [
            state_rows,
            metric_scale.reshape(nodes, 1, lanes),
            coef,
            order_b,
            flux_table,
            damp_table,
            inlet,
            inlet_table,
            mix_index,
            precond,
        ],
        "hhsvvvvvvv",
        scratch=[
            pltpu.VMEM((inst, nv, ROWS, lanes), F32),
            pltpu.VMEM((ROWS, lanes), F32),
            pltpu.SemaphoreType.DMA((1 + inst * nv,)),
        ],
        name="prep",
    )

    def bulk(xs, lhs_ref):
        cols = []
        lane = lax.broadcasted_iota(jnp.int32, (ENDS // 2, lanes), 1)
        for x in xs:
            ends = []
            for part in x:
                first = jnp.concatenate([part[a:b] for a, b in FIRST], axis=0)
                last = jnp.concatenate([part[a:b] for a, b in LAST], axis=0)
                ends.append(jnp.where(lane == lanes - 1, last, pltpu.roll(first, lanes - 1, 1)))
                ends.append(jnp.where(lane == 0, 0.0, pltpu.roll(last, 1, 1)))
            if nv % 2:
                ends.append(jnp.zeros((ENDS, lanes), F32))
            cols.append(jnp.concatenate(list(x) + ends, axis=0))
        high, low = halves(jnp.concatenate(cols, axis=1) if len(cols) > 1 else cols[0])
        both = dot32(lhs_ref[...], jnp.concatenate([high, high], axis=0))
        return both + dot32(lhs_ref[:, 0:depth], low)

    def block_of(result, n, v):
        return result[v * ROWS : (v + 1) * ROWS, n * lanes : (n + 1) * lanes]

    def whole(lo_ref, z_ref, hi_ref, n, at, v):
        return jnp.concatenate([lo_ref[n, v], z_ref[at, v, FACE:HIGH, :], hi_ref[n, v]], axis=0)


    def advance(z, lo, hi, extra, first, size, flops=0):
        def kernel(*refs):
            z_ref, lo_ref, hi_ref, m_ref, p_ref, lhs_ref = refs[:6]
            out_ref = refs[-1]
            metric_value = m_ref[...]
            for at in range(0, size, 2):
                ids = list(range(at, min(at + 2, size)))
                xs = [[whole(lo_ref, z_ref, hi_ref, n, n, v) for v in range(nv)] for n in ids]
                result = bulk(xs, lhs_ref)
                for m, n in enumerate(ids):
                    res = [metric_value * block_of(result, m, v) for v in range(nv)]
                    if extra is not None:
                        res = [res[v] + refs[6][n, v] for v in range(nv)]
                    for v in range(nv):
                        weights = [p_ref[first + n, v, pl.ds(w, 1), :] for w in range(nv)]
                        out_ref[n, v] = xs[m][v] - mixed(weights, res)

        ins = [z, lo, hi, metric, precond, lhs]
        ins = ins + ([] if extra is None else [extra])
        return call(
            kernel,
            [shape(size, nv, ROWS, lanes)],
            ins,
            "vvvvvv" + ("" if extra is None else "v"),
            flops=flops,
            name="advance",
        )[0]

    def face_terms(n, lo_ref, hi_ref, below, above, table_of, mf_ref):
        position = lax.rem(lax.axis_index("elem") + PR // 2, PR)
        low_w, high_w = [], []
        for v in range(nv):
            sign = -1.0 if v == 2 else 1.0
            low_w.append(jnp.where(position == 0, sign * lo_ref[n, v], below[v]))
            high_w.append(jnp.where(position == PR - 1, sign * hi_ref[n, v], above[v]))
        lows, highs = [], []
        for v in range(nv):
            lows.append(mf_ref[0] * mixed([table_of(0, v, w) for w in range(nv)], low_w))
            highs.append(mf_ref[1] * mixed([table_of(1, v, w) for w in range(nv)], high_w))
        return lows, highs

    def swap_faces(lo, hi):
        return along_elem(hi, 1), along_elem(lo, -1)

    def close_faces(z, lo, hi, below, above, first, size, send=True):
        def kernel(z_ref, lo_ref, hi_ref, below_ref, above_ref, mf_ref, pc_ref, nlo_ref, nhi_ref, *sends):
            for n in range(size):

                def table_of(side, v, w, n=n):
                    return pc_ref[side, first + n, v, pl.ds(w, 1), :]

                flat = not sends
                below = [below_ref[n * nv + v] if flat else get_rows(below_ref, (n,), v) for v in range(nv)]
                above = [above_ref[n * nv + v] if flat else get_rows(above_ref, (n,), v) for v in range(nv)]
                lows, highs = face_terms(n, lo_ref, hi_ref, below, above, table_of, mf_ref)
                for v in range(nv):
                    new_lo, new_hi = z_ref[n, v, 0:FACE, :] - lows[v], z_ref[n, v, HIGH:ROWS, :] - highs[v]
                    nlo_ref[n, v], nhi_ref[n, v] = new_lo, new_hi
                    if sends:
                        put_rows(sends[0], (n,), v, new_lo)
                        put_rows(sends[1], (n,), v, new_hi)

        return call(
            kernel,
            [shape(size, nv, FACE, lanes)] * 2 + ([shape(size, ROWS, lanes)] * 2 if send else []),
            [z, lo, hi, below, above, metric_face, face_update],
            "v" * 7,
            name="faces",
        )

    def paired_first(z, lo, hi, spec, first):
        def kernel(z_ref, lo_ref, hi_ref, m_ref, p_ref, lhs_ref, spec_ref, out_ref, down_ref, up_ref, send_down_ref, send_up_ref):
            metric_value = m_ref[...]
            for at in range(0, per, 2):
                ids = list(range(at, min(at + 2, per)))
                xs = [[whole(lo_ref, z_ref, hi_ref, n, n, v) for v in range(nv)] for n in ids]
                result = bulk(xs, lhs_ref)
                for m, n in enumerate(ids):
                    res = [metric_value * block_of(result, m, v) + spec_ref[n, v] for v in range(nv)]
                    for v in range(nv):
                        weights = [p_ref[first + n, v, pl.ds(w, 1), :] for w in range(nv)]
                        value = xs[m][v] - mixed(weights, res)
                        out_ref[n, v] = value
                        down_ref[0, n, v], up_ref[0, n, v] = lo_ref[n, v], hi_ref[n, v]
                        down_ref[1, n, v], up_ref[1, n, v] = value[0:FACE], value[HIGH:ROWS]
                        put_rows(send_down_ref, (0, n), v, lo_ref[n, v])
                        put_rows(send_up_ref, (0, n), v, hi_ref[n, v])
                        put_rows(send_down_ref, (1, n), v, value[0:FACE])
                        put_rows(send_up_ref, (1, n), v, value[HIGH:ROWS])

        return call(
            kernel,
            [shape(per, nv, ROWS, lanes)]
            + [shape(2, per, nv, FACE, lanes)] * 2
            + [shape(2, per, ROWS, lanes)] * 2,
            [z, lo, hi, metric, precond, lhs, spec],
            "v" * 7,
            name="paired_first",
        )

    def paired_second(z, down, up, below, above, below_table, above_table, spec, first):
        def kernel(*refs):
            z_ref, down_ref, up_ref, below_ref, above_ref = refs[:5]
            low_ref, high_ref, below_table_ref, above_table_ref = refs[5:9]
            m_ref, p_ref, lhs_ref, spec_ref, out_ref, out_lo_ref, out_hi_ref, send_lo_ref, send_hi_ref = refs[9:]
            metric_value = m_ref[...]
            position = lax.rem(lax.axis_index("elem") + PR // 2, PR)

            def update(table_ref, n, values):
                result = []
                for v in range(nv):
                    at, row = table_place((first + n) * nv + v)
                    weights = [table_ref[at, pl.ds(row + w, 1), :] for w in range(nv)]
                    result.append(table_ref[scale_at] * mixed(weights, values))
                return result

            def across(at, own, other):
                return [
                    jnp.where(position == at, -own[v] if v == 2 else own[v], other[v]) for v in range(nv)
                ]

            def minus(a, b):
                return [p - q for p, q in zip(a, b)]

            for at in range(0, per, 2):
                ids = list(range(at, min(at + 2, per)))
                xs, beyond = [], []
                for n in ids:
                    lo, zlo = ([down_ref[k, n, v] for v in range(nv)] for k in range(2))
                    hi, zhi = ([up_ref[k, n, v] for v in range(nv)] for k in range(2))
                    low_w, low_z = ([get_rows(below_ref, (k, n), v) for v in range(nv)] for k in range(2))
                    high_w, high_z = ([get_rows(above_ref, (k, n), v) for v in range(nv)] for k in range(2))
                    new_lo = minus(zlo, update(low_ref, n, across(0, lo, low_w)))
                    new_hi = minus(zhi, update(high_ref, n, across(PR - 1, hi, high_w)))
                    next_low = across(0, new_lo, minus(low_z, update(below_table_ref, n, lo)))
                    next_high = across(PR - 1, new_hi, minus(high_z, update(above_table_ref, n, hi)))
                    xs.append(
                        [
                            jnp.concatenate([new_lo[v], z_ref[n, v, FACE:HIGH, :], new_hi[v]], axis=0)
                            for v in range(nv)
                        ]
                    )
                    beyond.append((update(low_ref, n, next_low), update(high_ref, n, next_high)))
                result = bulk(xs, lhs_ref)
                for m, n in enumerate(ids):
                    res = [metric_value * block_of(result, m, v) + spec_ref[n, v] for v in range(nv)]
                    for v in range(nv):
                        weights = [p_ref[first + n, v, pl.ds(w, 1), :] for w in range(nv)]
                        value = xs[m][v] - mixed(weights, res)
                        lo, hi = value[0:FACE] - beyond[m][0][v], value[HIGH:ROWS] - beyond[m][1][v]
                        out_ref[n, v] = value
                        out_lo_ref[n, v] = lo
                        out_hi_ref[n, v] = hi
                        put_rows(send_lo_ref, (n,), v, lo)
                        put_rows(send_hi_ref, (n,), v, hi)

        return call(
            kernel,
            [shape(per, nv, ROWS, lanes)]
            + [shape(per, nv, FACE, lanes)] * 2
            + [shape(per, ROWS, lanes)] * 2,
            [z, down, up, below, above, low_table, high_table, below_table, above_table]
            + [metric, precond, lhs, spec],
            "v" * 13,
            name="paired_second",
        )

    def circ_extra(z, lo, hi):
        x = jnp.concatenate([lo, z[:, :, FACE:HIGH], hi], axis=2)
        picks = np.zeros((2, 25, ROWS), dtype=np.float32)
        picks[0, np.arange(25), node_row[0:25]] = 1.0
        picks[1, np.arange(25), node_row[100:125]] = 1.0
        exact = lax.Precision.HIGHEST

        def picked(which):
            return jnp.einsum("pq,nvqa->nvpa", picks[which], x, precision=exact)

        def mix(values):
            return jnp.einsum("vw,nwqa->nvqa", flux_jacobians[0], values, precision=exact)

        def placed(which, values):
            return jnp.einsum("pq,nvpa->nvqa", picks[which], values, precision=exact)

        above, below = along_elem(picked(0), -PR), along_elem(picked(1), PR)
        high_term = 5.0 * (mix(above) - damping[0] * above)
        low_term = -5.0 * (mix(below) + damping[0] * below)
        return metric * (placed(1, high_term) + placed(0, low_term))

    below0, above0 = swap_faces(low_table, high_table)
    t0 = advance(x0, lo0, hi0, None if own_circ else circ_extra(x0, lo0, hi0), 0, inst)
    tlo, thi = close_faces(t0, lo0, hi0, below0, above0, 0, inst, send=False)

    half_pair = n_tm % 2 == 0

    def weight(offset, sign):
        return 0.5 * (coupling_value(offset, count) + sign * coupling_value(offset + count // 2, count))

    def weighted(terms):
        terms = [(c, x) for c, x in terms if abs(c) > 1e-12]
        return mixed([c for c, _ in terms], [x for _, x in terms])

    def coupling_kernel(*refs):
        x_refs, outs = refs[:n_tm], refs[n_tm:]

        def body(step, carry):
            v, rows = step // (block // 8), pl.ds(pl.multiple_of((step % (block // 8)) * 8, 8), 8)
            x = [[x_refs[d][i, v, rows, :] for i in range(inst)] for d in range(n_tm)]
            if half_pair:
                half = n_tm // 2
                sources = [(d, i) for d in range(half) for i in range(inst)]
                sums = [x[d][i] + x[d + half][i] for d, i in sources]
                diffs = [x[d][i] - x[d + half][i] for d, i in sources]
                for e in range(half):
                    for j in range(inst):
                        offsets = [inst * (e + d) + j - i for d, i in sources]
                        even = weighted([(weight(o, 1), s) for o, s in zip(offsets, sums)])
                        odd = weighted([(weight(o, -1), s) for o, s in zip(offsets, diffs)])
                        outs[e * groups + j // per][j % per, v, rows, :] = even + odd
                        outs[(e + half) * groups + j // per][j % per, v, rows, :] = even - odd
            else:
                sources = [(d, i) for d in range(n_tm) for i in range(inst)]
                for e in range(n_tm):
                    for j in range(inst):
                        offsets = [inst * (e + d) + j - i for d, i in sources]
                        outs[e * groups + j // per][j % per, v, rows, :] = weighted(
                            [(coupling_value(o, count), x[d][i]) for o, (d, i) in zip(offsets, sources)]
                        )
            return carry

        lax.fori_loop(0, nv * (block // 8), body, 0)

    coupled = call(
        coupling_kernel,
        [shape(per, nv, block, lanes)] * (n_tm * groups),
        arrived,
        "v" * n_tm,
        name="coupling",
    )
    spectral = [[coupled[g]] + [None] * (n_tm - 1) for g in range(groups)]
    for g in range(groups):
        for e in sorted(range(1, n_tm), key=lambda e: abs(2 * e - n_tm)):
            spectral[g][e] = along_tm(coupled[e * groups + g], e)

    def first_pass(parts, first, flops=0):
        distances = list(range(n_tm))
        if first > 0:
            distances.sort(key=lambda d: min(d, n_tm - d))

        def kernel(*refs):
            part_refs = [refs[distances.index(d)] for d in range(n_tm)]
            t_ref, tlo_ref, thi_ref, p_ref, col_ref, order_ref = refs[n_tm : n_tm + 6]
            x_ref, lo_ref, hi_ref, s_ref, send_lo_ref, send_hi_ref, buf = refs[n_tm + 6 :]
            me = lax.axis_index("tm")
            for d in range(n_tm):
                start = pl.multiple_of(lax.rem(me - d + n_tm, n_tm) * block, block)
                for n in range(per):
                    for v in range(nv):
                        buf[n, v, pl.ds(start, block), :] = part_refs[d][n, v]
            lane = lax.broadcasted_iota(jnp.int32, (ROWS, lanes), 1)
            for n in range(per):
                natural = jnp.concatenate([buf[n, v] for v in range(nv)], axis=1)
                moved = reorder(order_ref[...], natural, 2)
                terms = []
                for v in range(nv):
                    c = (first + n) * nv + v
                    column = jnp.broadcast_to(col_ref[:, c : c + 1], (ROWS, lanes))
                    term = moved[:, v * lanes : (v + 1) * lanes] + jnp.where(lane == 0, column, 0.0)
                    s_ref[n, v] = term
                    terms.append(term)
                for v in range(nv):
                    weights = [p_ref[first + n, v, pl.ds(w, 1), :] for w in range(nv)]
                    x = whole(tlo_ref, t_ref, thi_ref, first + n, first + n, v) - mixed(weights, terms)
                    x_ref[n, v] = x
                    lo_ref[n, v] = x[0:FACE]
                    hi_ref[n, v] = x[HIGH:ROWS]
                    put_rows(send_lo_ref, (n,), v, x[0:FACE])
                    put_rows(send_hi_ref, (n,), v, x[HIGH:ROWS])

        return call(
            kernel,
            [
                shape(per, nv, ROWS, lanes),
                shape(per, nv, FACE, lanes),
                shape(per, nv, FACE, lanes),
                shape(per, nv, ROWS, lanes),
                shape(per, ROWS, lanes),
                shape(per, ROWS, lanes),
            ],
            [parts[d] for d in distances] + [t0, tlo, thi, precond, inlet_cols, spectral_order.astype(ml_dtypes.bfloat16)],
            "v" * (n_tm + 6),
            scratch=[pltpu.VMEM((per, nv, ROWS, lanes), F32)],
            flops=flops,
            name="first_pass",
        )

    def write_out(moved_ref, out_ref, sem, first, work, meanwhile=None):
        copies = []
        for n in range(per):
            work(n)
            for v in range(nv):
                copy = pltpu.make_async_copy(
                    moved_ref.at[n, v, pl.ds(0, nodes), :], out_ref.at[first + n, v, :, 0, :], sem.at[n, v]
                )
                copy.start()
                copies.append(copy)
        if meanwhile is not None:
            meanwhile()
        for copy in copies:
            copy.wait()

    def last_bulk(z, lo, hi, extra, first, out):
        def kernel(*refs):
            z_ref, lo_ref, hi_ref, m_ref, lhs_ref, extra_ref, back_ref = refs[:7]
            r_ref, out_ref, buf, sem = refs[-4:]
            metric_value = m_ref[...]

            def work(n):
                x = [whole(lo_ref, z_ref, hi_ref, n, n, v) for v in range(nv)]
                moved = reorder(back_ref[...], jnp.concatenate(x, axis=1), 3)
                for v in range(nv):
                    buf[n, v] = moved[:, v * lanes : (v + 1) * lanes]

            def residual():
                for at in range(0, per, 2):
                    ids = list(range(at, min(at + 2, per)))
                    xs = [[whole(lo_ref, z_ref, hi_ref, n, n, v) for v in range(nv)] for n in ids]
                    result = bulk(xs, lhs_ref)
                    for m, n in enumerate(ids):
                        for v in range(nv):
                            r_ref[n, v] = metric_value * block_of(result, m, v) + extra_ref[n, v]

            write_out(buf, out_ref, sem, first, work, residual)

        ins = [z, lo, hi, metric, lhs, extra, back_b] + ([] if out is None else [out])
        return call(
            kernel,
            [shape(per, nv, ROWS, lanes), shape(inst, nv, nodes, 1, lanes)],
            ins,
            "vvvvvvv" + ("" if out is None else "a"),
            out_spaces="va",
            scratch=[pltpu.VMEM((per, nv, ROWS, lanes), F32), pltpu.SemaphoreType.DMA((per, nv))],
            alias=None if out is None else {7: 1},
            name="last_bulk",
        )

    def last_faces(r, lo, hi, below, above, first, out):
        def kernel(*refs):
            r_ref, lo_ref, hi_ref, below_ref, above_ref, mf_ref, fc_ref, back_ref = refs[:8]
            out_ref, buf, sem = refs[-3:]

            def table_of(side, v, w):
                return fc_ref[side, v, pl.ds(w, 1), :]

            def work(n):
                below = [get_rows(below_ref, (n,), v) for v in range(nv)]
                above = [get_rows(above_ref, (n,), v) for v in range(nv)]
                lows, highs = face_terms(n, lo_ref, hi_ref, below, above, table_of, mf_ref)
                full = [
                    jnp.concatenate(
                        [
                            r_ref[n, v, 0:FACE, :] + lows[v],
                            r_ref[n, v, FACE:HIGH, :],
                            r_ref[n, v, HIGH:ROWS, :] + highs[v],
                        ],
                        axis=0,
                    )
                    for v in range(nv)
                ]
                moved = reorder(back_ref[...], jnp.concatenate(full, axis=1), 2)
                for v in range(nv):
                    buf[n, v] = moved[:, v * lanes : (v + 1) * lanes]

            write_out(buf, out_ref, sem, first, work)

        ins = [r, lo, hi, below, above, metric_face, face_coef, back_b] + ([] if out is None else [out])
        return call(
            kernel,
            [shape(inst, nv, nodes, 1, lanes)],
            ins,
            "vvvvvvvv" + ("" if out is None else "a"),
            out_spaces="a",
            scratch=[pltpu.VMEM((per, nv, ROWS, lanes), F32), pltpu.SemaphoreType.DMA((per, nv))],
            alias=None if out is None else {8: 0},
            name="last_faces",
        )[0]

    new_state, final_residual = None, None
    chains, last = [None] * groups, None

    def begin(g, swap):
        parts = spectral[g] if last is None else [after(spectral[g][0], last)] + spectral[g][1:]
        z, lo, hi, spec, send_lo, send_hi = first_pass(parts, g * per, LONG if g == groups - 1 else 0)
        chains[g] = (z, lo, hi, swap_faces(send_lo, send_hi) if swap else None, spec)
        return lo

    def local_part(g, count_done):
        nonlocal new_state
        z, lo, hi, swapped, spec = chains[g]
        extra = spec if own_circ else spec + circ_extra(z, lo, hi)
        extra = extra if last is None else after(extra, last)
        if count_done < PASSES - 1:
            z = advance(z, lo, hi, extra, g * per, per, LONG)
        else:
            z, new_state = last_bulk(z, lo, hi, extra, g * per, new_state)
        chains[g] = (z, lo, hi, swapped, spec)
        return z

    def face_part(g, count_done):
        nonlocal final_residual
        z, lo, hi, (below, above), spec = chains[g]
        z = after(z, last)
        if count_done < PASSES - 1:
            lo, hi, *sends = close_faces(z, lo, hi, below, above, g * per, per)
            chains[g] = (z, lo, hi, swap_faces(*sends), spec)
            return lo
        final_residual = last_faces(z, lo, hi, below, above, g * per, final_residual)
        return final_residual

    def pair_begin(g):
        z, lo, hi, _, spec = chains[g]
        z, down, up, send_down, send_up = paired_first(z, lo, hi, after(spec, last), g * per)
        chains[g] = (z, down, up, swap_faces(send_down, send_up), spec)
        return z

    def pair_end(g, *before):
        z, down, up, (below, above), spec = chains[g]
        z, lo, hi, *sends = paired_second(
            z, down, up, below, above, below0, above0, after(spec, last), g * per
        )
        chains[g] = (z, lo, hi, sends, spec)
        return z

    def pair_swap(g):
        z, lo, hi, sends, spec = chains[g]
        sends = lax.optimization_barrier((*sends, last))[:2]
        chains[g] = (z, lo, hi, swap_faces(*sends), spec)

    end = groups - 1
    if own_circ and PASSES == 3:
        for g in range(end):
            last = begin(g, False)
            last = pair_begin(g)
        last = begin(end, True)
        last = local_part(end, 0)
        for g in range(end):
            last = pair_end(g)
        last = face_part(end, 0)
        last = local_part(end, 1)
        for g in range(end):
            pair_swap(g)
        last = face_part(end, 1)
        for g in range(groups):
            last = local_part(g, 2)
        for g in range(groups):
            last = face_part(g, 2)
    else:
        for g in range(groups):
            last = begin(g, True)
            for count_done in range(PASSES):
                last = local_part(g, count_done)
                last = face_part(g, count_done)
    return (new_state.reshape(state.shape), final_residual.reshape(state.shape))


def solution(mesh):
    in_specs = (
        P("tm", None, "elem", None, None),
        P("elem", None, None),
        P(),
        P("tm", None, None, "elem", None),
        P("tm", None, "elem", None),
    )
    out_specs = (P("tm", None, "elem", None, None), P("tm", None, "elem", None, None))
    return jax.shard_map(
        per_device, mesh=mesh, in_specs=in_specs, out_specs=out_specs, check_vma=False
    )
```

```python
import math

import jax
import jax.numpy as jnp
import ml_dtypes
import numpy as np
from jax import lax
from jax.experimental import pallas as pl
from jax.experimental.pallas import tpu as pltpu
from jax.sharding import PartitionSpec as P

PR = 8
PASSES = 3
GROUPS = 2
ROWS = 128
FACE = 32
HIGH = 96

F32 = jnp.float32
BF16 = jnp.bfloat16


def gll_derivative():
    points = np.array([-1.0, -math.sqrt(3.0 / 7.0), 0.0, math.sqrt(3.0 / 7.0), 1.0])
    legendre = (35.0 * points**4 - 30.0 * points**2 + 3.0) / 8.0
    identity = np.eye(5, dtype=bool)
    spacing = np.where(identity, 1.0, points[:, None] - points[None, :])
    matrix = legendre[:, None] / legendre[None, :] / spacing
    corner = np.array([-5.0, 0.0, 0.0, 0.0, 5.0])[None, :]
    return np.where(identity, corner, matrix)


def coupling_value(offset, count):
    offset = offset % count
    if offset == 0:
        return 0.0
    angle = math.pi * offset / count
    return 0.5 * (-1.0) ** offset * math.cos(angle) / math.sin(angle)


FIRST = ((8, 16), (24, 40), (104, 112))
LAST = ((16, 24), (40, 56), (112, 120))
ENDS = 64


def node_rows():
    rows = np.zeros((5, 5, 5), dtype=np.int64)
    face_rest = list(range(0, 11)) + [16, 17, 18, 24]
    rest = [40] + list(range(56, HIGH)) + list(range(HIGH + 25, ROWS))
    face_used, used = 0, 0
    for i in range(5):
        for k in range(5):
            if k in (0, 4):
                local = (11 if k == 0 else 19) + i
            else:
                local = face_rest[face_used]
                face_used += 1
            rows[i, 0, k], rows[i, 4, k] = local, HIGH + local
            for j in range(1, 4):
                if k in (0, 4):
                    rows[i, j, k] = (25 if k == 0 else 41) + 3 * i + j - 1
                else:
                    rows[i, j, k] = rest[used]
                    used += 1
    return rows.reshape(125)


def end_rows():
    return [r for part in (FIRST, LAST) for a, b in part for r in range(a, b)]


def tables(own_circ):
    table = gll_derivative()
    eye = np.eye(5)
    first, last = np.diag([1.0, 0, 0, 0, 0]), np.diag([0, 0, 0, 0, 1.0])
    to_first, to_last = np.zeros((5, 5)), np.zeros((5, 5))
    to_first[0, 4] = 1.0
    to_last[4, 0] = 1.0

    def along(matrix, direction):
        parts = [eye, eye, eye]
        parts[direction] = matrix
        return np.kron(np.kron(parts[0], parts[1]), parts[2])

    rows = node_rows()
    order = np.zeros((ROWS, ROWS))
    order[rows, np.arange(125)] = 1.0

    def placed(matrix):
        return order[:, :125] @ matrix @ order[:, :125].T

    mix, damp = [], []
    for d in range(3):
        mix.append(placed(along(table - 5.0 * last + 5.0 * first, d)))
        damp.append(placed(along(5.0 * last + 5.0 * first, d)))
    if own_circ:
        mix[0] = mix[0] + placed(along(5.0 * to_last - 5.0 * to_first, 0))
        damp[0] = damp[0] + placed(along(-5.0 * to_last - 5.0 * to_first, 0))
    ends = end_rows()
    axial_mix = placed(along(5.0 * to_last - 5.0 * to_first, 2))[:, ends]
    axial_damp = placed(along(-5.0 * to_last - 5.0 * to_first, 2))[:, ends]
    none = np.zeros((ROWS, ENDS))

    def pair(matrix):
        return [np.concatenate([matrix, none], 1), np.concatenate([none, matrix], 1)]

    fluxes = np.stack(mix + pair(axial_mix)).astype(np.float32)
    dampers = np.stack(damp + pair(axial_damp)).astype(np.float32)
    return order, fluxes, dampers


def halves(values):
    high = values.astype(BF16)
    low = (values - high.astype(F32)).astype(BF16)
    return high, low


def dot32(a, b):
    return jnp.dot(a, b, preferred_element_type=F32)


def reorder(matrix, values, terms):
    total = None
    for _ in range(terms):
        part = values.astype(BF16)
        moved = dot32(matrix, part)
        total = moved if total is None else total + moved
        values = values - part.astype(F32)
    return total


SIDE = 25


def put_rows(ref, at, v, value):
    ref[(*at, pl.ds(SIDE * v, SIDE), slice(None))] = value[0:SIDE]


def get_rows(ref, at, v):
    rows = ref[(*at, pl.ds(SIDE * v, SIDE), slice(None))]
    return jnp.concatenate([rows, jnp.zeros((FACE - SIDE, rows.shape[1]), F32)], axis=0)


def mixed(weights, parts):
    total = weights[0] * parts[0]
    for weight, part in zip(weights[1:], parts[1:]):
        total = total + weight * part
    return total


VMEM_LIMIT = 20 * 2**20
LONG = 2 * 10**9


def call(kernel, outs, ins, in_spaces, out_spaces=None, scratch=(), flops=0, alias=None, name=None):
    out_spaces = out_spaces or ["v"] * len(outs)
    space = {"v": pltpu.VMEM, "s": pltpu.SMEM, "a": pl.ANY, "h": pltpu.HBM}
    return pl.pallas_call(
        kernel,
        out_shape=outs,
        in_specs=[pl.BlockSpec(memory_space=space[s]) for s in in_spaces],
        out_specs=[pl.BlockSpec(memory_space=space[s]) for s in out_spaces],
        scratch_shapes=list(scratch),
        input_output_aliases=alias or {},
        compiler_params=pltpu.CompilerParams(vmem_limit_bytes=VMEM_LIMIT),
        cost_estimate=pl.CostEstimate(flops=max(flops, 1), bytes_accessed=1, transcendentals=0),
        name=name,
    )(*ins)


def shape(*dims, dtype=F32):
    return jax.ShapeDtypeStruct(dims, dtype)


def per_device(state, metric_scale, flux_jacobians, preconditioner, inflow):
    inst, nv, _, nodes, lanes = state.shape
    n_tm = lax.axis_size("tm")
    n_elem = lax.axis_size("elem")
    count = inst * n_tm
    own_circ = n_elem == PR
    block = ROWS // n_tm
    groups = GROUPS if inst % GROUPS == 0 else 1
    per = inst // groups
    order, flux_table, damp_table = tables(own_circ)
    order_b = order.astype(ml_dtypes.bfloat16)
    back_b = np.ascontiguousarray(order.T).astype(ml_dtypes.bfloat16)
    pairs = (nv + 1) // 2
    depth = nv * ROWS + pairs * 2 * ENDS
    node_row = node_rows()
    inlet_table = np.zeros((ROWS, ROWS), dtype=np.float32)
    inlet_table[node_row[0::5], np.arange(25)] = 1.0

    damping = jnp.max(jnp.sum(jnp.abs(flux_jacobians), axis=2), axis=1)
    coef = jnp.concatenate([flux_jacobians.reshape(-1), damping])
    precond = preconditioner.reshape(inst, nv, nv, lanes)
    inlet = jnp.pad(inflow.reshape(inst * nv, 25), ((0, ROWS - inst * nv), (0, ROWS - 25)))
    mix_index = np.full((ROWS, ROWS), -1, dtype=np.int32)
    for n in range(inst):
        for v in range(nv):
            for w in range(nv):
                mix_index[n * nv + w, n * nv + v] = v * nv + w

    def jac(ref, d, v, w):
        return ref[(d * nv + v) * nv + w]

    def damp(ref, d):
        return ref[3 * nv * nv + d]

    state_rows = state.reshape(inst, nv, nodes, 1, lanes)
    starts = [min(q * block, nodes - block) for q in range(n_tm)]
    spectral_order = np.zeros((ROWS, ROWS))
    for q in range(n_tm):
        for r in range(block):
            if starts[q] + r >= q * block:
                spectral_order[:, q * block + r] = order[:, starts[q] + r]

    def pack_kernel(state_ref, *refs):
        outs, sem = refs[:n_tm], refs[n_tm]
        me = lax.axis_index("tm")
        copies = []
        for d in range(n_tm):
            start = jnp.minimum(lax.rem(me + d, n_tm) * block, nodes - block)
            copies.append(
                pltpu.make_async_copy(state_ref.at[:, :, pl.ds(start, block), 0, :], outs[d], sem.at[d])
            )
        for copy in copies:
            copy.start()
        for copy in copies:
            copy.wait()

    piece = shape(inst, nv, block, lanes)
    pieces = call(
        pack_kernel,
        [piece] * n_tm,
        [state_rows],
        "h",
        scratch=[pltpu.SemaphoreType.DMA((n_tm,))],
        name="pack",
    )

    def after(x, *before):
        return lax.optimization_barrier((x, *before))[0]

    def along_tm(x, d):
        return lax.ppermute(x, "tm", [(i, (i + d) % n_tm) for i in range(n_tm)])

    def along_elem(x, d):
        return lax.ppermute(x, "elem", [(i, (i + d) % n_elem) for i in range(n_elem)])

    arrived = [pieces[0]] + [None] * (n_tm - 1)
    for d in sorted(range(1, n_tm), key=lambda d: abs(2 * d - n_tm)):
        arrived[d] = along_tm(pieces[d], d)

    scale_at = inst * nv + -(-inst * nv // (FACE // 8))

    def table_place(index):
        return inst * nv + index // (FACE // 8), 8 * (index % (FACE // 8))

    def prep_kernel(
        state_ref, metric_ref, coef_ref, order_ref, flux_ref, damp_ref, inlet_ref, inlet_table_ref, mix_ref, p_ref,
        x_ref, lo_ref, hi_ref, m_ref, mf_ref, lhs_ref, col_ref, fc_ref, pc_ref, low_table_ref, high_table_ref, padded_ref, buf, sem,
    ):
        buf[pl.ds(ROWS - 8, 8), :] = jnp.zeros((8, lanes), F32)
        padded_ref[:, :, pl.ds(ROWS - 8, 8), :] = jnp.zeros((inst, nv, 8, lanes), F32)
        copies = [
            pltpu.make_async_copy(metric_ref.at[:, 0, :], buf.at[pl.ds(0, nodes), :], sem.at[0]),
        ]
        for n in range(inst):
            for v in range(nv):
                copies.append(
                    pltpu.make_async_copy(
                        state_ref.at[n, v, :, 0, :],
                        padded_ref.at[n, v, pl.ds(0, nodes), :],
                        sem.at[1 + n * nv + v],
                    )
                )
        for copy in copies:
            copy.start()
        for copy in copies:
            copy.wait()
        metric = reorder(order_ref[...], buf[...], 3)
        m_ref[...] = metric
        row = lax.broadcasted_iota(jnp.int32, (FACE, lanes), 0)
        mf_ref[0] = jnp.where(row < 25, metric[0:FACE], 0.0)
        mf_ref[1] = jnp.where(row < 25, metric[HIGH:ROWS], 0.0)
        for v in range(nv):
            for w in range(nv):
                value, own = jac(coef_ref, 1, v, w), damp(coef_ref, 1) if v == w else 0.0
                fc_ref[0, v, pl.ds(w, 1), :] = jnp.full((1, lanes), -5.0 * (value + own), F32)
                fc_ref[1, v, pl.ds(w, 1), :] = jnp.full((1, lanes), 5.0 * (value - own), F32)
        for side in range(2):
            tables_of = [fc_ref[side, u] for u in range(nv)]
            for n in range(inst):
                for v in range(nv):
                    weights = [p_ref[n, v, pl.ds(u, 1), :] for u in range(nv)]
                    update = mixed(weights, tables_of)
                    pc_ref[side, n, v] = update
                    at, row = table_place(n * nv + v)
                    table_ref = (low_table_ref, high_table_ref)[side]
                    table_ref[at, pl.ds(row, 8), :] = jnp.concatenate(
                        [update, jnp.zeros((8 - nv, lanes), F32)], axis=0
                    )
            for spare in range(inst * nv, (scale_at - inst * nv) * (FACE // 8)):
                at, row = table_place(spare)
                table_ref[at, pl.ds(row, 8), :] = jnp.zeros((8, lanes), F32)
            table_ref[scale_at] = mf_ref[side]
        for v in range(nv):
            rows = pl.ds(v * ROWS, ROWS)
            for w in range(nv):
                total = mixed([jac(coef_ref, d, v, w) for d in range(3)], [flux_ref[d] for d in range(3)])
                if v == w:
                    for d in range(3):
                        total = total + damp(coef_ref, d) * damp_ref[d]
                high, low = halves(total)
                at = w * ROWS
                lhs_ref[rows, pl.ds(at, ROWS)] = high
                lhs_ref[rows, pl.ds(depth + at, ROWS)] = low
            for c in range(pairs):
                total = jac(coef_ref, 2, v, 2 * c) * flux_ref[3]
                if 2 * c + 1 < nv:
                    total = total + jac(coef_ref, 2, v, 2 * c + 1) * flux_ref[4]
                if v // 2 == c:
                    total = total + damp(coef_ref, 2) * damp_ref[3 + v % 2]
                high, low = halves(total)
                at = nv * ROWS + c * 2 * ENDS
                lhs_ref[rows, pl.ds(at, 2 * ENDS)] = high
                lhs_ref[rows, pl.ds(depth + at, 2 * ENDS)] = low
        cols = lax.dot_general(
            inlet_table_ref[...],
            inlet_ref[...],
            (((1,), (1,)), ((), ())),
            precision=lax.Precision.HIGHEST,
            preferred_element_type=F32,
        )
        blend = jnp.zeros((ROWS, ROWS), F32)
        for v in range(nv):
            for w in range(nv):
                value = jac(coef_ref, 2, v, w)
                if v == w:
                    value = value + damp(coef_ref, 2)
                blend = jnp.where(mix_ref[...] == v * nv + w, -5.0 * value, blend)
        cols = jnp.dot(cols, blend, precision=lax.Precision.HIGHEST, preferred_element_type=F32)
        col_ref[...] = metric[:, 0:1] * cols
        for n in range(inst):
            natural = jnp.concatenate([padded_ref[n, v] for v in range(nv)], axis=1)
            moved = reorder(order_ref[...], natural, 3)
            for v in range(nv):
                part = moved[:, v * lanes : (v + 1) * lanes]
                x_ref[n, v] = part
                lo_ref[n, v] = part[0:FACE]
                hi_ref[n, v] = part[HIGH:ROWS]
                low_table_ref[n * nv + v] = part[0:FACE]
                high_table_ref[n * nv + v] = part[HIGH:ROWS]

    x0, lo0, hi0, metric, metric_face, lhs, inlet_cols, face_coef, face_update, low_table, high_table = call(
        prep_kernel,
        [
            shape(inst, nv, ROWS, lanes),
            shape(inst, nv, FACE, lanes),
            shape(inst, nv, FACE, lanes),
            shape(ROWS, lanes),
            shape(2, FACE, lanes),
            shape(nv * ROWS, 2 * depth, dtype=BF16),
            shape(ROWS, ROWS),
            shape(2, nv, nv, lanes),
            shape(2, inst, nv, nv, lanes),
            shape(scale_at + 1, FACE, lanes),
            shape(scale_at + 1, FACE, lanes),
        ],
        [
            state_rows,
            metric_scale.reshape(nodes, 1, lanes),
            coef,
            order_b,
            flux_table,
            damp_table,
            inlet,
            inlet_table,
            mix_index,
            precond,
        ],
        "hhsvvvvvvv",
        scratch=[
            pltpu.VMEM((inst, nv, ROWS, lanes), F32),
            pltpu.VMEM((ROWS, lanes), F32),
            pltpu.SemaphoreType.DMA((1 + inst * nv,)),
        ],
        name="prep",
    )

    def bulk(xs, lhs_ref):
        cols = []
        lane = lax.broadcasted_iota(jnp.int32, (ENDS // 2, lanes), 1)
        for x in xs:
            ends = []
            for part in x:
                first = jnp.concatenate([part[a:b] for a, b in FIRST], axis=0)
                last = jnp.concatenate([part[a:b] for a, b in LAST], axis=0)
                ends.append(jnp.where(lane == lanes - 1, last, pltpu.roll(first, lanes - 1, 1)))
                ends.append(jnp.where(lane == 0, 0.0, pltpu.roll(last, 1, 1)))
            if nv % 2:
                ends.append(jnp.zeros((ENDS, lanes), F32))
            cols.append(jnp.concatenate(list(x) + ends, axis=0))
        high, low = halves(jnp.concatenate(cols, axis=1) if len(cols) > 1 else cols[0])
        both = dot32(lhs_ref[...], jnp.concatenate([high, high], axis=0))
        return both + dot32(lhs_ref[:, 0:depth], low)

    def block_of(result, n, v):
        return result[v * ROWS : (v + 1) * ROWS, n * lanes : (n + 1) * lanes]

    def whole(lo_ref, z_ref, hi_ref, n, at, v):
        return jnp.concatenate([lo_ref[n, v], z_ref[at, v, FACE:HIGH, :], hi_ref[n, v]], axis=0)


    def advance(z, lo, hi, extra, first, size, flops=0):
        def kernel(*refs):
            z_ref, lo_ref, hi_ref, m_ref, p_ref, lhs_ref = refs[:6]
            out_ref = refs[-1]
            metric_value = m_ref[...]
            for at in range(0, size, 2):
                ids = list(range(at, min(at + 2, size)))
                xs = [[whole(lo_ref, z_ref, hi_ref, n, n, v) for v in range(nv)] for n in ids]
                result = bulk(xs, lhs_ref)
                for m, n in enumerate(ids):
                    res = [metric_value * block_of(result, m, v) for v in range(nv)]
                    if extra is not None:
                        res = [res[v] + refs[6][n, v] for v in range(nv)]
                    for v in range(nv):
                        weights = [p_ref[first + n, v, pl.ds(w, 1), :] for w in range(nv)]
                        out_ref[n, v] = xs[m][v] - mixed(weights, res)

        ins = [z, lo, hi, metric, precond, lhs]
        ins = ins + ([] if extra is None else [extra])
        return call(
            kernel,
            [shape(size, nv, ROWS, lanes)],
            ins,
            "vvvvvv" + ("" if extra is None else "v"),
            flops=flops,
            name="advance",
        )[0]

    def face_terms(n, lo_ref, hi_ref, below, above, table_of, mf_ref):
        position = lax.rem(lax.axis_index("elem") + PR // 2, PR)
        low_w, high_w = [], []
        for v in range(nv):
            sign = -1.0 if v == 2 else 1.0
            low_w.append(jnp.where(position == 0, sign * lo_ref[n, v], below[v]))
            high_w.append(jnp.where(position == PR - 1, sign * hi_ref[n, v], above[v]))
        lows, highs = [], []
        for v in range(nv):
            lows.append(mf_ref[0] * mixed([table_of(0, v, w) for w in range(nv)], low_w))
            highs.append(mf_ref[1] * mixed([table_of(1, v, w) for w in range(nv)], high_w))
        return lows, highs

    def swap_faces(lo, hi):
        return along_elem(hi, 1), along_elem(lo, -1)

    def close_faces(z, lo, hi, below, above, first, size, send=True):
        def kernel(z_ref, lo_ref, hi_ref, below_ref, above_ref, mf_ref, pc_ref, nlo_ref, nhi_ref, *sends):
            for n in range(size):

                def table_of(side, v, w, n=n):
                    return pc_ref[side, first + n, v, pl.ds(w, 1), :]

                flat = not sends
                below = [below_ref[n * nv + v] if flat else get_rows(below_ref, (n,), v) for v in range(nv)]
                above = [above_ref[n * nv + v] if flat else get_rows(above_ref, (n,), v) for v in range(nv)]
                lows, highs = face_terms(n, lo_ref, hi_ref, below, above, table_of, mf_ref)
                for v in range(nv):
                    new_lo, new_hi = z_ref[n, v, 0:FACE, :] - lows[v], z_ref[n, v, HIGH:ROWS, :] - highs[v]
                    nlo_ref[n, v], nhi_ref[n, v] = new_lo, new_hi
                    if sends:
                        put_rows(sends[0], (n,), v, new_lo)
                        put_rows(sends[1], (n,), v, new_hi)

        return call(
            kernel,
            [shape(size, nv, FACE, lanes)] * 2 + ([shape(size, ROWS, lanes)] * 2 if send else []),
            [z, lo, hi, below, above, metric_face, face_update],
            "v" * 7,
            name="faces",
        )

    def paired_first(z, lo, hi, spec, first):
        def kernel(z_ref, lo_ref, hi_ref, m_ref, p_ref, lhs_ref, spec_ref, out_ref, down_ref, up_ref, send_down_ref, send_up_ref):
            metric_value = m_ref[...]
            for at in range(0, per, 2):
                ids = list(range(at, min(at + 2, per)))
                xs = [[whole(lo_ref, z_ref, hi_ref, n, n, v) for v in range(nv)] for n in ids]
                result = bulk(xs, lhs_ref)
                for m, n in enumerate(ids):
                    res = [metric_value * block_of(result, m, v) + spec_ref[n, v] for v in range(nv)]
                    for v in range(nv):
                        weights = [p_ref[first + n, v, pl.ds(w, 1), :] for w in range(nv)]
                        value = xs[m][v] - mixed(weights, res)
                        out_ref[n, v] = value
                        down_ref[0, n, v], up_ref[0, n, v] = lo_ref[n, v], hi_ref[n, v]
                        down_ref[1, n, v], up_ref[1, n, v] = value[0:FACE], value[HIGH:ROWS]
                        put_rows(send_down_ref, (0, n), v, lo_ref[n, v])
                        put_rows(send_up_ref, (0, n), v, hi_ref[n, v])
                        put_rows(send_down_ref, (1, n), v, value[0:FACE])
                        put_rows(send_up_ref, (1, n), v, value[HIGH:ROWS])

        return call(
            kernel,
            [shape(per, nv, ROWS, lanes)]
            + [shape(2, per, nv, FACE, lanes)] * 2
            + [shape(2, per, ROWS, lanes)] * 2,
            [z, lo, hi, metric, precond, lhs, spec],
            "v" * 7,
            name="paired_first",
        )

    def paired_second(z, down, up, below, above, below_table, above_table, spec, first):
        def kernel(*refs):
            z_ref, down_ref, up_ref, below_ref, above_ref = refs[:5]
            low_ref, high_ref, below_table_ref, above_table_ref = refs[5:9]
            m_ref, p_ref, lhs_ref, spec_ref, out_ref, out_lo_ref, out_hi_ref, send_lo_ref, send_hi_ref = refs[9:]
            metric_value = m_ref[...]
            position = lax.rem(lax.axis_index("elem") + PR // 2, PR)

            def update(table_ref, n, values):
                result = []
                for v in range(nv):
                    at, row = table_place((first + n) * nv + v)
                    weights = [table_ref[at, pl.ds(row + w, 1), :] for w in range(nv)]
                    result.append(table_ref[scale_at] * mixed(weights, values))
                return result

            def across(at, own, other):
                return [
                    jnp.where(position == at, -own[v] if v == 2 else own[v], other[v]) for v in range(nv)
                ]

            def minus(a, b):
                return [p - q for p, q in zip(a, b)]

            for at in range(0, per, 2):
                ids = list(range(at, min(at + 2, per)))
                xs, beyond = [], []
                for n in ids:
                    lo, zlo = ([down_ref[k, n, v] for v in range(nv)] for k in range(2))
                    hi, zhi = ([up_ref[k, n, v] for v in range(nv)] for k in range(2))
                    low_w, low_z = ([get_rows(below_ref, (k, n), v) for v in range(nv)] for k in range(2))
                    high_w, high_z = ([get_rows(above_ref, (k, n), v) for v in range(nv)] for k in range(2))
                    new_lo = minus(zlo, update(low_ref, n, across(0, lo, low_w)))
                    new_hi = minus(zhi, update(high_ref, n, across(PR - 1, hi, high_w)))
                    next_low = across(0, new_lo, minus(low_z, update(below_table_ref, n, lo)))
                    next_high = across(PR - 1, new_hi, minus(high_z, update(above_table_ref, n, hi)))
                    xs.append(
                        [
                            jnp.concatenate([new_lo[v], z_ref[n, v, FACE:HIGH, :], new_hi[v]], axis=0)
                            for v in range(nv)
                        ]
                    )
                    beyond.append((update(low_ref, n, next_low), update(high_ref, n, next_high)))
                result = bulk(xs, lhs_ref)
                for m, n in enumerate(ids):
                    res = [metric_value * block_of(result, m, v) + spec_ref[n, v] for v in range(nv)]
                    for v in range(nv):
                        weights = [p_ref[first + n, v, pl.ds(w, 1), :] for w in range(nv)]
                        value = xs[m][v] - mixed(weights, res)
                        lo, hi = value[0:FACE] - beyond[m][0][v], value[HIGH:ROWS] - beyond[m][1][v]
                        out_ref[n, v] = value
                        out_lo_ref[n, v] = lo
                        out_hi_ref[n, v] = hi
                        put_rows(send_lo_ref, (n,), v, lo)
                        put_rows(send_hi_ref, (n,), v, hi)

        return call(
            kernel,
            [shape(per, nv, ROWS, lanes)]
            + [shape(per, nv, FACE, lanes)] * 2
            + [shape(per, ROWS, lanes)] * 2,
            [z, down, up, below, above, low_table, high_table, below_table, above_table]
            + [metric, precond, lhs, spec],
            "v" * 13,
            name="paired_second",
        )

    def circ_extra(z, lo, hi):
        x = jnp.concatenate([lo, z[:, :, FACE:HIGH], hi], axis=2)
        picks = np.zeros((2, 25, ROWS), dtype=np.float32)
        picks[0, np.arange(25), node_row[0:25]] = 1.0
        picks[1, np.arange(25), node_row[100:125]] = 1.0
        exact = lax.Precision.HIGHEST

        def picked(which):
            return jnp.einsum("pq,nvqa->nvpa", picks[which], x, precision=exact)

        def mix(values):
            return jnp.einsum("vw,nwqa->nvqa", flux_jacobians[0], values, precision=exact)

        def placed(which, values):
            return jnp.einsum("pq,nvpa->nvqa", picks[which], values, precision=exact)

        above, below = along_elem(picked(0), -PR), along_elem(picked(1), PR)
        high_term = 5.0 * (mix(above) - damping[0] * above)
        low_term = -5.0 * (mix(below) + damping[0] * below)
        return metric * (placed(1, high_term) + placed(0, low_term))

    below0, above0 = swap_faces(low_table, high_table)
    t0 = advance(x0, lo0, hi0, None if own_circ else circ_extra(x0, lo0, hi0), 0, inst)
    tlo, thi = close_faces(t0, lo0, hi0, below0, above0, 0, inst, send=False)

    half_pair = n_tm % 2 == 0

    def weight(offset, sign):
        return 0.5 * (coupling_value(offset, count) + sign * coupling_value(offset + count // 2, count))

    def weighted(terms):
        terms = [(c, x) for c, x in terms if abs(c) > 1e-12]
        return mixed([c for c, _ in terms], [x for _, x in terms])

    def coupling_kernel(*refs):
        x_refs, outs = refs[:n_tm], refs[n_tm:]

        def body(step, carry):
            v, rows = step // (block // 8), pl.ds(pl.multiple_of((step % (block // 8)) * 8, 8), 8)
            x = [[x_refs[d][i, v, rows, :] for i in range(inst)] for d in range(n_tm)]
            if half_pair:
                half = n_tm // 2
                sources = [(d, i) for d in range(half) for i in range(inst)]
                sums = [x[d][i] + x[d + half][i] for d, i in sources]
                diffs = [x[d][i] - x[d + half][i] for d, i in sources]
                for e in range(half):
                    for j in range(inst):
                        offsets = [inst * (e + d) + j - i for d, i in sources]
                        even = weighted([(weight(o, 1), s) for o, s in zip(offsets, sums)])
                        odd = weighted([(weight(o, -1), s) for o, s in zip(offsets, diffs)])
                        outs[e * groups + j // per][j % per, v, rows, :] = even + odd
                        outs[(e + half) * groups + j // per][j % per, v, rows, :] = even - odd
            else:
                sources = [(d, i) for d in range(n_tm) for i in range(inst)]
                for e in range(n_tm):
                    for j in range(inst):
                        offsets = [inst * (e + d) + j - i for d, i in sources]
                        outs[e * groups + j // per][j % per, v, rows, :] = weighted(
                            [(coupling_value(o, count), x[d][i]) for o, (d, i) in zip(offsets, sources)]
                        )
            return carry

        lax.fori_loop(0, nv * (block // 8), body, 0)

    coupled = call(
        coupling_kernel,
        [shape(per, nv, block, lanes)] * (n_tm * groups),
        arrived,
        "v" * n_tm,
        name="coupling",
    )
    spectral = [[coupled[g]] + [None] * (n_tm - 1) for g in range(groups)]
    for g in range(groups):
        for e in sorted(range(1, n_tm), key=lambda e: abs(2 * e - n_tm)):
            spectral[g][e] = along_tm(coupled[e * groups + g], e)

    def first_pass(parts, first, flops=0):
        distances = list(range(n_tm))
        if first > 0:
            distances.sort(key=lambda d: min(d, n_tm - d))

        def kernel(*refs):
            part_refs = [refs[distances.index(d)] for d in range(n_tm)]
            t_ref, tlo_ref, thi_ref, p_ref, col_ref, order_ref = refs[n_tm : n_tm + 6]
            x_ref, lo_ref, hi_ref, s_ref, send_lo_ref, send_hi_ref, buf = refs[n_tm + 6 :]
            me = lax.axis_index("tm")
            for d in range(n_tm):
                start = pl.multiple_of(lax.rem(me - d + n_tm, n_tm) * block, block)
                for n in range(per):
                    for v in range(nv):
                        buf[n, v, pl.ds(start, block), :] = part_refs[d][n, v]
            lane = lax.broadcasted_iota(jnp.int32, (ROWS, lanes), 1)
            for n in range(per):
                natural = jnp.concatenate([buf[n, v] for v in range(nv)], axis=1)
                moved = reorder(order_ref[...], natural, 2)
                terms = []
                for v in range(nv):
                    c = (first + n) * nv + v
                    column = jnp.broadcast_to(col_ref[:, c : c + 1], (ROWS, lanes))
                    term = moved[:, v * lanes : (v + 1) * lanes] + jnp.where(lane == 0, column, 0.0)
                    s_ref[n, v] = term
                    terms.append(term)
                for v in range(nv):
                    weights = [p_ref[first + n, v, pl.ds(w, 1), :] for w in range(nv)]
                    x = whole(tlo_ref, t_ref, thi_ref, first + n, first + n, v) - mixed(weights, terms)
                    x_ref[n, v] = x
                    lo_ref[n, v] = x[0:FACE]
                    hi_ref[n, v] = x[HIGH:ROWS]
                    put_rows(send_lo_ref, (n,), v, x[0:FACE])
                    put_rows(send_hi_ref, (n,), v, x[HIGH:ROWS])

        return call(
            kernel,
            [
                shape(per, nv, ROWS, lanes),
                shape(per, nv, FACE, lanes),
                shape(per, nv, FACE, lanes),
                shape(per, nv, ROWS, lanes),
                shape(per, ROWS, lanes),
                shape(per, ROWS, lanes),
            ],
            [parts[d] for d in distances] + [t0, tlo, thi, precond, inlet_cols, spectral_order.astype(ml_dtypes.bfloat16)],
            "v" * (n_tm + 6),
            scratch=[pltpu.VMEM((per, nv, ROWS, lanes), F32)],
            flops=flops,
            name="first_pass",
        )

    def write_out(moved_ref, out_ref, sem, first, work, meanwhile=None):
        copies = []
        for n in range(per):
            work(n)
            for v in range(nv):
                copy = pltpu.make_async_copy(
                    moved_ref.at[n, v, pl.ds(0, nodes), :], out_ref.at[first + n, v, :, 0, :], sem.at[n, v]
                )
                copy.start()
                copies.append(copy)
        if meanwhile is not None:
            meanwhile()
        for copy in copies:
            copy.wait()

    def last_bulk(z, lo, hi, extra, first, out):
        def kernel(*refs):
            z_ref, lo_ref, hi_ref, m_ref, lhs_ref, extra_ref, back_ref = refs[:7]
            r_ref, out_ref, buf, sem = refs[-4:]
            metric_value = m_ref[...]

            def work(n):
                x = [whole(lo_ref, z_ref, hi_ref, n, n, v) for v in range(nv)]
                moved = reorder(back_ref[...], jnp.concatenate(x, axis=1), 3)
                for v in range(nv):
                    buf[n, v] = moved[:, v * lanes : (v + 1) * lanes]

            def residual():
                for at in range(0, per, 2):
                    ids = list(range(at, min(at + 2, per)))
                    xs = [[whole(lo_ref, z_ref, hi_ref, n, n, v) for v in range(nv)] for n in ids]
                    result = bulk(xs, lhs_ref)
                    for m, n in enumerate(ids):
                        for v in range(nv):
                            r_ref[n, v] = metric_value * block_of(result, m, v) + extra_ref[n, v]

            write_out(buf, out_ref, sem, first, work, residual)

        ins = [z, lo, hi, metric, lhs, extra, back_b] + ([] if out is None else [out])
        return call(
            kernel,
            [shape(per, nv, ROWS, lanes), shape(inst, nv, nodes, 1, lanes)],
            ins,
            "vvvvvvv" + ("" if out is None else "a"),
            out_spaces="va",
            scratch=[pltpu.VMEM((per, nv, ROWS, lanes), F32), pltpu.SemaphoreType.DMA((per, nv))],
            alias=None if out is None else {7: 1},
            name="last_bulk",
        )

    def last_faces(r, lo, hi, below, above, first, out):
        def kernel(*refs):
            r_ref, lo_ref, hi_ref, below_ref, above_ref, mf_ref, fc_ref, back_ref = refs[:8]
            out_ref, buf, sem = refs[-3:]

            def table_of(side, v, w):
                return fc_ref[side, v, pl.ds(w, 1), :]

            def work(n):
                below = [get_rows(below_ref, (n,), v) for v in range(nv)]
                above = [get_rows(above_ref, (n,), v) for v in range(nv)]
                lows, highs = face_terms(n, lo_ref, hi_ref, below, above, table_of, mf_ref)
                full = [
                    jnp.concatenate(
                        [
                            r_ref[n, v, 0:FACE, :] + lows[v],
                            r_ref[n, v, FACE:HIGH, :],
                            r_ref[n, v, HIGH:ROWS, :] + highs[v],
                        ],
                        axis=0,
                    )
                    for v in range(nv)
                ]
                moved = reorder(back_ref[...], jnp.concatenate(full, axis=1), 2)
                for v in range(nv):
                    buf[n, v] = moved[:, v * lanes : (v + 1) * lanes]

            write_out(buf, out_ref, sem, first, work)

        ins = [r, lo, hi, below, above, metric_face, face_coef, back_b] + ([] if out is None else [out])
        return call(
            kernel,
            [shape(inst, nv, nodes, 1, lanes)],
            ins,
            "vvvvvvvv" + ("" if out is None else "a"),
            out_spaces="a",
            scratch=[pltpu.VMEM((per, nv, ROWS, lanes), F32), pltpu.SemaphoreType.DMA((per, nv))],
            alias=None if out is None else {8: 0},
            name="last_faces",
        )[0]

    new_state, final_residual = None, None
    chains, last = [None] * groups, None

    def begin(g, swap):
        parts = spectral[g] if last is None else [after(spectral[g][0], last)] + spectral[g][1:]
        z, lo, hi, spec, send_lo, send_hi = first_pass(parts, g * per, LONG if g == groups - 1 else 0)
        chains[g] = (z, lo, hi, swap_faces(send_lo, send_hi) if swap else None, spec)
        return lo

    def local_part(g, count_done):
        nonlocal new_state
        z, lo, hi, swapped, spec = chains[g]
        extra = spec if own_circ else spec + circ_extra(z, lo, hi)
        extra = extra if last is None else after(extra, last)
        if count_done < PASSES - 1:
            z = advance(z, lo, hi, extra, g * per, per, LONG)
        else:
            z, new_state = last_bulk(z, lo, hi, extra, g * per, new_state)
        chains[g] = (z, lo, hi, swapped, spec)
        return z

    def face_part(g, count_done):
        nonlocal final_residual
        z, lo, hi, (below, above), spec = chains[g]
        z = after(z, last)
        if count_done < PASSES - 1:
            lo, hi, *sends = close_faces(z, lo, hi, below, above, g * per, per)
            chains[g] = (z, lo, hi, swap_faces(*sends), spec)
            return lo
        final_residual = last_faces(z, lo, hi, below, above, g * per, final_residual)
        return final_residual

    def pair_begin(g):
        z, lo, hi, _, spec = chains[g]
        z, down, up, send_down, send_up = paired_first(z, lo, hi, after(spec, last), g * per)
        chains[g] = (z, down, up, swap_faces(send_down, send_up), spec)
        return z

    def pair_end(g, *before):
        z, down, up, (below, above), spec = chains[g]
        z, lo, hi, *sends = paired_second(
            z, down, up, below, above, below0, above0, after(spec, last), g * per
        )
        chains[g] = (z, lo, hi, sends, spec)
        return z

    def pair_swap(g):
        z, lo, hi, sends, spec = chains[g]
        sends = lax.optimization_barrier((*sends, last))[:2]
        chains[g] = (z, lo, hi, swap_faces(*sends), spec)

    end = groups - 1
    if own_circ and PASSES == 3:
        for g in range(end):
            last = begin(g, False)
            last = pair_begin(g)
        last = begin(end, False)
        last = pair_begin(end)
        for g in range(end):
            last = pair_end(g)
            pair_swap(g)
            last = local_part(g, 2)
        last = pair_end(end)
        pair_swap(end)
        for g in range(end):
            last = face_part(g, 2)
        last = local_part(end, 2)
        last = face_part(end, 2)
    else:
        for g in range(groups):
            last = begin(g, True)
            for count_done in range(PASSES):
                last = local_part(g, count_done)
                last = face_part(g, count_done)
    return (new_state.reshape(state.shape), final_residual.reshape(state.shape))


def solution(mesh):
    in_specs = (
        P("tm", None, "elem", None, None),
        P("elem", None, None),
        P(),
        P("tm", None, None, "elem", None),
        P("tm", None, "elem", None),
    )
    out_specs = (P("tm", None, "elem", None, None), P("tm", None, "elem", None, None))
    return jax.shard_map(
        per_device, mesh=mesh, in_specs=in_specs, out_specs=out_specs, check_vma=False
    )
```

```python
import math

import jax
import jax.numpy as jnp
import ml_dtypes
import numpy as np
from jax import lax
from jax.experimental import pallas as pl
from jax.experimental.pallas import tpu as pltpu
from jax.sharding import PartitionSpec as P

PR = 8
PASSES = 3
GROUPS = 2
ROWS = 128
FACE = 32
HIGH = 96

F32 = jnp.float32
BF16 = jnp.bfloat16


def gll_derivative():
    points = np.array([-1.0, -math.sqrt(3.0 / 7.0), 0.0, math.sqrt(3.0 / 7.0), 1.0])
    legendre = (35.0 * points**4 - 30.0 * points**2 + 3.0) / 8.0
    identity = np.eye(5, dtype=bool)
    spacing = np.where(identity, 1.0, points[:, None] - points[None, :])
    matrix = legendre[:, None] / legendre[None, :] / spacing
    corner = np.array([-5.0, 0.0, 0.0, 0.0, 5.0])[None, :]
    return np.where(identity, corner, matrix)


def coupling_value(offset, count):
    offset = offset % count
    if offset == 0:
        return 0.0
    angle = math.pi * offset / count
    return 0.5 * (-1.0) ** offset * math.cos(angle) / math.sin(angle)


FIRST = ((8, 16), (24, 40), (104, 112))
LAST = ((16, 24), (40, 56), (112, 120))
ENDS = 64


def node_rows():
    rows = np.zeros((5, 5, 5), dtype=np.int64)
    face_rest = list(range(0, 11)) + [16, 17, 18, 24]
    rest = [40] + list(range(56, HIGH)) + list(range(HIGH + 25, ROWS))
    face_used, used = 0, 0
    for i in range(5):
        for k in range(5):
            if k in (0, 4):
                local = (11 if k == 0 else 19) + i
            else:
                local = face_rest[face_used]
                face_used += 1
            rows[i, 0, k], rows[i, 4, k] = local, HIGH + local
            for j in range(1, 4):
                if k in (0, 4):
                    rows[i, j, k] = (25 if k == 0 else 41) + 3 * i + j - 1
                else:
                    rows[i, j, k] = rest[used]
                    used += 1
    return rows.reshape(125)


def end_rows():
    return [r for part in (FIRST, LAST) for a, b in part for r in range(a, b)]


def tables(own_circ):
    table = gll_derivative()
    eye = np.eye(5)
    first, last = np.diag([1.0, 0, 0, 0, 0]), np.diag([0, 0, 0, 0, 1.0])
    to_first, to_last = np.zeros((5, 5)), np.zeros((5, 5))
    to_first[0, 4] = 1.0
    to_last[4, 0] = 1.0

    def along(matrix, direction):
        parts = [eye, eye, eye]
        parts[direction] = matrix
        return np.kron(np.kron(parts[0], parts[1]), parts[2])

    rows = node_rows()
    order = np.zeros((ROWS, ROWS))
    order[rows, np.arange(125)] = 1.0

    def placed(matrix):
        return order[:, :125] @ matrix @ order[:, :125].T

    mix, damp = [], []
    for d in range(3):
        mix.append(placed(along(table - 5.0 * last + 5.0 * first, d)))
        damp.append(placed(along(5.0 * last + 5.0 * first, d)))
    if own_circ:
        mix[0] = mix[0] + placed(along(5.0 * to_last - 5.0 * to_first, 0))
        damp[0] = damp[0] + placed(along(-5.0 * to_last - 5.0 * to_first, 0))
    ends = end_rows()
    axial_mix = placed(along(5.0 * to_last - 5.0 * to_first, 2))[:, ends]
    axial_damp = placed(along(-5.0 * to_last - 5.0 * to_first, 2))[:, ends]
    none = np.zeros((ROWS, ENDS))

    def pair(matrix):
        return [np.concatenate([matrix, none], 1), np.concatenate([none, matrix], 1)]

    fluxes = np.stack(mix + pair(axial_mix)).astype(np.float32)
    dampers = np.stack(damp + pair(axial_damp)).astype(np.float32)
    return order, fluxes, dampers


def halves(values):
    high = values.astype(BF16)
    low = (values - high.astype(F32)).astype(BF16)
    return high, low


def dot32(a, b):
    return jnp.dot(a, b, preferred_element_type=F32)


def reorder(matrix, values, terms):
    total = None
    for _ in range(terms):
        part = values.astype(BF16)
        moved = dot32(matrix, part)
        total = moved if total is None else total + moved
        values = values - part.astype(F32)
    return total


SIDE = 25


def put_rows(ref, at, v, value):
    ref[(*at, pl.ds(SIDE * v, SIDE), slice(None))] = value[0:SIDE]


def get_rows(ref, at, v):
    rows = ref[(*at, pl.ds(SIDE * v, SIDE), slice(None))]
    return jnp.concatenate([rows, jnp.zeros((FACE - SIDE, rows.shape[1]), F32)], axis=0)


def mixed(weights, parts):
    total = weights[0] * parts[0]
    for weight, part in zip(weights[1:], parts[1:]):
        total = total + weight * part
    return total


VMEM_LIMIT = 20 * 2**20
LONG = 2 * 10**9


def call(kernel, outs, ins, in_spaces, out_spaces=None, scratch=(), flops=0, alias=None, name=None):
    out_spaces = out_spaces or ["v"] * len(outs)
    space = {"v": pltpu.VMEM, "s": pltpu.SMEM, "a": pl.ANY, "h": pltpu.HBM}
    return pl.pallas_call(
        kernel,
        out_shape=outs,
        in_specs=[pl.BlockSpec(memory_space=space[s]) for s in in_spaces],
        out_specs=[pl.BlockSpec(memory_space=space[s]) for s in out_spaces],
        scratch_shapes=list(scratch),
        input_output_aliases=alias or {},
        compiler_params=pltpu.CompilerParams(vmem_limit_bytes=VMEM_LIMIT),
        cost_estimate=pl.CostEstimate(flops=max(flops, 1), bytes_accessed=1, transcendentals=0),
        name=name,
    )(*ins)


def shape(*dims, dtype=F32):
    return jax.ShapeDtypeStruct(dims, dtype)


def per_device(state, metric_scale, flux_jacobians, preconditioner, inflow):
    inst, nv, _, nodes, lanes = state.shape
    n_tm = lax.axis_size("tm")
    n_elem = lax.axis_size("elem")
    count = inst * n_tm
    own_circ = n_elem == PR
    block = ROWS // n_tm
    groups = GROUPS if inst % GROUPS == 0 else 1
    per = inst // groups
    order, flux_table, damp_table = tables(own_circ)
    order_b = order.astype(ml_dtypes.bfloat16)
    back_b = np.ascontiguousarray(order.T).astype(ml_dtypes.bfloat16)
    pairs = (nv + 1) // 2
    depth = nv * ROWS + pairs * 2 * ENDS
    node_row = node_rows()
    inlet_table = np.zeros((ROWS, ROWS), dtype=np.float32)
    inlet_table[node_row[0::5], np.arange(25)] = 1.0

    damping = jnp.max(jnp.sum(jnp.abs(flux_jacobians), axis=2), axis=1)
    coef = jnp.concatenate([flux_jacobians.reshape(-1), damping])
    precond = preconditioner.reshape(inst, nv, nv, lanes)
    inlet = jnp.pad(inflow.reshape(inst * nv, 25), ((0, ROWS - inst * nv), (0, ROWS - 25)))
    mix_index = np.full((ROWS, ROWS), -1, dtype=np.int32)
    for n in range(inst):
        for v in range(nv):
            for w in range(nv):
                mix_index[n * nv + w, n * nv + v] = v * nv + w

    def jac(ref, d, v, w):
        return ref[(d * nv + v) * nv + w]

    def damp(ref, d):
        return ref[3 * nv * nv + d]

    state_rows = state.reshape(inst, nv, nodes, 1, lanes)
    starts = [min(q * block, nodes - block) for q in range(n_tm)]
    spectral_order = np.zeros((ROWS, ROWS))
    for q in range(n_tm):
        for r in range(block):
            if starts[q] + r >= q * block:
                spectral_order[:, q * block + r] = order[:, starts[q] + r]

    def pack_kernel(state_ref, *refs):
        outs, sem = refs[:n_tm], refs[n_tm]
        me = lax.axis_index("tm")
        copies = []
        for d in range(n_tm):
            start = jnp.minimum(lax.rem(me + d, n_tm) * block, nodes - block)
            copies.append(
                pltpu.make_async_copy(state_ref.at[:, :, pl.ds(start, block), 0, :], outs[d], sem.at[d])
            )
        for copy in copies:
            copy.start()
        for copy in copies:
            copy.wait()

    piece = shape(inst, nv, block, lanes)
    pieces = call(
        pack_kernel,
        [piece] * n_tm,
        [state_rows],
        "h",
        scratch=[pltpu.SemaphoreType.DMA((n_tm,))],
        name="pack",
    )

    def after(x, *before):
        return lax.optimization_barrier((x, *before))[0]

    def along_tm(x, d):
        return lax.ppermute(x, "tm", [(i, (i + d) % n_tm) for i in range(n_tm)])

    def along_elem(x, d):
        return lax.ppermute(x, "elem", [(i, (i + d) % n_elem) for i in range(n_elem)])

    arrived = [pieces[0]] + [None] * (n_tm - 1)
    for d in sorted(range(1, n_tm), key=lambda d: abs(2 * d - n_tm)):
        arrived[d] = along_tm(pieces[d], d)

    scale_at = inst * nv + -(-inst * nv // (FACE // 8))

    def table_place(index):
        return inst * nv + index // (FACE // 8), 8 * (index % (FACE // 8))

    def prep_kernel(
        state_ref, metric_ref, coef_ref, order_ref, flux_ref, damp_ref, inlet_ref, inlet_table_ref, mix_ref, p_ref,
        x_ref, lo_ref, hi_ref, m_ref, mf_ref, lhs_ref, col_ref, fc_ref, pc_ref, low_table_ref, high_table_ref, padded_ref, buf, sem,
    ):
        buf[pl.ds(ROWS - 8, 8), :] = jnp.zeros((8, lanes), F32)
        padded_ref[:, :, pl.ds(ROWS - 8, 8), :] = jnp.zeros((inst, nv, 8, lanes), F32)
        copies = [
            pltpu.make_async_copy(metric_ref.at[:, 0, :], buf.at[pl.ds(0, nodes), :], sem.at[0]),
        ]
        for n in range(inst):
            for v in range(nv):
                copies.append(
                    pltpu.make_async_copy(
                        state_ref.at[n, v, :, 0, :],
                        padded_ref.at[n, v, pl.ds(0, nodes), :],
                        sem.at[1 + n * nv + v],
                    )
                )
        for copy in copies:
            copy.start()
        for copy in copies:
            copy.wait()
        metric = reorder(order_ref[...], buf[...], 3)
        m_ref[...] = metric
        row = lax.broadcasted_iota(jnp.int32, (FACE, lanes), 0)
        mf_ref[0] = jnp.where(row < 25, metric[0:FACE], 0.0)
        mf_ref[1] = jnp.where(row < 25, metric[HIGH:ROWS], 0.0)
        for v in range(nv):
            for w in range(nv):
                value, own = jac(coef_ref, 1, v, w), damp(coef_ref, 1) if v == w else 0.0
                fc_ref[0, v, pl.ds(w, 1), :] = jnp.full((1, lanes), -5.0 * (value + own), F32)
                fc_ref[1, v, pl.ds(w, 1), :] = jnp.full((1, lanes), 5.0 * (value - own), F32)
        for side in range(2):
            tables_of = [fc_ref[side, u] for u in range(nv)]
            for n in range(inst):
                for v in range(nv):
                    weights = [p_ref[n, v, pl.ds(u, 1), :] for u in range(nv)]
                    update = mixed(weights, tables_of)
                    pc_ref[side, n, v] = update
                    at, row = table_place(n * nv + v)
                    table_ref = (low_table_ref, high_table_ref)[side]
                    table_ref[at, pl.ds(row, 8), :] = jnp.concatenate(
                        [update, jnp.zeros((8 - nv, lanes), F32)], axis=0
                    )
            for spare in range(inst * nv, (scale_at - inst * nv) * (FACE // 8)):
                at, row = table_place(spare)
                table_ref[at, pl.ds(row, 8), :] = jnp.zeros((8, lanes), F32)
            table_ref[scale_at] = mf_ref[side]
        for v in range(nv):
            rows = pl.ds(v * ROWS, ROWS)
            for w in range(nv):
                total = mixed([jac(coef_ref, d, v, w) for d in range(3)], [flux_ref[d] for d in range(3)])
                if v == w:
                    for d in range(3):
                        total = total + damp(coef_ref, d) * damp_ref[d]
                high, low = halves(total)
                at = w * ROWS
                lhs_ref[rows, pl.ds(at, ROWS)] = high
                lhs_ref[rows, pl.ds(depth + at, ROWS)] = low
            for c in range(pairs):
                total = jac(coef_ref, 2, v, 2 * c) * flux_ref[3]
                if 2 * c + 1 < nv:
                    total = total + jac(coef_ref, 2, v, 2 * c + 1) * flux_ref[4]
                if v // 2 == c:
                    total = total + damp(coef_ref, 2) * damp_ref[3 + v % 2]
                high, low = halves(total)
                at = nv * ROWS + c * 2 * ENDS
                lhs_ref[rows, pl.ds(at, 2 * ENDS)] = high
                lhs_ref[rows, pl.ds(depth + at, 2 * ENDS)] = low
        cols = lax.dot_general(
            inlet_table_ref[...],
            inlet_ref[...],
            (((1,), (1,)), ((), ())),
            precision=lax.Precision.HIGHEST,
            preferred_element_type=F32,
        )
        blend = jnp.zeros((ROWS, ROWS), F32)
        for v in range(nv):
            for w in range(nv):
                value = jac(coef_ref, 2, v, w)
                if v == w:
                    value = value + damp(coef_ref, 2)
                blend = jnp.where(mix_ref[...] == v * nv + w, -5.0 * value, blend)
        cols = jnp.dot(cols, blend, precision=lax.Precision.HIGHEST, preferred_element_type=F32)
        col_ref[...] = metric[:, 0:1] * cols
        for n in range(inst):
            natural = jnp.concatenate([padded_ref[n, v] for v in range(nv)], axis=1)
            moved = reorder(order_ref[...], natural, 3)
            for v in range(nv):
                part = moved[:, v * lanes : (v + 1) * lanes]
                x_ref[n, v] = part
                lo_ref[n, v] = part[0:FACE]
                hi_ref[n, v] = part[HIGH:ROWS]
                low_table_ref[n * nv + v] = part[0:FACE]
                high_table_ref[n * nv + v] = part[HIGH:ROWS]

    x0, lo0, hi0, metric, metric_face, lhs, inlet_cols, face_coef, face_update, low_table, high_table = call(
        prep_kernel,
        [
            shape(inst, nv, ROWS, lanes),
            shape(inst, nv, FACE, lanes),
            shape(inst, nv, FACE, lanes),
            shape(ROWS, lanes),
            shape(2, FACE, lanes),
            shape(nv * ROWS, 2 * depth, dtype=BF16),
            shape(ROWS, ROWS),
            shape(2, nv, nv, lanes),
            shape(2, inst, nv, nv, lanes),
            shape(scale_at + 1, FACE, lanes),
            shape(scale_at + 1, FACE, lanes),
        ],
        [
            state_rows,
            metric_scale.reshape(nodes, 1, lanes),
            coef,
            order_b,
            flux_table,
            damp_table,
            inlet,
            inlet_table,
            mix_index,
            precond,
        ],
        "hhsvvvvvvv",
        scratch=[
            pltpu.VMEM((inst, nv, ROWS, lanes), F32),
            pltpu.VMEM((ROWS, lanes), F32),
            pltpu.SemaphoreType.DMA((1 + inst * nv,)),
        ],
        name="prep",
    )

    def bulk(xs, lhs_ref):
        cols = []
        lane = lax.broadcasted_iota(jnp.int32, (ENDS // 2, lanes), 1)
        for x in xs:
            ends = []
            for part in x:
                first = jnp.concatenate([part[a:b] for a, b in FIRST], axis=0)
                last = jnp.concatenate([part[a:b] for a, b in LAST], axis=0)
                ends.append(jnp.where(lane == lanes - 1, last, pltpu.roll(first, lanes - 1, 1)))
                ends.append(jnp.where(lane == 0, 0.0, pltpu.roll(last, 1, 1)))
            if nv % 2:
                ends.append(jnp.zeros((ENDS, lanes), F32))
            cols.append(jnp.concatenate(list(x) + ends, axis=0))
        high, low = halves(jnp.concatenate(cols, axis=1) if len(cols) > 1 else cols[0])
        both = dot32(lhs_ref[...], jnp.concatenate([high, high], axis=0))
        return both + dot32(lhs_ref[:, 0:depth], low)

    def block_of(result, n, v):
        return result[v * ROWS : (v + 1) * ROWS, n * lanes : (n + 1) * lanes]

    def whole(lo_ref, z_ref, hi_ref, n, at, v):
        return jnp.concatenate([lo_ref[n, v], z_ref[at, v, FACE:HIGH, :], hi_ref[n, v]], axis=0)


    def advance(z, lo, hi, extra, first, size, flops=0):
        def kernel(*refs):
            z_ref, lo_ref, hi_ref, m_ref, p_ref, lhs_ref = refs[:6]
            out_ref = refs[-1]
            metric_value = m_ref[...]
            for at in range(0, size, 2):
                ids = list(range(at, min(at + 2, size)))
                xs = [[whole(lo_ref, z_ref, hi_ref, n, n, v) for v in range(nv)] for n in ids]
                result = bulk(xs, lhs_ref)
                for m, n in enumerate(ids):
                    res = [metric_value * block_of(result, m, v) for v in range(nv)]
                    if extra is not None:
                        res = [res[v] + refs[6][n, v] for v in range(nv)]
                    for v in range(nv):
                        weights = [p_ref[first + n, v, pl.ds(w, 1), :] for w in range(nv)]
                        out_ref[n, v] = xs[m][v] - mixed(weights, res)

        ins = [z, lo, hi, metric, precond, lhs]
        ins = ins + ([] if extra is None else [extra])
        return call(
            kernel,
            [shape(size, nv, ROWS, lanes)],
            ins,
            "vvvvvv" + ("" if extra is None else "v"),
            flops=flops,
            name="advance",
        )[0]

    def face_terms(n, lo_ref, hi_ref, below, above, table_of, mf_ref):
        position = lax.rem(lax.axis_index("elem") + PR // 2, PR)
        low_w, high_w = [], []
        for v in range(nv):
            sign = -1.0 if v == 2 else 1.0
            low_w.append(jnp.where(position == 0, sign * lo_ref[n, v], below[v]))
            high_w.append(jnp.where(position == PR - 1, sign * hi_ref[n, v], above[v]))
        lows, highs = [], []
        for v in range(nv):
            lows.append(mf_ref[0] * mixed([table_of(0, v, w) for w in range(nv)], low_w))
            highs.append(mf_ref[1] * mixed([table_of(1, v, w) for w in range(nv)], high_w))
        return lows, highs

    def swap_faces(lo, hi):
        return along_elem(hi, 1), along_elem(lo, -1)

    def close_faces(z, lo, hi, below, above, first, size, send=True):
        def kernel(z_ref, lo_ref, hi_ref, below_ref, above_ref, mf_ref, pc_ref, nlo_ref, nhi_ref, *sends):
            for n in range(size):

                def table_of(side, v, w, n=n):
                    return pc_ref[side, first + n, v, pl.ds(w, 1), :]

                flat = not sends
                below = [below_ref[n * nv + v] if flat else get_rows(below_ref, (n,), v) for v in range(nv)]
                above = [above_ref[n * nv + v] if flat else get_rows(above_ref, (n,), v) for v in range(nv)]
                lows, highs = face_terms(n, lo_ref, hi_ref, below, above, table_of, mf_ref)
                for v in range(nv):
                    new_lo, new_hi = z_ref[n, v, 0:FACE, :] - lows[v], z_ref[n, v, HIGH:ROWS, :] - highs[v]
                    nlo_ref[n, v], nhi_ref[n, v] = new_lo, new_hi
                    if sends:
                        put_rows(sends[0], (n,), v, new_lo)
                        put_rows(sends[1], (n,), v, new_hi)

        return call(
            kernel,
            [shape(size, nv, FACE, lanes)] * 2 + ([shape(size, ROWS, lanes)] * 2 if send else []),
            [z, lo, hi, below, above, metric_face, face_update],
            "v" * 7,
            name="faces",
        )

    def paired_first(z, lo, hi, spec, first):
        def kernel(z_ref, lo_ref, hi_ref, m_ref, p_ref, lhs_ref, spec_ref, out_ref, down_ref, up_ref, send_down_ref, send_up_ref):
            metric_value = m_ref[...]
            for at in range(0, per, 2):
                ids = list(range(at, min(at + 2, per)))
                xs = [[whole(lo_ref, z_ref, hi_ref, n, n, v) for v in range(nv)] for n in ids]
                result = bulk(xs, lhs_ref)
                for m, n in enumerate(ids):
                    res = [metric_value * block_of(result, m, v) + spec_ref[n, v] for v in range(nv)]
                    for v in range(nv):
                        weights = [p_ref[first + n, v, pl.ds(w, 1), :] for w in range(nv)]
                        value = xs[m][v] - mixed(weights, res)
                        out_ref[n, v] = value
                        down_ref[0, n, v], up_ref[0, n, v] = lo_ref[n, v], hi_ref[n, v]
                        down_ref[1, n, v], up_ref[1, n, v] = value[0:FACE], value[HIGH:ROWS]
                        put_rows(send_down_ref, (0, n), v, lo_ref[n, v])
                        put_rows(send_up_ref, (0, n), v, hi_ref[n, v])
                        put_rows(send_down_ref, (1, n), v, value[0:FACE])
                        put_rows(send_up_ref, (1, n), v, value[HIGH:ROWS])

        return call(
            kernel,
            [shape(per, nv, ROWS, lanes)]
            + [shape(2, per, nv, FACE, lanes)] * 2
            + [shape(2, per, ROWS, lanes)] * 2,
            [z, lo, hi, metric, precond, lhs, spec],
            "v" * 7,
            name="paired_first",
        )

    def paired_second(z, down, up, below, above, below_table, above_table, spec, first):
        def kernel(*refs):
            z_ref, down_ref, up_ref, below_ref, above_ref = refs[:5]
            low_ref, high_ref, below_table_ref, above_table_ref = refs[5:9]
            m_ref, p_ref, lhs_ref, spec_ref, out_ref, out_lo_ref, out_hi_ref, send_lo_ref, send_hi_ref = refs[9:]
            metric_value = m_ref[...]
            position = lax.rem(lax.axis_index("elem") + PR // 2, PR)

            def update(table_ref, n, values):
                result = []
                for v in range(nv):
                    at, row = table_place((first + n) * nv + v)
                    weights = [table_ref[at, pl.ds(row + w, 1), :] for w in range(nv)]
                    result.append(table_ref[scale_at] * mixed(weights, values))
                return result

            def across(at, own, other):
                return [
                    jnp.where(position == at, -own[v] if v == 2 else own[v], other[v]) for v in range(nv)
                ]

            def minus(a, b):
                return [p - q for p, q in zip(a, b)]

            for at in range(0, per, 2):
                ids = list(range(at, min(at + 2, per)))
                xs, beyond = [], []
                for n in ids:
                    lo, zlo = ([down_ref[k, n, v] for v in range(nv)] for k in range(2))
                    hi, zhi = ([up_ref[k, n, v] for v in range(nv)] for k in range(2))
                    low_w, low_z = ([get_rows(below_ref, (k, n), v) for v in range(nv)] for k in range(2))
                    high_w, high_z = ([get_rows(above_ref, (k, n), v) for v in range(nv)] for k in range(2))
                    new_lo = minus(zlo, update(low_ref, n, across(0, lo, low_w)))
                    new_hi = minus(zhi, update(high_ref, n, across(PR - 1, hi, high_w)))
                    next_low = across(0, new_lo, minus(low_z, update(below_table_ref, n, lo)))
                    next_high = across(PR - 1, new_hi, minus(high_z, update(above_table_ref, n, hi)))
                    xs.append(
                        [
                            jnp.concatenate([new_lo[v], z_ref[n, v, FACE:HIGH, :], new_hi[v]], axis=0)
                            for v in range(nv)
                        ]
                    )
                    beyond.append((update(low_ref, n, next_low), update(high_ref, n, next_high)))
                result = bulk(xs, lhs_ref)
                for m, n in enumerate(ids):
                    res = [metric_value * block_of(result, m, v) + spec_ref[n, v] for v in range(nv)]
                    for v in range(nv):
                        weights = [p_ref[first + n, v, pl.ds(w, 1), :] for w in range(nv)]
                        value = xs[m][v] - mixed(weights, res)
                        lo, hi = value[0:FACE] - beyond[m][0][v], value[HIGH:ROWS] - beyond[m][1][v]
                        out_ref[n, v] = value
                        out_lo_ref[n, v] = lo
                        out_hi_ref[n, v] = hi
                        put_rows(send_lo_ref, (n,), v, lo)
                        put_rows(send_hi_ref, (n,), v, hi)

        return call(
            kernel,
            [shape(per, nv, ROWS, lanes)]
            + [shape(per, nv, FACE, lanes)] * 2
            + [shape(per, ROWS, lanes)] * 2,
            [z, down, up, below, above, low_table, high_table, below_table, above_table]
            + [metric, precond, lhs, spec],
            "v" * 13,
            name="paired_second",
        )

    def circ_extra(z, lo, hi):
        x = jnp.concatenate([lo, z[:, :, FACE:HIGH], hi], axis=2)
        picks = np.zeros((2, 25, ROWS), dtype=np.float32)
        picks[0, np.arange(25), node_row[0:25]] = 1.0
        picks[1, np.arange(25), node_row[100:125]] = 1.0
        exact = lax.Precision.HIGHEST

        def picked(which):
            return jnp.einsum("pq,nvqa->nvpa", picks[which], x, precision=exact)

        def mix(values):
            return jnp.einsum("vw,nwqa->nvqa", flux_jacobians[0], values, precision=exact)

        def placed(which, values):
            return jnp.einsum("pq,nvpa->nvqa", picks[which], values, precision=exact)

        above, below = along_elem(picked(0), -PR), along_elem(picked(1), PR)
        high_term = 5.0 * (mix(above) - damping[0] * above)
        low_term = -5.0 * (mix(below) + damping[0] * below)
        return metric * (placed(1, high_term) + placed(0, low_term))

    below0, above0 = swap_faces(low_table, high_table)
    t0 = advance(x0, lo0, hi0, None if own_circ else circ_extra(x0, lo0, hi0), 0, inst)
    tlo, thi = close_faces(t0, lo0, hi0, below0, above0, 0, inst, send=False)

    half_pair = n_tm % 2 == 0

    def weight(offset, sign):
        return 0.5 * (coupling_value(offset, count) + sign * coupling_value(offset + count // 2, count))

    def weighted(terms):
        terms = [(c, x) for c, x in terms if abs(c) > 1e-12]
        return mixed([c for c, _ in terms], [x for _, x in terms])

    def coupling_kernel(*refs):
        x_refs, outs = refs[:n_tm], refs[n_tm:]

        def body(step, carry):
            v, rows = step // (block // 8), pl.ds(pl.multiple_of((step % (block // 8)) * 8, 8), 8)
            x = [[x_refs[d][i, v, rows, :] for i in range(inst)] for d in range(n_tm)]
            if half_pair:
                half = n_tm // 2
                sources = [(d, i) for d in range(half) for i in range(inst)]
                sums = [x[d][i] + x[d + half][i] for d, i in sources]
                diffs = [x[d][i] - x[d + half][i] for d, i in sources]
                for e in range(half):
                    for j in range(inst):
                        offsets = [inst * (e + d) + j - i for d, i in sources]
                        even = weighted([(weight(o, 1), s) for o, s in zip(offsets, sums)])
                        odd = weighted([(weight(o, -1), s) for o, s in zip(offsets, diffs)])
                        outs[e * groups + j // per][j % per, v, rows, :] = even + odd
                        outs[(e + half) * groups + j // per][j % per, v, rows, :] = even - odd
            else:
                sources = [(d, i) for d in range(n_tm) for i in range(inst)]
                for e in range(n_tm):
                    for j in range(inst):
                        offsets = [inst * (e + d) + j - i for d, i in sources]
                        outs[e * groups + j // per][j % per, v, rows, :] = weighted(
                            [(coupling_value(o, count), x[d][i]) for o, (d, i) in zip(offsets, sources)]
                        )
            return carry

        lax.fori_loop(0, nv * (block // 8), body, 0)

    coupled = call(
        coupling_kernel,
        [shape(per, nv, block, lanes)] * (n_tm * groups),
        arrived,
        "v" * n_tm,
        name="coupling",
    )
    spectral = [[coupled[g]] + [None] * (n_tm - 1) for g in range(groups)]
    for g in range(groups):
        for e in sorted(range(1, n_tm), key=lambda e: abs(2 * e - n_tm)):
            spectral[g][e] = along_tm(coupled[e * groups + g], e)

    def first_pass(parts, first, flops=0, send=True):
        distances = list(range(n_tm))
        if first > 0:
            distances.sort(key=lambda d: min(d, n_tm - d))

        def kernel(*refs):
            part_refs = [refs[distances.index(d)] for d in range(n_tm)]
            t_ref, tlo_ref, thi_ref, p_ref, col_ref, order_ref = refs[n_tm : n_tm + 6]
            x_ref, lo_ref, hi_ref, s_ref, *sends, buf = refs[n_tm + 6 :]
            me = lax.axis_index("tm")
            for d in range(n_tm):
                start = pl.multiple_of(lax.rem(me - d + n_tm, n_tm) * block, block)
                for n in range(per):
                    for v in range(nv):
                        buf[n, v, pl.ds(start, block), :] = part_refs[d][n, v]
            lane = lax.broadcasted_iota(jnp.int32, (ROWS, lanes), 1)
            for n in range(per):
                natural = jnp.concatenate([buf[n, v] for v in range(nv)], axis=1)
                moved = reorder(order_ref[...], natural, 2)
                terms = []
                for v in range(nv):
                    c = (first + n) * nv + v
                    column = jnp.broadcast_to(col_ref[:, c : c + 1], (ROWS, lanes))
                    term = moved[:, v * lanes : (v + 1) * lanes] + jnp.where(lane == 0, column, 0.0)
                    s_ref[n, v] = term
                    terms.append(term)
                for v in range(nv):
                    weights = [p_ref[first + n, v, pl.ds(w, 1), :] for w in range(nv)]
                    x = whole(tlo_ref, t_ref, thi_ref, first + n, first + n, v) - mixed(weights, terms)
                    x_ref[n, v] = x
                    lo_ref[n, v] = x[0:FACE]
                    hi_ref[n, v] = x[HIGH:ROWS]
                    if sends:
                        put_rows(sends[0], (n,), v, x[0:FACE])
                        put_rows(sends[1], (n,), v, x[HIGH:ROWS])

        return call(
            kernel,
            [
                shape(per, nv, ROWS, lanes),
                shape(per, nv, FACE, lanes),
                shape(per, nv, FACE, lanes),
                shape(per, nv, ROWS, lanes),
            ]
            + ([shape(per, ROWS, lanes)] * 2 if send else []),
            [parts[d] for d in distances] + [t0, tlo, thi, precond, inlet_cols, spectral_order.astype(ml_dtypes.bfloat16)],
            "v" * (n_tm + 6),
            scratch=[pltpu.VMEM((per, nv, ROWS, lanes), F32)],
            flops=flops,
            name="first_pass",
        )

    def write_out(moved_ref, out_ref, sem, first, work, meanwhile=None):
        copies = []
        for n in range(per):
            work(n)
            for v in range(nv):
                copy = pltpu.make_async_copy(
                    moved_ref.at[n, v, pl.ds(0, nodes), :], out_ref.at[first + n, v, :, 0, :], sem.at[n, v]
                )
                copy.start()
                copies.append(copy)
        if meanwhile is not None:
            meanwhile()
        for copy in copies:
            copy.wait()

    def last_bulk(z, lo, hi, extra, first, out):
        def kernel(*refs):
            z_ref, lo_ref, hi_ref, m_ref, lhs_ref, extra_ref, back_ref = refs[:7]
            r_ref, out_ref, buf, sem = refs[-4:]
            metric_value = m_ref[...]

            def work(n):
                x = [whole(lo_ref, z_ref, hi_ref, n, n, v) for v in range(nv)]
                moved = reorder(back_ref[...], jnp.concatenate(x, axis=1), 3)
                for v in range(nv):
                    buf[n, v] = moved[:, v * lanes : (v + 1) * lanes]

            def residual():
                for at in range(0, per, 2):
                    ids = list(range(at, min(at + 2, per)))
                    xs = [[whole(lo_ref, z_ref, hi_ref, n, n, v) for v in range(nv)] for n in ids]
                    result = bulk(xs, lhs_ref)
                    for m, n in enumerate(ids):
                        for v in range(nv):
                            r_ref[n, v] = metric_value * block_of(result, m, v) + extra_ref[n, v]

            write_out(buf, out_ref, sem, first, work, residual)

        ins = [z, lo, hi, metric, lhs, extra, back_b] + ([] if out is None else [out])
        return call(
            kernel,
            [shape(per, nv, ROWS, lanes), shape(inst, nv, nodes, 1, lanes)],
            ins,
            "vvvvvvv" + ("" if out is None else "a"),
            out_spaces="va",
            scratch=[pltpu.VMEM((per, nv, ROWS, lanes), F32), pltpu.SemaphoreType.DMA((per, nv))],
            alias=None if out is None else {7: 1},
            name="last_bulk",
        )

    def last_faces(r, lo, hi, below, above, first, out):
        def kernel(*refs):
            r_ref, lo_ref, hi_ref, below_ref, above_ref, mf_ref, fc_ref, back_ref = refs[:8]
            out_ref, buf, sem = refs[-3:]

            def table_of(side, v, w):
                return fc_ref[side, v, pl.ds(w, 1), :]

            def work(n):
                below = [get_rows(below_ref, (n,), v) for v in range(nv)]
                above = [get_rows(above_ref, (n,), v) for v in range(nv)]
                lows, highs = face_terms(n, lo_ref, hi_ref, below, above, table_of, mf_ref)
                full = [
                    jnp.concatenate(
                        [
                            r_ref[n, v, 0:FACE, :] + lows[v],
                            r_ref[n, v, FACE:HIGH, :],
                            r_ref[n, v, HIGH:ROWS, :] + highs[v],
                        ],
                        axis=0,
                    )
                    for v in range(nv)
                ]
                moved = reorder(back_ref[...], jnp.concatenate(full, axis=1), 2)
                for v in range(nv):
                    buf[n, v] = moved[:, v * lanes : (v + 1) * lanes]

            write_out(buf, out_ref, sem, first, work)

        ins = [r, lo, hi, below, above, metric_face, face_coef, back_b] + ([] if out is None else [out])
        return call(
            kernel,
            [shape(inst, nv, nodes, 1, lanes)],
            ins,
            "vvvvvvvv" + ("" if out is None else "a"),
            out_spaces="a",
            scratch=[pltpu.VMEM((per, nv, ROWS, lanes), F32), pltpu.SemaphoreType.DMA((per, nv))],
            alias=None if out is None else {8: 0},
            name="last_faces",
        )[0]

    new_state, final_residual = None, None
    chains, last = [None] * groups, None

    def begin(g, swap):
        parts = spectral[g] if last is None else [after(spectral[g][0], last)] + spectral[g][1:]
        z, lo, hi, spec, *sends = first_pass(parts, g * per, LONG if g == groups - 1 else 0, swap)
        chains[g] = (z, lo, hi, swap_faces(*sends) if swap else None, spec)
        return lo

    def local_part(g, count_done):
        nonlocal new_state
        z, lo, hi, swapped, spec = chains[g]
        extra = spec if own_circ else spec + circ_extra(z, lo, hi)
        extra = extra if last is None else after(extra, last)
        if count_done < PASSES - 1:
            z = advance(z, lo, hi, extra, g * per, per, LONG)
        else:
            z, new_state = last_bulk(z, lo, hi, extra, g * per, new_state)
        chains[g] = (z, lo, hi, swapped, spec)
        return z

    def face_part(g, count_done):
        nonlocal final_residual
        z, lo, hi, (below, above), spec = chains[g]
        z = after(z, last)
        if count_done < PASSES - 1:
            lo, hi, *sends = close_faces(z, lo, hi, below, above, g * per, per)
            chains[g] = (z, lo, hi, swap_faces(*sends), spec)
            return lo
        final_residual = last_faces(z, lo, hi, below, above, g * per, final_residual)
        return final_residual

    def pair_begin(g):
        z, lo, hi, _, spec = chains[g]
        z, down, up, send_down, send_up = paired_first(z, lo, hi, after(spec, last), g * per)
        chains[g] = (z, down, up, swap_faces(send_down, send_up), spec)
        return z

    def pair_end(g, *before):
        z, down, up, (below, above), spec = chains[g]
        z, lo, hi, *sends = paired_second(
            z, down, up, below, above, below0, above0, after(spec, last), g * per
        )
        chains[g] = (z, lo, hi, sends, spec)
        return z

    def pair_swap(g):
        z, lo, hi, sends, spec = chains[g]
        sends = lax.optimization_barrier((*sends, last))[:2]
        chains[g] = (z, lo, hi, swap_faces(*sends), spec)

    end = groups - 1
    if own_circ and PASSES == 3:
        for g in range(end):
            last = begin(g, False)
            last = pair_begin(g)
        last = begin(end, False)
        last = pair_begin(end)
        for g in range(end):
            last = pair_end(g)
            pair_swap(g)
            last = local_part(g, 2)
        last = pair_end(end)
        pair_swap(end)
        for g in range(end):
            last = face_part(g, 2)
        last = local_part(end, 2)
        last = face_part(end, 2)
    else:
        for g in range(groups):
            last = begin(g, True)
            for count_done in range(PASSES):
                last = local_part(g, count_done)
                last = face_part(g, count_done)
    return (new_state.reshape(state.shape), final_residual.reshape(state.shape))


def solution(mesh):
    in_specs = (
        P("tm", None, "elem", None, None),
        P("elem", None, None),
        P(),
        P("tm", None, None, "elem", None),
        P("tm", None, "elem", None),
    )
    out_specs = (P("tm", None, "elem", None, None), P("tm", None, "elem", None, None))
    return jax.shard_map(
        per_device, mesh=mesh, in_specs=in_specs, out_specs=out_specs, check_vma=False
    )
```
